128 devices in a mesh: grp: 4 (over z), ep: 32 (over x, y, core).
Axes of the slice: x: 4, y: 4, z: 4, core: 2. Of those that a mesh axis runs over, the one named last changes fastest.
Arguments:
- tokens: bfloat16 [4, 2048, 3584], P('grp', 'ep'), may hold values from -6 to 6
- route_ids: int32 [4, 2048, 8], P('grp', 'ep'), may hold values from 0 to 63, as said below
- route_gates: bfloat16 [4, 2048, 8], P('grp', 'ep'), may hold values from 0.049804688 to 0.59765625
- w_gate: bfloat16 [4, 32, 3584, 1024], P('grp', 'ep'), may hold values from -0.09375 to 0.09375
- w_up: bfloat16 [4, 32, 3584, 1024], P('grp', 'ep'), may hold values from -0.09375 to 0.09375
- w_down: bfloat16 [4, 32, 1024, 3584], P('grp', 'ep'), may hold values from -0.1875 to 0.1875
- hot_source: int32 [32], P('ep'), may hold values from 0 to 3
Outputs:
- moe_output: bfloat16 [4, 2048, 3584], P('grp', 'ep')
The draws below stay inside these ranges and needn't reach their ends.
Inputs may be any that keep to these rules, and one draw needn't show every extreme that they name: `route_ids`: each row names 8 different slots of its group. No slot is named by more than 16 rows of one device, and in each group some slot is named by exactly 16 rows of every device.
All inputs are finite; a program needn't handle non-finite values.
Results may differ from the reference program's by a relative error of at most 0.0057.
Values may be sent and summed in bfloat16 or wider, within the bound.
No kernel may reach another device: no remote copies, remote signals or barrier semaphores. Data moves between devices by JAX's collectives and lax.ppermute only.
A program may use at most 192 MiB of HBM per device.

```python
import jax
import jax.numpy as jnp
from jax import lax

D = 3584
FF = 1024
TOPK = 8
ROWS_DEV = 64
SEND_CAP = 16
TOKENS_GRP = 2048
N_GRP = 4
N_EP = 32


def draw_route_ids(key, part):
    key = jax.random.fold_in(key, 7)
    slot_count = 2 * N_EP
    mean_load = ROWS_DEV * TOPK // slot_count
    hot_key, block_key = jax.random.split(key)
    hot_slots = jax.random.randint(hot_key, (N_GRP,), 0, slot_count, dtype=jnp.int32)
    pair_index = jnp.arange(slot_count // 2, dtype=jnp.int32)
    positions = jnp.arange(ROWS_DEV * TOPK, dtype=jnp.int32)

    def one_block(block_number):
        own_key = jax.random.fold_in(block_key, block_number)
        order_key, spread_key = jax.random.split(own_key)
        order = jax.random.permutation(order_key, slot_count).astype(jnp.int32)
        spread = jax.random.randint(spread_key, (slot_count // 2,), -mean_load, mean_load + 1, dtype=jnp.int32)
        group_hot = hot_slots[block_number // N_EP]
        where_hot = jnp.sum(jnp.arange(slot_count, dtype=jnp.int32) * (order == group_hot).astype(jnp.int32))
        sign_hot = 1 - 2 * (where_hot % 2)
        spread = jnp.where(pair_index == where_hot // 2, sign_hot * mean_load, spread)
        pair_counts = jnp.stack([mean_load + spread, mean_load - spread], axis=1).reshape(slot_count)
        counts = jnp.zeros((slot_count,), jnp.int32).at[order].set(pair_counts)
        ends = jnp.cumsum(counts)
        slot_at = jnp.sum((ends[None, :] <= positions[:, None]).astype(jnp.int32), axis=1)
        return slot_at.reshape(TOPK, ROWS_DEV).T
    blocks = jax.vmap(one_block)(jnp.arange(N_GRP * N_EP, dtype=jnp.int32))
    return blocks.reshape(N_GRP, N_EP * ROWS_DEV, TOPK).astype(jnp.int32)


def with_ends(values, stream_key, low, top_value):
    index_at = [jax.random.randint(jax.random.fold_in(stream_key, axis), (), 0, length) for axis, length in enumerate(values.shape)]
    longest = values.shape.index(max(values.shape))
    beside = index_at[:longest] + [(index_at[longest] + 1) % values.shape[longest]] + index_at[longest + 1:]
    return values.at[tuple(index_at)].set(low).at[tuple(beside)].set(top_value)


def levels(key, dims, shards, least, largest):
    gain = 1.0
    for position, parts in shards:
        steps = jax.random.uniform(jax.random.fold_in(jax.random.fold_in(key, 6), position), (parts,), jnp.float32, least / len(shards), largest / len(shards))
        gain = gain * jnp.repeat(jnp.exp(steps), dims[position] // parts).reshape((-1,) + (1,) * (len(dims) - 1 - position))
    return gain


def scatter_about(key, shape, width, bound, cuts=(), held_as=jnp.bfloat16):
    entries = jax.random.normal(key, shape, jnp.float32) * width
    if len(cuts) > 0:
        entries = levels(key, shape, cuts, -0.22, 0.18) * entries
    return jnp.clip(entries, min=-bound, max=bound).astype(held_as)


def setup_inputs(seed: int = 0) -> dict:
    key_list = jax.random.split(jax.random.key(seed), 8)
    return {
        "tokens": scatter_about(key_list[0], (N_GRP, TOKENS_GRP, D), 1.0, 6.0, ((0, 4), (1, 32))),
        "route_ids": draw_route_ids(jax.random.fold_in(key_list[7], 71), 0),
        "route_gates": jnp.clip(0.049804688 + 0.54785156 * jax.random.uniform(key_list[2], (N_GRP, TOKENS_GRP, TOPK), jnp.float32) ** levels(key_list[2], (N_GRP, TOKENS_GRP, TOPK), ((0, 4), (1, 32)), -0.2, 0.2), 0.049804688, 0.59765625).astype(jnp.bfloat16),
        "w_gate": scatter_about(key_list[3], (N_GRP, N_EP, D, FF), D ** -0.5, 0.09375, ((0, 4), (1, 32))),
        "w_up": scatter_about(key_list[4], (N_GRP, N_EP, D, FF), D ** -0.5, 0.09375, ((0, 4), (1, 32))),
        "w_down": scatter_about(key_list[5], (N_GRP, N_EP, FF, D), FF ** -0.5, 0.1875, ((0, 4), (1, 32))),
        "hot_source": with_ends(jax.random.randint(key_list[6], (N_EP,), 0, N_GRP), jax.random.fold_in(key_list[6], 1), 0, N_GRP - 1).astype(jnp.int32),
    }


def expert_apply(inputs, weight_gate, weight_up, weight_down):
    gate_part = jnp.dot(inputs, weight_gate, preferred_element_type=jnp.float32)
    up_part = jnp.dot(inputs, weight_up, preferred_element_type=jnp.float32)
    hidden = (jax.nn.silu(gate_part) * up_part).astype(jnp.bfloat16)
    return jnp.dot(hidden, weight_down, preferred_element_type=jnp.float32).astype(jnp.bfloat16)


def arrival_places(slot_ids, slot_count):
    onehot = (slot_ids[..., None] == jnp.arange(slot_count, dtype=jnp.int32)).astype(jnp.int32)
    before = jnp.cumsum(onehot, axis=-2) - onehot
    return jnp.sum(before * onehot, axis=-1)


def reference(tokens, route_ids, route_gates, w_gate, w_up, w_down, hot_source):
    slot_count = 2 * N_EP
    block_size = ROWS_DEV * TOPK
    owner_rows = N_EP * SEND_CAP
    block_index = jnp.arange(N_EP, dtype=jnp.int32)[:, None]
    row_in_block = (jnp.arange(block_size, dtype=jnp.int32) // TOPK)[None, :]

    def group_output(group_index):
        slot_ids = route_ids[group_index].reshape(N_EP, block_size)
        places = arrival_places(slot_ids, slot_count)
        target = (slot_ids % N_EP) * (2 * owner_rows) + ((slot_ids // N_EP) * N_EP + block_index) * SEND_CAP + places
        sources = block_index * ROWS_DEV + row_in_block
        lookup_table = jnp.full((N_EP * 2 * owner_rows,), N_EP * ROWS_DEV, jnp.int32).at[target.reshape(-1)].set(sources.reshape(-1))
        weights = jnp.zeros((N_EP * 2 * owner_rows,), jnp.float32).at[target.reshape(-1)].set(route_gates[group_index].reshape(-1).astype(jnp.float32))
        lookup_table = lookup_table.reshape(N_EP, 2, owner_rows)
        weights = weights.reshape(N_EP, 2, owner_rows)
        padded = jnp.concatenate([tokens[group_index], jnp.zeros((1, D), tokens.dtype)], axis=0)

        def device_step(running_sum, owner_index):
            picked = padded[lookup_table[owner_index]]
            donor_group = hot_source[owner_index]
            own_out = expert_apply(picked[0], w_gate[group_index, owner_index], w_up[group_index, owner_index], w_down[group_index, owner_index])
            hot_out = expert_apply(picked[1], w_gate[donor_group, owner_index], w_up[donor_group, owner_index], w_down[donor_group, owner_index])
            values = jnp.stack([own_out, hot_out]).astype(jnp.float32) * weights[owner_index][:, :, None]
            running_sum = running_sum.at[lookup_table[owner_index].reshape(-1)].add(values.reshape(-1, D))
            return running_sum, None

        initial = jnp.zeros((N_EP * ROWS_DEV + 1, D), jnp.float32)
        running_sum, unused = lax.scan(device_step, initial, jnp.arange(N_EP, dtype=jnp.int32))
        return running_sum[:-1].astype(jnp.bfloat16)

    return lax.map(group_output, jnp.arange(N_GRP, dtype=jnp.int32))
```

```python
import jax
import jax.numpy as jnp
from jax import lax
from jax.sharding import PartitionSpec as P

BOTH = ("grp", "ep")


def down_copy(w_down, donor, pieces):
    n = lax.axis_size("grp")
    me = lax.axis_index("grp")
    half = w_down.shape[0] // 2
    size = half // pieces
    parts = []
    for sign in (1, -1):
        mine = w_down[:half] if sign == 1 else w_down[half:]
        mine = mine.reshape(pieces, size, mine.shape[1])
        distance = lax.rem((me - donor) * sign + 2 * n, n)
        pairs = [(i, (i + sign) % n) for i in range(n)]
        held = mine
        for step in range(pieces + n - 2):
            out_index = jnp.clip(step - distance, 0, pieces - 1)
            piece = lax.dynamic_index_in_dim(held, out_index, 0, keepdims=False)
            arrived = lax.ppermute(piece, "grp", pairs)
            in_index = step - distance + 1
            place = jnp.clip(in_index, 0, pieces - 1)
            keep = (distance > 0) & (in_index >= 0) & (in_index < pieces)
            old = lax.dynamic_index_in_dim(held, place, 0, keepdims=False)
            held = lax.dynamic_update_index_in_dim(held, jnp.where(keep, arrived, old), place, 0)
        parts.append(held.reshape(half, -1))
    return jnp.concatenate(parts, axis=0)


def places(member):
    count = jnp.cumsum(member.astype(jnp.int32), axis=-1)
    return jnp.where(member, count - 1, -1)


def local(tokens, route_ids, route_gates, w_gate, w_up, w_down, hot_source):
    n_grp, n_ep = lax.axis_size("grp"), lax.axis_size("ep")
    grp, ep = lax.axis_index("grp"), lax.axis_index("ep")
    rows = tokens[0]
    row_count, width = rows.shape
    picks = route_ids.shape[2]
    capacity = row_count * picks // n_ep * n_ep
    group_rows = row_count * n_ep
    donor = hot_source[0]
    own_gate, own_up, own_down = w_gate[0, 0], w_up[0, 0], w_down[0, 0]

    info = jnp.concatenate([route_ids[0].astype(jnp.bfloat16), route_gates[0]], axis=1)
    info = lax.all_gather(info.reshape(-1), BOTH, tiled=True).reshape(n_grp, group_rows, 2 * picks)
    every = lax.all_gather(rows, BOTH, tiled=True).reshape(n_grp, group_rows, width)
    hot_down = down_copy(own_down, donor, 8)

    ids = info[:, :, :picks].astype(jnp.int32)
    gates = info[:, :, picks:]
    my_ids = lax.dynamic_index_in_dim(ids, grp, 0, keepdims=False)
    my_gates = lax.dynamic_index_in_dim(gates, grp, 0, keepdims=False)
    own_pos = places(jnp.any(my_ids == ep, axis=-1))
    hot_pos = places(jnp.any(ids == ep + n_ep, axis=-1))
    my_hot_pos = lax.dynamic_index_in_dim(hot_pos, grp, 0, keepdims=False)
    own_scale = jnp.sum(jnp.where(my_ids == ep, my_gates, 0), axis=-1)
    hot_scale = jnp.sum(jnp.where(my_ids == ep + n_ep, my_gates, 0), axis=-1)

    slots = jnp.arange(capacity, dtype=jnp.int32)
    mine = lax.dynamic_index_in_dim(every, grp, 0, keepdims=False)
    own_pick = (own_pos[None, :] == slots[:, None]).astype(jnp.bfloat16)
    hot_pick = (hot_pos[:, None, :] == slots[None, :, None]).astype(jnp.bfloat16)
    own_rows = jnp.dot(own_pick, mine, preferred_element_type=jnp.float32).astype(jnp.bfloat16)
    hot_rows = jnp.einsum("gpr,grd->gpd", hot_pick, every, preferred_element_type=jnp.float32).astype(jnp.bfloat16)

    def hidden_of(inputs):
        gate_part = jnp.dot(inputs, own_gate, preferred_element_type=jnp.float32)
        up_part = jnp.dot(inputs, own_up, preferred_element_type=jnp.float32)
        return (jax.nn.silu(gate_part) * up_part).astype(jnp.bfloat16)

    own_hidden = hidden_of(own_rows)
    hot_hidden = hidden_of(hot_rows.reshape(n_grp * capacity, width))
    hot_hidden = jnp.where(donor == grp, hot_hidden, jnp.zeros_like(hot_hidden))
    hot_hidden = lax.psum_scatter(hot_hidden, "grp", tiled=True)

    own_out = jnp.dot(own_hidden, own_down, preferred_element_type=jnp.float32).astype(jnp.bfloat16)
    hot_out = jnp.dot(hot_hidden, hot_down, preferred_element_type=jnp.float32).astype(jnp.bfloat16)
    own_put = jnp.where(own_pos[:, None] == slots[None, :], own_scale[:, None], 0).astype(jnp.bfloat16)
    hot_put = jnp.where(my_hot_pos[:, None] == slots[None, :], hot_scale[:, None], 0).astype(jnp.bfloat16)
    partial = jnp.dot(own_put, own_out, preferred_element_type=jnp.float32) + jnp.dot(
        hot_put, hot_out, preferred_element_type=jnp.float32
    )
    return lax.psum_scatter(partial.astype(jnp.bfloat16), "ep", tiled=True)[None]


def solution(mesh):
    placed = (
        P("grp", "ep", None),
        P("grp", "ep", None),
        P("grp", "ep", None),
        P("grp", "ep", None, None),
        P("grp", "ep", None, None),
        P("grp", "ep", None, None),
        P("ep"),
    )
    return jax.shard_map(
        local, mesh=mesh, in_specs=placed, out_specs=P("grp", "ep", None), check_vma=False
    )
```

```python
import functools

import jax
import jax.numpy as jnp
from jax import lax
from jax.experimental import pallas as pl
from jax.experimental.pallas import tpu as pltpu
from jax.sharding import PartitionSpec as P

SIDE = 4
BLOCK = 4
WINDOW = 128
ALIGN = 64
TILE = 128
EARLY = (0, 1, 3)
LATE = (2,)
VMEM = 58 * 1024 * 1024


def ep_of(x, y, core):
    return (x * SIDE + y) * 2 + core


def moved(index, ring, step):
    x, y, core = index // (2 * SIDE), index // 2 % SIDE, index % 2
    if (ring == 0) == (core == 0):
        return ep_of(x, (y + step) % SIDE, core)
    return ep_of((x + step) % SIDE, y, core)


def shift_z(value, step):
    return lax.ppermute(value, "grp", [(i, (i + step) % SIDE) for i in range(SIDE)])


def shift_ring(value, ring, step):
    count = 2 * SIDE * SIDE
    return lax.ppermute(value, "ep", [(i, moved(i, ring, step)) for i in range(count)])


def swap_cores(value):
    count = 2 * SIDE * SIDE
    return lax.ppermute(value, "ep", [(i, i ^ 1) for i in range(count)])


def down_copy(w_down, distance, pieces):
    half = w_down.shape[0] // 2
    size = half // pieces
    parts = []
    for sign in (1, -1):
        held = w_down[:half] if sign == 1 else w_down[half:]
        held = held.reshape(pieces, size, held.shape[1])
        away = distance if sign == 1 else lax.rem(SIDE - distance, SIDE)
        for step in range(pieces + SIDE - 2):
            piece = lax.dynamic_index_in_dim(held, jnp.clip(step - away, 0, pieces - 1), 0, keepdims=False)
            arrived = shift_z(piece, sign)
            index = step - away + 1
            place = jnp.clip(index, 0, pieces - 1)
            keep = (away > 0) & (index >= 0) & (index < pieces)
            old = lax.dynamic_index_in_dim(held, place, 0, keepdims=False)
            held = lax.dynamic_update_index_in_dim(held, jnp.where(keep, arrived, old), place, 0)
        parts.append(held.reshape(half, -1))
    return parts


def hidden_kernel(blocks, capacity, sources, meta, places, gate_hbm, up_hbm, *rest):
    count = max(piece for block in sources for piece, _ in block) + 1
    pieces = rest[:count]
    own_out, hot_out, gate, up, gathered, compact, weight_sems, row_sems = rest[count:]
    rows = pieces[0].shape[2]
    width = gate.shape[0]
    hidden = gate.shape[1]
    block_rows = BLOCK * rows
    wide = 512 if width % 512 == 0 else 256
    me = meta[0]
    donates = meta[1] == 1

    def load(distance, slot):
        for block, units in enumerate(sources):
            for unit, (piece, place) in enumerate(units):
                pltpu.make_async_copy(
                    pieces[piece].at[place, distance],
                    gathered.at[slot, pl.ds(block * block_rows + unit * rows, rows)],
                    row_sems.at[slot],
                ).start()

    def arrive(slot):
        pltpu.make_async_copy(gathered.at[slot], gathered.at[slot], row_sems.at[slot]).wait()

    def serve(segment, slot, store):
        compact[...] = jnp.zeros_like(compact)

        def pick(block, carry):
            start = meta[2 + segment * (blocks + 1) + block]
            start = pl.multiple_of(start, ALIGN)
            place = places[pl.ds(segment * blocks + block, 1), :] - start
            slots = lax.broadcasted_iota(jnp.int32, (WINDOW, block_rows), 0)
            choose = jnp.where(slots == place, 1.0, 0.0).astype(jnp.bfloat16)

            def part(n, carry):
                columns = pl.ds(pl.multiple_of(n * wide, wide), wide)
                values = gathered[slot, pl.ds(pl.multiple_of(block * block_rows, block_rows), block_rows), columns]
                found = jnp.dot(choose, values, preferred_element_type=jnp.float32).astype(jnp.bfloat16)
                compact[pl.ds(start, WINDOW), columns] = compact[pl.ds(start, WINDOW), columns] + found
                return carry

            return lax.fori_loop(0, width // wide, part, carry)

        lax.fori_loop(0, blocks, pick, 0)

        def tile(t, carry):
            span = pl.ds(pl.multiple_of(t * TILE, TILE), TILE)

            def part(n, carry):
                columns = pl.ds(pl.multiple_of(n * 256, 256), 256)
                gate_part = jnp.dot(compact[span, :], gate[:, columns], preferred_element_type=jnp.float32)
                up_part = jnp.dot(compact[span, :], up[:, columns], preferred_element_type=jnp.float32)
                store(span, columns, (jax.nn.silu(gate_part) * up_part).astype(jnp.bfloat16))
                return carry

            return lax.fori_loop(0, hidden // 256, part, carry)

        lax.fori_loop(0, meta[2 + segment * (blocks + 1) + blocks], tile, 0)

    weights = (
        pltpu.make_async_copy(gate_hbm, gate, weight_sems.at[0]),
        pltpu.make_async_copy(up_hbm, up, weight_sems.at[1]),
    )
    load(0, 0)
    for copy in weights:
        copy.start()
    own_out[...] = jnp.zeros_like(own_out)
    hot_out[...] = jnp.zeros_like(hot_out)

    def own_store(span, columns, value):
        own_out[span, columns] = value

    for distance in range(SIDE):
        slot = distance % 2
        group = lax.rem(me + distance, SIDE)

        def hot_store(span, columns, value, group=group):
            hot_out[group, span, columns] = value

        if distance < SIDE - 1:
            pl.when(donates)(functools.partial(load, distance + 1, 1 - slot))
        if distance == 0:
            arrive(slot)
            for copy in weights:
                copy.wait()
            serve(0, slot, own_store)
        else:
            pl.when(donates)(functools.partial(arrive, slot))
        pl.when(donates)(functools.partial(serve, 1 + distance, slot, hot_store))


def hidden_call(blocks, capacity, sources, meta, places, gate, up, pieces):
    rows = pieces[0].shape[2]
    width, hidden = gate.shape
    block_rows = BLOCK * rows
    anywhere = pl.BlockSpec(memory_space=pl.ANY)
    tiles = 5 * capacity // TILE
    return pl.pallas_call(
        functools.partial(hidden_kernel, blocks, capacity, sources),
        in_specs=[pl.BlockSpec(memory_space=pltpu.SMEM), pl.BlockSpec(memory_space=pltpu.VMEM)]
        + [anywhere] * (2 + len(pieces)),
        out_specs=[pl.BlockSpec(memory_space=pltpu.VMEM)] * 2,
        out_shape=[
            jax.ShapeDtypeStruct((capacity, hidden), jnp.bfloat16),
            jax.ShapeDtypeStruct((SIDE, capacity, hidden), jnp.bfloat16),
        ],
        scratch_shapes=[
            pltpu.VMEM((width, hidden), jnp.bfloat16),
            pltpu.VMEM((width, hidden), jnp.bfloat16),
            pltpu.VMEM((2, blocks * block_rows, width), jnp.bfloat16),
            pltpu.VMEM((capacity, width), jnp.bfloat16),
            pltpu.SemaphoreType.DMA((2,)),
            pltpu.SemaphoreType.DMA((2,)),
        ],
        compiler_params=pltpu.CompilerParams(vmem_limit_bytes=VMEM),
        cost_estimate=pl.CostEstimate(
            flops=tiles * TILE * width * hidden * 4,
            bytes_accessed=2 * width * hidden * 2 + 4 * blocks * block_rows * width * 2,
            transcendentals=tiles * TILE * hidden,
        ),
    )(meta, places, gate, up, *pieces)


def combine_kernel(starts, routes, own_early, own_late, hot_early, hot_late, down, copied_low, copied_high,
                   mine, theirs, outs, pair):
    early = own_early.shape[0]
    late = own_late.shape[0]
    half = copied_low.shape[0]
    total = early + late
    block_rows = mine.shape[0] // SIDE

    def put(begin, size, value):
        outs[pl.ds(begin, size), :] = value.astype(jnp.bfloat16)

    put(0, early, jnp.dot(own_early[...], down[...], preferred_element_type=jnp.float32))
    put(early, late, jnp.dot(own_late[...], down[...], preferred_element_type=jnp.float32))
    for begin, size, ref in ((total, early, hot_early), (total + early, late, hot_late)):
        put(
            begin,
            size,
            jnp.dot(ref[:, :half], copied_low[...], preferred_element_type=jnp.float32)
            + jnp.dot(ref[:, half:], copied_high[...], preferred_element_type=jnp.float32),
        )

    for out, first in ((theirs, SIDE), (mine, 0)):

        def block(b, carry, out=out, first=first):
            own_start = pl.multiple_of(starts[2 * (first + b)], ALIGN)
            hot_start = pl.multiple_of(starts[2 * (first + b) + 1], ALIGN)
            span = pl.ds(pl.multiple_of((first + b) * block_rows, block_rows), block_rows)
            slots = lax.broadcasted_iota(jnp.int32, (block_rows, WINDOW), 1).astype(jnp.float32)
            own = jnp.where(routes[span, 0:1] - own_start.astype(jnp.float32) == slots, routes[span, 1:2], 0.0)
            hot = jnp.where(routes[span, 2:3] - hot_start.astype(jnp.float32) == slots, routes[span, 3:4], 0.0)
            scale = jnp.concatenate([own.astype(jnp.bfloat16), hot.astype(jnp.bfloat16)], axis=1)
            pair[:WINDOW, :] = outs[pl.ds(own_start, WINDOW), :]
            pair[WINDOW:, :] = outs[pl.ds(total + hot_start, WINDOW), :]
            value = jnp.dot(scale, pair[...], preferred_element_type=jnp.float32)
            out[pl.ds(pl.multiple_of(b * block_rows, block_rows), block_rows), :] = value.astype(jnp.bfloat16)
            return carry

        lax.fori_loop(0, SIDE, block, 0)


def combine_call(part, parts, starts, routes, own_early, own_late, hot_early, hot_late, down, copied_low, copied_high):
    width = down.shape[1] // parts
    wide = 256
    steps = width // wide
    rows = routes.shape[0]
    whole = pl.BlockSpec(memory_space=pltpu.VMEM)
    offset = part * steps
    column = lambda ref: pl.BlockSpec((ref.shape[0], wide), lambda n: (0, offset + n))
    result = pl.BlockSpec((rows // 2, wide), lambda n: (0, n))
    slots = 2 * (own_early.shape[0] + own_late.shape[0])
    hidden = down.shape[0]
    return pl.pallas_call(
        combine_kernel,
        grid=(steps,),
        in_specs=[pl.BlockSpec(memory_space=pltpu.SMEM)] + [whole] * 5 + [column(down), column(copied_low), column(copied_high)],
        out_specs=[result, result],
        out_shape=[jax.ShapeDtypeStruct((rows // 2, width), jnp.bfloat16)] * 2,
        scratch_shapes=[pltpu.VMEM((slots, wide), jnp.bfloat16), pltpu.VMEM((2 * WINDOW, wide), jnp.bfloat16)],
        compiler_params=pltpu.CompilerParams(vmem_limit_bytes=VMEM),
        cost_estimate=pl.CostEstimate(
            flops=2 * slots * hidden * width + 4 * rows * WINDOW * width,
            bytes_accessed=4 * hidden * width + 2 * rows * width,
            transcendentals=0,
        ),
    )(starts, routes, own_early, own_late, hot_early, hot_late, down, copied_low, copied_high)


def add(*values):
    return sum(v.astype(jnp.float32) for v in values).astype(jnp.bfloat16)


def sum_to_owners(mine, theirs, rows):
    width = mine.shape[1]
    theirs = swap_cores(theirs)
    total = add(mine, theirs).reshape(SIDE, SIDE, rows, width)
    for ring, shape in ((1, (SIDE, rows, width)), (0, (rows, width))):
        cut = shape[0] // 2
        ahead = shift_ring(total[2, :cut], ring, 1)
        behind = shift_ring(total[2, cut:], ring, -1)
        forward = jnp.concatenate([add(total[1, :cut], ahead), total[1, cut:]], axis=0)
        backward = jnp.concatenate([total[3, :cut], add(total[3, cut:], behind)], axis=0)
        total = add(total[0], shift_ring(forward, ring, 1), shift_ring(backward, ring, -1))
    return total


def local(tokens, route_ids, route_gates, w_gate, w_up, w_down, hot_source):
    n_ep = lax.axis_size("ep")
    grp, ep = lax.axis_index("grp"), lax.axis_index("ep")
    rows = tokens[0]
    row_count, width = rows.shape
    picks = route_ids.shape[2]
    cap = row_count * picks // n_ep
    donor = hot_source[0]
    own_gate, own_up, own_down = w_gate[0, 0], w_up[0, 0], w_down[0, 0]

    info = jnp.concatenate([route_ids[0].astype(jnp.bfloat16), route_gates[0]], axis=1)
    info = lax.all_gather(info.reshape(-1), ("grp", "ep"), tiled=True)
    info = info.reshape(SIDE, n_ep, row_count, 2 * picks)

    below, above = shift_z(rows, 1), shift_z(rows, -1)
    cut = row_count // 2
    far = (shift_z(below[:cut], 1), shift_z(above[cut:], -1))
    unit = jnp.stack([rows, above, jnp.concatenate(far, axis=0), below])
    below, above = shift_ring(unit, 0, 1), shift_ring(unit, 0, -1)
    far = (shift_ring(below[:2], 0, 1), shift_ring(above[2:], 0, -1))
    near = jnp.stack([unit, above, jnp.concatenate(far, axis=0), below])
    below, above = shift_ring(near, 1, 1), shift_ring(near, 1, -1)
    far_low, far_high = shift_ring(below[:2], 1, 1), shift_ring(above[2:], 1, -1)
    early = [near, above, below]
    early = early + [swap_cores(piece) for piece in early]
    late = [far_low, far_high]
    late = late + [swap_cores(piece) for piece in late]

    copied_low, copied_high = down_copy(own_down, lax.rem(grp - donor + SIDE, SIDE), 8)

    core = lax.rem(ep, 2)
    x, y = ep // (2 * SIDE), lax.rem(ep // 2, SIDE)

    def source(other, second, first):
        at = jnp.where(other == 1, 1 - core, core)
        dx = jnp.where(at == 0, second, first)
        dy = jnp.where(at == 0, first, second)
        return ep_of(lax.rem(x + dx, SIDE), lax.rem(y + dy, SIDE), at)

    order = [(other, second) for seconds in (EARLY, LATE) for other in (0, 1) for second in seconds]
    units = jnp.stack([source(other, second, first) for other, second in order for first in range(SIDE)])
    groups = lax.rem(grp + jnp.arange(SIDE, dtype=jnp.int32), SIDE)
    ids = info[:, :, :, :picks].astype(jnp.int32)
    scales = info[:, :, :, picks:].astype(jnp.float32)
    is_own = (ids == ep)[grp]
    is_hot = ids == ep + n_ep
    member = jnp.concatenate([jnp.any(is_own, axis=-1)[None], jnp.any(is_hot, axis=-1)[groups]], axis=0)[:, units]
    own_scale = jnp.sum(jnp.where(is_own, scales[grp], 0.0), axis=-1)[units]
    hot_scale = jnp.sum(jnp.where(is_hot[grp], scales[grp], 0.0), axis=-1)[units]
    block_rows = BLOCK * row_count
    member = member.reshape(1 + SIDE, len(order), block_rows).astype(jnp.int32)
    donates = (donor == grp).astype(jnp.int32)

    first_late = 2 * len(EARLY)
    places, windows, metas = [], [], []
    for begin, end in ((0, first_late), (first_late, len(order))):
        blocks = end - begin
        capacity = blocks * BLOCK * cap
        here = member[:, begin:end].reshape(1 + SIDE, blocks * block_rows)
        after = jnp.cumsum(here, axis=1)
        place = jnp.where(here == 1, after - 1, -1).reshape(1 + SIDE, blocks, block_rows)
        after = after.reshape(1 + SIDE, blocks, block_rows)
        before = jnp.concatenate([jnp.zeros((1 + SIDE, 1), jnp.int32), after[:, :-1, -1]], axis=1)
        window = jnp.minimum(before // ALIGN * ALIGN, capacity - WINDOW)
        tiles = (after[:, -1, -1] + TILE - 1) // TILE
        meta = jnp.concatenate([window, tiles[:, None]], axis=1).reshape(-1)
        metas.append(jnp.concatenate([jnp.stack([grp, donates]), meta]))
        places.append(place)
        windows.append(window)

    pieces_of = {0: lambda o: o * 3, 1: lambda o: o * 3 + 1, 3: lambda o: o * 3 + 2}
    early_sources = [[(pieces_of[second](other), first) for first in range(SIDE)] for other, second in order[:first_late]]
    late_sources = [[(other * 2 + first // 2, first % 2) for first in range(SIDE)] for other, _ in order[first_late:]]
    own_hidden, hot_hidden = [], []
    for sources, pieces, place, meta in (
        (early_sources, early, places[0], metas[0]),
        (late_sources, late, places[1], metas[1]),
    ):
        blocks = len(sources)
        own, hot = hidden_call(
            blocks, blocks * BLOCK * cap, sources, meta, place.reshape(-1, block_rows), own_gate, own_up, pieces
        )
        own_hidden.append(own)
        hot_hidden.append(lax.psum_scatter(hot.reshape(-1, hot.shape[2]), "grp", tiled=True))

    early_slots = first_late * BLOCK * cap
    place = jnp.concatenate([places[0][:2], jnp.where(places[1][:2] < 0, -1, places[1][:2] + early_slots)], axis=1)
    window = jnp.concatenate([windows[0][:2], windows[1][:2] + early_slots], axis=1)
    wanted = [order.index((other, second)) for other in (0, 1) for second in range(SIDE)]
    scale = jnp.stack([own_scale, hot_scale]).reshape(2, len(order), block_rows)
    take = lambda value: jnp.stack([value[:, index] for index in wanted], axis=1)
    place, window, scale = take(place), take(window), take(scale)
    starts = window.T.reshape(-1)
    routes = jnp.stack([place[0].astype(jnp.float32), scale[0], place[1].astype(jnp.float32), scale[1]], axis=-1)
    routes = routes.reshape(len(order) * block_rows, 4)

    parts = 2
    results = []
    for part in range(parts):
        mine, theirs = combine_call(
            part, parts, starts, routes, own_hidden[0], own_hidden[1], hot_hidden[0], hot_hidden[1],
            own_down, copied_low, copied_high,
        )
        results.append(sum_to_owners(mine, theirs, row_count))
    return jnp.concatenate(results, axis=1)[None]


def solution(mesh):
    placed = (
        P("grp", "ep", None),
        P("grp", "ep", None),
        P("grp", "ep", None),
        P("grp", "ep", None, None),
        P("grp", "ep", None, None),
        P("grp", "ep", None, None),
        P("ep"),
    )
    return jax.shard_map(
        local, mesh=mesh, in_specs=placed, out_specs=P("grp", "ep", None), check_vma=False
    )
```

```python
import functools

import jax
import jax.numpy as jnp
from jax import lax
from jax.experimental import pallas as pl
from jax.experimental.pallas import tpu as pltpu
from jax.sharding import PartitionSpec as P

SIDE = 4
SEGMENTS = 1 + SIDE
BLOCK = 4
WINDOW = 128
ALIGN = 16
EARLY = (0, 1, 3)
LATE = (2,)
VMEM = 60 * 1024 * 1024


def ep_of(x, y, core):
    return (x * SIDE + y) * 2 + core


def moved(index, ring, step):
    x, y, core = index // (2 * SIDE), index // 2 % SIDE, index % 2
    if (ring == 0) == (core == 0):
        return ep_of(x, (y + step) % SIDE, core)
    return ep_of((x + step) % SIDE, y, core)


def shift_z(value, step):
    return lax.ppermute(value, "grp", [(i, (i + step) % SIDE) for i in range(SIDE)])


def shift_ring(value, ring, step):
    count = 2 * SIDE * SIDE
    return lax.ppermute(value, "ep", [(i, moved(i, ring, step)) for i in range(count)])


def swap_cores(value):
    count = 2 * SIDE * SIDE
    return lax.ppermute(value, "ep", [(i, i ^ 1) for i in range(count)])


def from_all(shift, value):
    return jnp.stack([value, shift(value, -1), shift(value, 2), shift(value, 1)])


def hidden_kernel(capacity, tile, sources, meta, places, gate_hbm, up_hbm, *rest):
    blocks = len(sources)
    count = max(piece for block in sources for piece, _ in block) + 1
    pieces = rest[:count]
    own_out, hot_out, gate, up, gathered, compact, packed, weight_sems, row_sems = rest[-9:]
    rows = pieces[0].shape[2]
    width, hidden = gate.shape
    block_rows = BLOCK * rows
    me, donates, total = meta[0], meta[1] == 1, meta[2]
    offsets, counts, begins = 3, 3 + SEGMENTS, 3 + 2 * SEGMENTS

    def load(block, distance):
        for unit, (piece, place) in enumerate(sources[block]):
            pltpu.make_async_copy(
                pieces[piece].at[place, distance],
                gathered.at[block, pl.ds(unit * rows, rows)],
                row_sems.at[block],
            ).start()

    def arrive(block):
        pltpu.make_async_copy(gathered.at[block], gathered.at[block], row_sems.at[block]).wait()

    def pick(segment, block):
        start = pl.multiple_of(meta[begins + segment * blocks + block], ALIGN)
        place = places[pl.ds(segment * blocks + block, 1), :] - start
        slots = lax.broadcasted_iota(jnp.int32, (WINDOW, block_rows), 0)
        choose = jnp.where(slots == place, 1.0, 0.0).astype(jnp.bfloat16)

        found = jnp.dot(choose, gathered[block], preferred_element_type=jnp.float32).astype(jnp.bfloat16)
        compact[pl.ds(start, ALIGN), :] = compact[pl.ds(start, ALIGN), :] + found[:ALIGN]
        compact[pl.ds(start + ALIGN, WINDOW - ALIGN), :] = found[ALIGN:]

    weights = (
        pltpu.make_async_copy(gate_hbm, gate, weight_sems.at[0]),
        pltpu.make_async_copy(up_hbm, up, weight_sems.at[1]),
    )
    for block in range(blocks):
        load(block, 0)
    for copy in weights:
        copy.start()
    compact[:ALIGN, :] = jnp.zeros((ALIGN, width), jnp.bfloat16)
    for block in range(blocks):
        arrive(block)
        pick(0, block)

    @pl.when(donates)
    def _():
        def group(distance, carry):
            for block in range(blocks):
                pl.when(distance > 0)(functools.partial(arrive, block))
                pick(1 + distance, block)
                pl.when(distance < SIDE - 1)(functools.partial(load, block, distance + 1))
            return carry
        lax.fori_loop(0, SIDE, group, 0)

    for copy in weights:
        copy.wait()

    def serve(t, carry):
        span = pl.ds(pl.multiple_of(t * tile, tile), tile)
        gate_part = jnp.dot(compact[span, :], gate[...], preferred_element_type=jnp.float32)
        up_part = jnp.dot(compact[span, :], up[...], preferred_element_type=jnp.float32)
        packed[span, :] = (jax.nn.silu(gate_part) * up_part).astype(jnp.bfloat16)
        return carry

    lax.fori_loop(0, lax.div(total + tile - 1, tile), serve, 0)

    def unpack(segment, store):
        for t in range(0, capacity, WINDOW):
            begin = pl.multiple_of(meta[offsets + segment] + t, ALIGN)
            live = lax.broadcasted_iota(jnp.int32, (WINDOW, hidden), 0) < meta[counts + segment] - t
            value = packed[pl.ds(begin, WINDOW), :]
            store(pl.ds(t, WINDOW), jnp.where(live, value, jnp.zeros_like(value)))

    def own_store(span, value):
        own_out[span, :] = value

    unpack(0, own_store)
    for distance in range(SIDE):
        group = lax.rem(me + distance, SIDE)

        def hot_store(span, value):
            hot_out[group, span, :] = value

        unpack(1 + distance, hot_store)


def hidden_call(capacity, tile, sources, meta, places, gate, up, pieces, after=()):
    rows = pieces[0].shape[2]
    width, hidden = gate.shape
    blocks = len(sources)
    block_rows = BLOCK * rows
    most = SEGMENTS * capacity + tile
    anywhere = pl.BlockSpec(memory_space=pl.ANY)
    return pl.pallas_call(
        functools.partial(hidden_kernel, capacity, tile, sources),
        in_specs=[pl.BlockSpec(memory_space=pltpu.SMEM), pl.BlockSpec(memory_space=pltpu.VMEM)]
        + [anywhere] * (2 + len(pieces) + len(after)),
        out_specs=[pl.BlockSpec(memory_space=pltpu.VMEM)] * 2,
        out_shape=[
            jax.ShapeDtypeStruct((capacity, hidden), jnp.bfloat16),
            jax.ShapeDtypeStruct((SIDE, capacity, hidden), jnp.bfloat16),
        ],
        scratch_shapes=[
            pltpu.VMEM((width, hidden), jnp.bfloat16),
            pltpu.VMEM((width, hidden), jnp.bfloat16),
            pltpu.VMEM((blocks, block_rows, width), jnp.bfloat16),
            pltpu.VMEM((most, width), jnp.bfloat16),
            pltpu.VMEM((most, hidden), jnp.bfloat16),
            pltpu.SemaphoreType.DMA((2,)),
            pltpu.SemaphoreType.DMA((blocks,)),
        ],
        compiler_params=pltpu.CompilerParams(vmem_limit_bytes=VMEM),
        cost_estimate=pl.CostEstimate(
            flops=SEGMENTS * capacity * width * hidden * 2,
            bytes_accessed=2 * width * hidden * 2 + 4 * blocks * block_rows * width * 2,
            transcendentals=SEGMENTS * capacity * hidden,
        ),
    )(meta, places, gate, up, *pieces, *after)

def tables(member, grp, donates):
    blocks, block_rows = member.shape[1:]
    after = jnp.cumsum(member.reshape(SEGMENTS, -1), axis=1).reshape(member.shape)
    counts = after[:, -1, -1]
    before = jnp.concatenate([jnp.zeros((SEGMENTS, 1), jnp.int32), after[:, :-1, -1]], axis=1)
    serves = jnp.where(jnp.arange(SEGMENTS) == 0, 1, donates)
    room = (counts + ALIGN - 1) // ALIGN * ALIGN * serves
    offsets = jnp.cumsum(room) - room
    begins = offsets[:, None] + before // ALIGN * ALIGN
    places = jnp.where(member == 1, offsets[:, None, None] + after - 1, -1).reshape(SEGMENTS * blocks, block_rows)
    meta = jnp.concatenate([jnp.stack([grp, donates, jnp.sum(room)]), offsets, counts * serves, begins.reshape(-1)])
    return meta.astype(jnp.int32), places, after, before


def combine_kernel(starts, scales, own_early, own_late, hot_early, hot_late, down, copied, theirs, mine, outs, pair):
    early = own_early.shape[0]
    late = own_late.shape[0]
    total = early + late
    block_rows = mine.shape[0] // SIDE

    outs[:early, :] = jnp.dot(own_early[...], down[...], preferred_element_type=jnp.float32).astype(jnp.bfloat16)
    outs[early:total, :] = jnp.dot(own_late[...], down[...], preferred_element_type=jnp.float32).astype(jnp.bfloat16)
    outs[total:total + early, :] = jnp.dot(hot_early[...], copied[...], preferred_element_type=jnp.float32).astype(jnp.bfloat16)
    outs[total + early:, :] = jnp.dot(hot_late[...], copied[...], preferred_element_type=jnp.float32).astype(jnp.bfloat16)

    for out, first in ((theirs, 0), (mine, SIDE)):
        for b in range(SIDE):
            own_start = pl.multiple_of(starts[2 * (first + b)], ALIGN)
            hot_start = pl.multiple_of(starts[2 * (first + b) + 1], ALIGN)
            pair[first + b, :WINDOW, :] = outs[pl.ds(own_start, WINDOW), :]
            pair[first + b, WINDOW:, :] = outs[pl.ds(total + hot_start, WINDOW), :]
            scale = scales[(first + b) * block_rows:(first + b + 1) * block_rows, :]
            value = jnp.dot(scale, pair[first + b], preferred_element_type=jnp.float32)
            out[b * block_rows:(b + 1) * block_rows, :] = value.astype(jnp.bfloat16)


def combine_call(part, parts, starts, scales, own_early, own_late, hot_early, hot_late, down, copied):
    hidden = down.shape[0]
    width = down.shape[1] // parts
    wide = width // 2 if width % 256 == 0 else width
    rows = scales.shape[0]
    whole = pl.BlockSpec(memory_space=pltpu.VMEM)
    offset = part * (width // wide)
    column = pl.BlockSpec((hidden, wide), lambda n: (0, offset + n))
    result = pl.BlockSpec((rows // 2, wide), lambda n: (0, n))
    slots = 2 * (own_early.shape[0] + own_late.shape[0])
    return pl.pallas_call(
        combine_kernel,
        grid=(width // wide,),
        in_specs=[pl.BlockSpec(memory_space=pltpu.SMEM)] + [whole] * 5 + [column, column],
        out_specs=[result, result],
        out_shape=[jax.ShapeDtypeStruct((rows // 2, width), jnp.bfloat16)] * 2,
        scratch_shapes=[pltpu.VMEM((slots, wide), jnp.bfloat16), pltpu.VMEM((2 * SIDE, 2 * WINDOW, wide), jnp.bfloat16)],
        compiler_params=pltpu.CompilerParams(vmem_limit_bytes=VMEM),
        cost_estimate=pl.CostEstimate(
            flops=2 * slots * hidden * width + 4 * rows * WINDOW * width,
            bytes_accessed=4 * hidden * width + 2 * rows * width,
            transcendentals=0,
        ),
    )(starts, scales, own_early, own_late, hot_early, hot_late, down, copied)


def add(*values):
    return sum(v.astype(jnp.float32) for v in values).astype(jnp.bfloat16)


def sum_to_owners(theirs, mine, rows):
    width = mine.shape[1]
    total = add(mine, swap_cores(theirs)).reshape(SIDE, SIDE, rows, width)
    for ring, shape in ((1, (SIDE, rows, width)), (0, (rows, width))):
        cut = shape[0] // 2
        ahead = shift_ring(total[2, :cut], ring, 1)
        behind = shift_ring(total[2, cut:], ring, -1)
        forward = jnp.concatenate([add(total[1, :cut], ahead), total[1, cut:]], axis=0)
        backward = jnp.concatenate([total[3, :cut], add(total[3, cut:], behind)], axis=0)
        total = add(total[0], shift_ring(forward, ring, 1), shift_ring(backward, ring, -1))
    return total


def local(tokens, route_ids, route_gates, w_gate, w_up, w_down, hot_source):
    n_ep = lax.axis_size("ep")
    grp, ep = lax.axis_index("grp"), lax.axis_index("ep")
    core, x, y = lax.rem(ep, 2), ep // (2 * SIDE), lax.rem(ep // 2, SIDE)
    rows = tokens[0]
    row_count, width = rows.shape
    picks = route_ids.shape[2]
    cap = row_count * picks // n_ep
    donor = hot_source[0]
    own_gate, own_up, own_down = w_gate[0, 0], w_up[0, 0], w_down[0, 0]

    info = jnp.concatenate([route_ids[0].astype(jnp.bfloat16), route_gates[0]], axis=1).T
    info = info.reshape(-1, 128)
    info = from_all(shift_z, info)
    info = from_all(lambda value, step: shift_ring(value, 0, step), info)
    info = from_all(lambda value, step: shift_ring(value, 1, step), info)
    info = jnp.stack([info, swap_cores(info)])
    info = info.reshape(2 * SIDE, SIDE, SIDE, 2 * picks, row_count)

    below, above = shift_z(rows, 1), shift_z(rows, -1)
    cut = row_count // 2
    far = (shift_z(below[:cut], 1), shift_z(above[cut:], -1))
    unit = jnp.stack([rows, above, jnp.concatenate(far, axis=0), below])
    gives = (donor == grp) & (unit[2, 0, 0] == unit[2, 0, 0])
    copied = lax.psum(jnp.where(gives, own_down, jnp.zeros_like(own_down)), "grp")
    below, above = shift_ring(unit, 0, 1), shift_ring(unit, 0, -1)
    far = (shift_ring(below[:2], 0, 1), shift_ring(above[2:], 0, -1))
    low, high = jnp.stack([unit, above]), jnp.stack([jnp.concatenate(far, axis=0), below])
    low_below, high_above = shift_ring(low, 1, 1), shift_ring(high, 1, -1)
    high_below, low_above = shift_ring(high, 1, 1), shift_ring(low, 1, -1)
    low_far, high_far = shift_ring(low_below, 1, 1), shift_ring(high_above, 1, -1)
    early = [low, high, low_above, high_above, low_below, high_below]
    early = early + [swap_cores(piece) for piece in early]
    late = [low_far, high_far]
    late = late + [swap_cores(piece) for piece in late]

    order = [(other, second) for seconds in (EARLY, LATE) for other in (0, 1) for second in seconds]
    info = jnp.stack([info[other * SIDE + second] for other, second in order])
    ids = info[:, :, :, :picks].astype(jnp.int32)
    gates = info[:, :, :, picks:].astype(jnp.float32)
    is_own, is_hot = ids[:, :, 0] == ep, ids == ep + n_ep
    block_rows = BLOCK * row_count
    member = jnp.concatenate([jnp.any(is_own, axis=2)[:, :, None], jnp.any(is_hot, axis=3)], axis=2)
    member = member.transpose(2, 0, 1, 3).reshape(SEGMENTS, len(order), block_rows).astype(jnp.int32)
    own_scale = jnp.sum(jnp.where(is_own, gates[:, :, 0], 0.0), axis=2).reshape(len(order), block_rows)
    hot_scale = jnp.sum(jnp.where(is_hot[:, :, 0], gates[:, :, 0], 0.0), axis=2).reshape(len(order), block_rows)
    donates = (donor == grp).astype(jnp.int32)

    first_late = 2 * len(EARLY)
    early_slots, late_slots = first_late * BLOCK * cap, 2 * len(LATE) * BLOCK * cap
    early_meta, early_places, early_after, early_before = tables(member[:, :first_late], grp, donates)
    late_meta, late_places, late_after, late_before = tables(member[:, first_late:], grp, donates)
    piece_of = {0: 0, 1: 2, 3: 4}
    early_sources = [
        [(6 * other + piece_of[second] + first // 2, first % 2) for first in range(SIDE)]
        for other, second in order[:first_late]
    ]
    late_sources = [[(2 * other + first // 2, first % 2) for first in range(SIDE)] for other, _ in order[first_late:]]

    def sent_back(hot):
        return lax.psum_scatter(hot.reshape(-1, hot.shape[2]), "grp", tiled=True)

    own_early, hot_early = hidden_call(
        early_slots, 256, early_sources, early_meta, early_places, own_gate, own_up, early
    )
    own_late, hot_late = hidden_call(
        late_slots, 128, late_sources, late_meta, late_places, own_gate, own_up, late, after=(own_early,)
    )
    hot_early, hot_late = sent_back(hot_early), sent_back(hot_late)

    after = jnp.concatenate([early_after[:2], late_after[:2] + early_slots], axis=1)
    before = jnp.concatenate([early_before[:2], late_before[:2] + early_slots], axis=1)
    wanted = [order.index((other, second)) for other in (1, 0) for second in range(SIDE)]
    take = lambda value: jnp.stack([value[:, index] for index in wanted], axis=1)
    starts = take(jnp.minimum(before // ALIGN * ALIGN, early_slots + late_slots - WINDOW))
    slots = jnp.arange(WINDOW, dtype=jnp.int32)
    chosen = (take(after) - 1 - starts[:, :, None])[..., None] == slots
    scale = take(jnp.stack([own_scale, hot_scale]))[..., None]
    scales = jnp.where(chosen, scale, 0.0).astype(jnp.bfloat16)
    scales = jnp.concatenate([scales[0], scales[1]], axis=-1).reshape(len(order) * block_rows, 2 * WINDOW)
    starts = starts.T.reshape(-1)

    parts = 2
    results = []
    for part in range(parts):
        theirs, mine = combine_call(
            part, parts, starts, scales, own_early, own_late, hot_early, hot_late, own_down, copied
        )
        results.append(sum_to_owners(theirs, mine, row_count))
    return jnp.concatenate(results, axis=1)[None]


def solution(mesh):
    placed = (
        P("grp", "ep", None),
        P("grp", "ep", None),
        P("grp", "ep", None),
        P("grp", "ep", None, None),
        P("grp", "ep", None, None),
        P("grp", "ep", None, None),
        P("ep"),
    )
    return jax.shard_map(
        local, mesh=mesh, in_specs=placed, out_specs=P("grp", "ep", None), check_vma=False
    )
```

```python
import functools

import jax
import jax.numpy as jnp
from jax import lax
from jax.experimental import pallas as pl
from jax.experimental.pallas import tpu as pltpu
from jax.sharding import PartitionSpec as P

SIDE = 4
SEGMENTS = 1 + SIDE
BLOCK = 4
WINDOW = 128
ALIGN = 16
STAGES = ((0,), (1, 3), (2,))
VMEM = 60 * 1024 * 1024


def ep_of(x, y, core):
    return (x * SIDE + y) * 2 + core


def moved(index, ring, step):
    x, y, core = index // (2 * SIDE), index // 2 % SIDE, index % 2
    if (ring == 0) == (core == 0):
        return ep_of(x, (y + step) % SIDE, core)
    return ep_of((x + step) % SIDE, y, core)


def shift_z(value, step):
    return lax.ppermute(value, "grp", [(i, (i + step) % SIDE) for i in range(SIDE)])


def shift_ring(value, ring, step):
    count = 2 * SIDE * SIDE
    return lax.ppermute(value, "ep", [(i, moved(i, ring, step)) for i in range(count)])


def swap_cores(value):
    count = 2 * SIDE * SIDE
    return lax.ppermute(value, "ep", [(i, i ^ 1) for i in range(count)])


def from_all(shift, value):
    return jnp.stack([value, shift(value, -1), shift(value, 2), shift(value, 1)])


def tie(value, *others):
    anywhere = pl.BlockSpec(memory_space=pl.ANY)
    return pl.pallas_call(
        lambda *refs: None,
        in_specs=[anywhere] * (1 + len(others)),
        out_specs=anywhere,
        out_shape=jax.ShapeDtypeStruct(value.shape, value.dtype),
        input_output_aliases={0: 0},
    )(value, *others)


def hidden_kernel(capacity, tile, sources, meta, places, gate_hbm, up_hbm, *rest):
    blocks = len(sources)
    count = max(piece for block in sources for piece, _ in block) + 1
    pieces = rest[:count]
    own_out, hot_out, gate, up, gathered, compact, packed, weight_sems, row_sems = rest[-9:]
    rows = pieces[0].shape[2]
    width, hidden = gate.shape
    block_rows = BLOCK * rows
    donates, total = meta[0] == 1, meta[1]
    offsets, counts, begins = 2, 2 + SEGMENTS, 2 + 2 * SEGMENTS

    def load(block, distance):
        for unit, (piece, place) in enumerate(sources[block]):
            pltpu.make_async_copy(
                pieces[piece].at[place, distance],
                gathered.at[block, pl.ds(unit * rows, rows)],
                row_sems.at[block],
            ).start()

    def arrive(block):
        pltpu.make_async_copy(gathered.at[block], gathered.at[block], row_sems.at[block]).wait()

    def pick(segment, block):
        start = pl.multiple_of(meta[begins + segment * blocks + block], ALIGN)
        place = places[pl.ds(segment * blocks + block, 1), :] - start
        slots = lax.broadcasted_iota(jnp.int32, (WINDOW, block_rows), 0)
        choose = jnp.where(slots == place, 1.0, 0.0).astype(jnp.bfloat16)

        found = jnp.dot(choose, gathered[block], preferred_element_type=jnp.float32).astype(jnp.bfloat16)
        compact[pl.ds(start, ALIGN), :] = compact[pl.ds(start, ALIGN), :] + found[:ALIGN]
        compact[pl.ds(start + ALIGN, WINDOW - ALIGN), :] = found[ALIGN:]

    weights = (
        pltpu.make_async_copy(gate_hbm, gate, weight_sems.at[0]),
        pltpu.make_async_copy(up_hbm, up, weight_sems.at[1]),
    )
    for block in range(blocks):
        load(block, 0)
    for copy in weights:
        copy.start()
    compact[:ALIGN, :] = jnp.zeros((ALIGN, width), jnp.bfloat16)
    for block in range(blocks):
        arrive(block)
        pick(0, block)

    @pl.when(donates)
    def _():
        def group(distance, carry):
            for block in range(blocks):
                pl.when(distance > 0)(functools.partial(arrive, block))
                pick(1 + distance, block)
                pl.when(distance < SIDE - 1)(functools.partial(load, block, distance + 1))
            return carry
        lax.fori_loop(0, SIDE, group, 0)

    for copy in weights:
        copy.wait()

    def serve(t, carry):
        span = pl.ds(pl.multiple_of(t * tile, tile), tile)
        gate_part = jnp.dot(compact[span, :], gate[...], preferred_element_type=jnp.float32)
        up_part = jnp.dot(compact[span, :], up[...], preferred_element_type=jnp.float32)
        packed[span, :] = (jax.nn.silu(gate_part) * up_part).astype(jnp.bfloat16)
        return carry

    lax.fori_loop(0, lax.div(total + tile - 1, tile), serve, 0)

    def unpack(segment, store):
        for t in range(0, capacity, WINDOW):
            begin = pl.multiple_of(meta[offsets + segment] + t, ALIGN)
            live = lax.broadcasted_iota(jnp.int32, (WINDOW, hidden), 0) < meta[counts + segment] - t
            value = packed[pl.ds(begin, WINDOW), :]
            store(pl.ds(t, WINDOW), jnp.where(live, value, jnp.zeros_like(value)))

    def own_store(span, value):
        own_out[span, :] = value

    unpack(0, own_store)
    for distance in range(SIDE):

        def hot_store(span, value, distance=distance):
            hot_out[distance, span, :] = value

        unpack(1 + distance, hot_store)


def hidden_call(capacity, tile, sources, meta, places, gate, up, pieces, after=()):
    rows = pieces[0].shape[2]
    width, hidden = gate.shape
    blocks = len(sources)
    block_rows = BLOCK * rows
    most = SEGMENTS * capacity + tile
    anywhere = pl.BlockSpec(memory_space=pl.ANY)
    return pl.pallas_call(
        functools.partial(hidden_kernel, capacity, tile, sources),
        in_specs=[pl.BlockSpec(memory_space=pltpu.SMEM), pl.BlockSpec(memory_space=pltpu.VMEM)]
        + [anywhere] * (2 + len(pieces) + len(after)),
        out_specs=[pl.BlockSpec(memory_space=pltpu.VMEM)] * 2,
        out_shape=[
            jax.ShapeDtypeStruct((capacity, hidden), jnp.bfloat16),
            jax.ShapeDtypeStruct((SIDE, capacity, hidden), jnp.bfloat16),
        ],
        scratch_shapes=[
            pltpu.VMEM((width, hidden), jnp.bfloat16),
            pltpu.VMEM((width, hidden), jnp.bfloat16),
            pltpu.VMEM((blocks, block_rows, width), jnp.bfloat16),
            pltpu.VMEM((most, width), jnp.bfloat16),
            pltpu.VMEM((most, hidden), jnp.bfloat16),
            pltpu.SemaphoreType.DMA((2,)),
            pltpu.SemaphoreType.DMA((blocks,)),
        ],
        compiler_params=pltpu.CompilerParams(vmem_limit_bytes=VMEM),
        cost_estimate=pl.CostEstimate(
            flops=SEGMENTS * capacity * width * hidden * 2,
            bytes_accessed=2 * width * hidden * 2 + 4 * blocks * block_rows * width * 2,
            transcendentals=SEGMENTS * capacity * hidden,
        ),
    )(meta, places, gate, up, *pieces, *after)

def tables(member, donates):
    blocks, block_rows = member.shape[1:]
    after = jnp.cumsum(member.reshape(SEGMENTS, -1), axis=1).reshape(member.shape)
    counts = after[:, -1, -1]
    before = jnp.concatenate([jnp.zeros((SEGMENTS, 1), jnp.int32), after[:, :-1, -1]], axis=1)
    serves = jnp.where(jnp.arange(SEGMENTS) == 0, 1, donates)
    room = (counts + ALIGN - 1) // ALIGN * ALIGN * serves
    offsets = jnp.cumsum(room) - room
    begins = offsets[:, None] + before // ALIGN * ALIGN
    places = jnp.where(member == 1, offsets[:, None, None] + after - 1, -1).reshape(SEGMENTS * blocks, block_rows)
    meta = jnp.concatenate([jnp.stack([donates, jnp.sum(room)]), offsets, counts * serves, begins.reshape(-1)])
    return meta.astype(jnp.int32), places, after, before


def combine_kernel(owns, hots, steps, starts, scales, *rest):
    own, hot = rest[:owns], rest[owns : owns + hots]
    copied = rest[owns + hots : owns + hots + steps]
    down, theirs, mine, outs, pair = rest[owns + hots + steps :]
    block_rows = mine.shape[0] // SIDE
    total = sum(ref.shape[0] for ref in own)

    def apply(begin, refs, weight):
        for ref in refs:
            value = jnp.dot(ref[...], weight[...], preferred_element_type=jnp.float32)
            outs[begin : begin + ref.shape[0], :] = value.astype(jnp.bfloat16)
            begin += ref.shape[0]

    apply(0, own, down)
    for step in range(steps):
        pl.when(pl.program_id(0) == step)(functools.partial(apply, total, hot, copied[step]))

    for out, first in ((theirs, 0), (mine, SIDE)):
        for b in range(SIDE):
            own_start = pl.multiple_of(starts[2 * (first + b)], ALIGN)
            hot_start = pl.multiple_of(starts[2 * (first + b) + 1], ALIGN)
            pair[first + b, :WINDOW, :] = outs[pl.ds(own_start, WINDOW), :]
            pair[first + b, WINDOW:, :] = outs[pl.ds(total + hot_start, WINDOW), :]
            scale = scales[(first + b) * block_rows : (first + b + 1) * block_rows, :]
            value = jnp.dot(scale, pair[first + b], preferred_element_type=jnp.float32)
            out[b * block_rows : (b + 1) * block_rows, :] = value.astype(jnp.bfloat16)


def combine_call(part, starts, scales, own, hot, copied, down):
    hidden, wide = copied[0].shape
    steps = len(copied)
    width = wide * steps
    rows = scales.shape[0]
    whole = pl.BlockSpec(memory_space=pltpu.VMEM)
    column = pl.BlockSpec((hidden, wide), lambda n: (0, part * steps + n))
    result = pl.BlockSpec((rows // 2, wide), lambda n: (0, n))
    slots = 2 * sum(value.shape[0] for value in own)
    return pl.pallas_call(
        functools.partial(combine_kernel, len(own), len(hot), steps),
        grid=(steps,),
        in_specs=[pl.BlockSpec(memory_space=pltpu.SMEM)] + [whole] * (1 + len(own) + len(hot) + steps) + [column],
        out_specs=[result, result],
        out_shape=[jax.ShapeDtypeStruct((rows // 2, width), jnp.bfloat16)] * 2,
        scratch_shapes=[pltpu.VMEM((slots, wide), jnp.bfloat16), pltpu.VMEM((2 * SIDE, 2 * WINDOW, wide), jnp.bfloat16)],
        compiler_params=pltpu.CompilerParams(vmem_limit_bytes=VMEM),
        cost_estimate=pl.CostEstimate(
            flops=2 * slots * hidden * width + 4 * rows * WINDOW * width,
            bytes_accessed=4 * hidden * width + 2 * rows * width,
            transcendentals=0,
        ),
    )(starts, scales, *own, *hot, *copied, down)


def add(*values):
    return sum(v.astype(jnp.float32) for v in values).astype(jnp.bfloat16)


def sent_back(hot):
    cut = hot.shape[1] // 2
    ahead, behind = shift_z(hot[2, :cut], 1), shift_z(hot[2, cut:], -1)
    forward = jnp.concatenate([hot[1, :cut] + ahead, hot[1, cut:]], axis=0)
    backward = jnp.concatenate([hot[3, :cut], hot[3, cut:] + behind], axis=0)
    return hot[0] + shift_z(forward, 1) + shift_z(backward, -1)


def sum_to_owners(theirs, mine, rows):
    width = mine.shape[1]
    total = add(mine, swap_cores(theirs)).reshape(SIDE, SIDE, rows, width)
    cut = SIDE // 2
    ahead = shift_ring(total[2, :cut], 1, 1)
    behind = shift_ring(total[2, cut:], 1, -1)
    forward = jnp.concatenate([add(total[1, :cut], ahead), total[1, cut:]], axis=0)
    backward = jnp.concatenate([total[3, :cut], add(total[3, cut:], behind)], axis=0)
    total = add(total[0], shift_ring(forward, 1, 1), shift_ring(backward, 1, -1))
    return add(total[0], shift_ring(total[1], 0, 1), shift_ring(total[3], 0, -1), shift_ring(total[2], 0, 2))


def local(tokens, route_ids, route_gates, w_gate, w_up, w_down, hot_source):
    n_ep = lax.axis_size("ep")
    grp, ep = lax.axis_index("grp"), lax.axis_index("ep")
    core, x, y = lax.rem(ep, 2), ep // (2 * SIDE), lax.rem(ep // 2, SIDE)
    rows = tokens[0]
    row_count, width = rows.shape
    picks = route_ids.shape[2]
    cap = row_count * picks // n_ep
    donor = hot_source[0]
    own_gate, own_up, own_down = w_gate[0, 0], w_up[0, 0], w_down[0, 0]

    parts, steps = 2, 2
    wide = width // (parts * steps)

    def down_part(index):
        columns = own_down[:, index * wide : (index + 1) * wide]
        return jnp.where(donor == grp, columns, jnp.zeros_like(columns))

    given = down_part(0)
    copied = [lax.psum(given, "grp")]

    info = jnp.concatenate([route_ids[0].astype(jnp.bfloat16), route_gates[0]], axis=1).T
    info = from_all(shift_z, info.reshape(-1, 128))
    below, above = shift_z(rows, 1), shift_z(rows, -1)
    cut = row_count // 2
    info = from_all(lambda value, step: shift_ring(value, 0, step), tie(info, below, above))
    far = (shift_z(below[:cut], 1), shift_z(above[cut:], -1))
    unit = tie(jnp.stack([rows, above, jnp.concatenate(far, axis=0), below]), info, given)
    below, above = shift_ring(unit, 0, 1), shift_ring(unit, 0, -1)
    info = from_all(lambda value, step: shift_ring(value, 1, step), info)
    far = (shift_ring(below[:2], 0, 1), shift_ring(above[2:], 0, -1))
    info = jnp.stack([info, swap_cores(info)])
    info = info.reshape(2 * SIDE, SIDE, SIDE, 2 * picks, row_count)
    low, high = jnp.stack([unit, above]), jnp.stack([jnp.concatenate(far, axis=0), below])
    low = tie(low, info)
    low_below, high_above = shift_ring(low, 1, 1), shift_ring(high, 1, -1)
    near = [low, high] + [swap_cores(low), swap_cores(high)]
    high_on, low_on = tie(high, low_below, high_above, copied[0]), tie(low, low_below, high_above, copied[0])
    copied.append(lax.psum(tie(down_part(1), copied[0]), "grp"))
    high_below, low_above = shift_ring(high_on, 1, 1), shift_ring(low_on, 1, -1)
    low_on, high_on = tie(low_below, high_below, low_above), tie(high_above, high_below, low_above)
    low_far, high_far = shift_ring(low_on, 1, 1), shift_ring(high_on, 1, -1)
    high_below, low_above = tie(high_below, copied[1]), tie(low_above, copied[1])
    copied.append(lax.psum(tie(down_part(2), copied[1]), "grp"))
    copied.append(lax.psum(tie(down_part(3), copied[2]), "grp"))
    beside = [low_above, high_above, low_below, high_below]
    beside = beside + [swap_cores(piece) for piece in beside]

    order = [(other, second) for seconds in STAGES for other in (0, 1) for second in seconds]
    info = jnp.stack([info[other * SIDE + second] for other, second in order])
    ids = info[:, :, :, :picks].astype(jnp.int32)
    gates = info[:, :, :, picks:].astype(jnp.float32)
    is_own, is_hot = ids[:, :, 0] == ep, ids == ep + n_ep
    block_rows = BLOCK * row_count
    member = jnp.concatenate([jnp.any(is_own, axis=2)[:, :, None], jnp.any(is_hot, axis=3)], axis=2)
    member = member.transpose(2, 0, 1, 3).reshape(SEGMENTS, len(order), block_rows).astype(jnp.int32)
    own_scale = jnp.sum(jnp.where(is_own, gates[:, :, 0], 0.0), axis=2).reshape(len(order), block_rows)
    hot_scale = jnp.sum(jnp.where(is_hot[:, :, 0], gates[:, :, 0], 0.0), axis=2).reshape(len(order), block_rows)
    donates = (donor == grp).astype(jnp.int32)

    own_hidden, hot_hidden, afters, befores = [], [], [], []
    begin, begin_slot = 0, 0
    for stage, seconds in enumerate(STAGES):
        if stage == 2:
            far = [tie(piece, own_hidden[-1], copied[2]) for piece in (low_far, high_far)]
            pieces = far + [swap_cores(piece) for piece in far]
        else:
            pieces = (near, beside)[stage]
        blocks = 2 * len(seconds)
        slots = blocks * BLOCK * cap
        meta, places, after, before = tables(member[:, begin : begin + blocks], donates)
        sources = [
            [(2 * block + first // 2, first % 2) for first in range(SIDE)] for block in range(blocks)
        ]
        own, hot = hidden_call(
            slots, 256 if blocks > 2 else 128, sources, meta, places, own_gate, own_up, pieces, after=own_hidden[-1:]
        )
        own_hidden.append(own)
        hot_hidden.append(hot)
        afters.append(after[:2] + begin_slot)
        befores.append(before[:2] + begin_slot)
        begin, begin_slot = begin + blocks, begin_slot + slots

    early = sent_back(jnp.concatenate(hot_hidden[:-1], axis=1))
    late = sent_back(tie(hot_hidden[-1], copied[3]))
    hot_hidden = [early, late]

    after, before = jnp.concatenate(afters, axis=1), jnp.concatenate(befores, axis=1)
    wanted = [order.index((other, second)) for other in (1, 0) for second in range(SIDE)]
    take = lambda value: jnp.stack([value[:, index] for index in wanted], axis=1)
    starts = take(jnp.minimum(before // ALIGN * ALIGN, begin_slot - WINDOW))
    slots = jnp.arange(WINDOW, dtype=jnp.int32)
    chosen = (take(after) - 1 - starts[:, :, None])[..., None] == slots
    scale = take(jnp.stack([own_scale, hot_scale]))[..., None]
    scales = jnp.where(chosen, scale, 0.0).astype(jnp.bfloat16)
    scales = jnp.concatenate([scales[0], scales[1]], axis=-1).reshape(len(order) * block_rows, 2 * WINDOW)
    starts = starts.T.reshape(-1)

    results = []
    for part in range(parts):
        here = copied[part * steps : (part + 1) * steps]
        theirs, mine = combine_call(part, starts, scales, own_hidden, hot_hidden, here, own_down)
        results.append(sum_to_owners(theirs, mine, row_count))
    return jnp.concatenate(results, axis=1)[None]


def solution(mesh):
    placed = (
        P("grp", "ep", None),
        P("grp", "ep", None),
        P("grp", "ep", None),
        P("grp", "ep", None, None),
        P("grp", "ep", None, None),
        P("grp", "ep", None, None),
        P("ep"),
    )
    return jax.shard_map(
        local, mesh=mesh, in_specs=placed, out_specs=P("grp", "ep", None), check_vma=False
    )
```

```python
import functools

import jax
import jax.numpy as jnp
from jax import lax
from jax.experimental import pallas as pl
from jax.experimental.pallas import tpu as pltpu
from jax.sharding import PartitionSpec as P

SIDE = 4
SEGMENTS = 1 + SIDE
BLOCK = 4
WINDOW = 128
ALIGN = 16
STAGES = ((0,), (1, 3), (2,))
VMEM = 60 * 1024 * 1024


def ep_of(x, y, core):
    return (x * SIDE + y) * 2 + core


def moved(index, ring, step):
    x, y, core = index // (2 * SIDE), index // 2 % SIDE, index % 2
    if (ring == 0) == (core == 0):
        return ep_of(x, (y + step) % SIDE, core)
    return ep_of((x + step) % SIDE, y, core)


def shift_z(value, step):
    return lax.ppermute(value, "grp", [(i, (i + step) % SIDE) for i in range(SIDE)])


def shift_ring(value, ring, step):
    count = 2 * SIDE * SIDE
    return lax.ppermute(value, "ep", [(i, moved(i, ring, step)) for i in range(count)])


def swap_cores(value):
    count = 2 * SIDE * SIDE
    return lax.ppermute(value, "ep", [(i, i ^ 1) for i in range(count)])


def pass_on(value):
    count = 2 * SIDE * SIDE
    pairs = [(g * count + i, (g + 1 - 2 * (i % 2)) % SIDE * count + i) for g in range(SIDE) for i in range(count)]
    return lax.ppermute(value, ("grp", "ep"), pairs)


def from_all(shift, value):
    return jnp.stack([value, shift(value, -1), shift(value, 2), shift(value, 1)])


def tie(value, *others):
    anywhere = pl.BlockSpec(memory_space=pl.ANY)
    return pl.pallas_call(
        lambda *refs: None,
        in_specs=[anywhere] * (1 + len(others)),
        out_specs=anywhere,
        out_shape=jax.ShapeDtypeStruct(value.shape, value.dtype),
        input_output_aliases={0: 0},
    )(value, *others)


def hidden_kernel(capacity, tile, sources, meta, places, gate_hbm, up_hbm, *rest):
    blocks = len(sources)
    count = max(piece for block in sources for piece, _ in block) + 1
    pieces = rest[:count]
    own_out, hot_out, gate, up, gathered, compact, packed, weight_sems, row_sems = rest[-9:]
    rows = pieces[0].shape[2]
    width, hidden = gate.shape
    block_rows = BLOCK * rows
    donates, total = meta[0] == 1, meta[1]
    offsets, counts, begins = 2, 2 + SEGMENTS, 2 + 2 * SEGMENTS

    def load(block, distance):
        for unit, (piece, place) in enumerate(sources[block]):
            pltpu.make_async_copy(
                pieces[piece].at[place, distance],
                gathered.at[block, pl.ds(unit * rows, rows)],
                row_sems.at[block],
            ).start()

    def arrive(block):
        pltpu.make_async_copy(gathered.at[block], gathered.at[block], row_sems.at[block]).wait()

    def pick(segment, block):
        start = pl.multiple_of(meta[begins + segment * blocks + block], ALIGN)
        place = places[pl.ds(segment * blocks + block, 1), :] - start
        slots = lax.broadcasted_iota(jnp.int32, (WINDOW, block_rows), 0)
        choose = jnp.where(slots == place, 1.0, 0.0).astype(jnp.bfloat16)

        found = jnp.dot(choose, gathered[block], preferred_element_type=jnp.float32).astype(jnp.bfloat16)
        compact[pl.ds(start, ALIGN), :] = compact[pl.ds(start, ALIGN), :] + found[:ALIGN]
        compact[pl.ds(start + ALIGN, WINDOW - ALIGN), :] = found[ALIGN:]

    weights = (
        pltpu.make_async_copy(gate_hbm, gate, weight_sems.at[0]),
        pltpu.make_async_copy(up_hbm, up, weight_sems.at[1]),
    )
    for block in range(blocks):
        load(block, 0)
    for copy in weights:
        copy.start()
    compact[:ALIGN, :] = jnp.zeros((ALIGN, width), jnp.bfloat16)
    for block in range(blocks):
        arrive(block)
        pick(0, block)

    @pl.when(donates)
    def _():
        def group(distance, carry):
            for block in range(blocks):
                pl.when(distance > 0)(functools.partial(arrive, block))
                pick(1 + distance, block)
                pl.when(distance < SIDE - 1)(functools.partial(load, block, distance + 1))
            return carry
        lax.fori_loop(0, SIDE, group, 0)

    for copy in weights:
        copy.wait()

    def serve(t, carry):
        span = pl.ds(pl.multiple_of(t * tile, tile), tile)
        gate_part = jnp.dot(compact[span, :], gate[...], preferred_element_type=jnp.float32)
        up_part = jnp.dot(compact[span, :], up[...], preferred_element_type=jnp.float32)
        packed[span, :] = (jax.nn.silu(gate_part) * up_part).astype(jnp.bfloat16)
        return carry

    lax.fori_loop(0, lax.div(total + tile - 1, tile), serve, 0)

    def unpack(segment, store):
        for t in range(0, capacity, WINDOW):
            begin = pl.multiple_of(meta[offsets + segment] + t, ALIGN)
            live = lax.broadcasted_iota(jnp.int32, (WINDOW, hidden), 0) < meta[counts + segment] - t
            value = packed[pl.ds(begin, WINDOW), :]
            store(pl.ds(t, WINDOW), jnp.where(live, value, jnp.zeros_like(value)))

    def own_store(span, value):
        own_out[span, :] = value

    unpack(0, own_store)
    for distance in range(SIDE):

        def hot_store(span, value, distance=distance):
            hot_out[distance, span, :] = value

        unpack(1 + distance, hot_store)


def hidden_call(capacity, tile, sources, meta, places, gate, up, pieces, after=()):
    rows = pieces[0].shape[2]
    width, hidden = gate.shape
    blocks = len(sources)
    block_rows = BLOCK * rows
    most = SEGMENTS * capacity + tile
    anywhere = pl.BlockSpec(memory_space=pl.ANY)
    return pl.pallas_call(
        functools.partial(hidden_kernel, capacity, tile, sources),
        in_specs=[pl.BlockSpec(memory_space=pltpu.SMEM), pl.BlockSpec(memory_space=pltpu.VMEM)]
        + [anywhere] * (2 + len(pieces) + len(after)),
        out_specs=[pl.BlockSpec(memory_space=pltpu.VMEM)] * 2,
        out_shape=[
            jax.ShapeDtypeStruct((capacity, hidden), jnp.bfloat16),
            jax.ShapeDtypeStruct((SIDE, capacity, hidden), jnp.bfloat16),
        ],
        scratch_shapes=[
            pltpu.VMEM((width, hidden), jnp.bfloat16),
            pltpu.VMEM((width, hidden), jnp.bfloat16),
            pltpu.VMEM((blocks, block_rows, width), jnp.bfloat16),
            pltpu.VMEM((most, width), jnp.bfloat16),
            pltpu.VMEM((most, hidden), jnp.bfloat16),
            pltpu.SemaphoreType.DMA((2,)),
            pltpu.SemaphoreType.DMA((blocks,)),
        ],
        compiler_params=pltpu.CompilerParams(vmem_limit_bytes=VMEM),
        cost_estimate=pl.CostEstimate(
            flops=SEGMENTS * capacity * width * hidden * 2,
            bytes_accessed=2 * width * hidden * 2 + 4 * blocks * block_rows * width * 2,
            transcendentals=SEGMENTS * capacity * hidden,
        ),
    )(meta, places, gate, up, *pieces, *after)

def tables(member, donates):
    blocks, block_rows = member.shape[1:]
    after = jnp.cumsum(member.reshape(SEGMENTS, -1), axis=1).reshape(member.shape)
    counts = after[:, -1, -1]
    before = jnp.concatenate([jnp.zeros((SEGMENTS, 1), jnp.int32), after[:, :-1, -1]], axis=1)
    serves = jnp.where(jnp.arange(SEGMENTS) == 0, 1, donates)
    room = (counts + ALIGN - 1) // ALIGN * ALIGN * serves
    offsets = jnp.cumsum(room) - room
    begins = offsets[:, None] + before // ALIGN * ALIGN
    places = jnp.where(member == 1, offsets[:, None, None] + after - 1, -1).reshape(SEGMENTS * blocks, block_rows)
    meta = jnp.concatenate([jnp.stack([donates, jnp.sum(room)]), offsets, counts * serves, begins.reshape(-1)])
    return meta.astype(jnp.int32), places, after, before


def down_kernel(stages, *rest):
    owns, hots = rest[:stages], rest[stages : stages + 1]
    down, low, high, out = rest[stages + 1 :]
    half = low.shape[0]
    begin = 0
    for ref in owns:
        value = jnp.dot(ref[...], down[...], preferred_element_type=jnp.float32)
        out[begin : begin + ref.shape[0], :] = value.astype(jnp.bfloat16)
        begin += ref.shape[0]
    for ref in hots:
        value = jnp.dot(ref[:, :half], low[...], preferred_element_type=jnp.float32)
        value += jnp.dot(ref[:, half:], high[...], preferred_element_type=jnp.float32)
        out[begin:, :] = value.astype(jnp.bfloat16)


def down_call(own, hot, down, low, high):
    hidden, width = down.shape
    wide = 512
    slots = sum(value.shape[0] for value in own) + hot.shape[0]
    whole = pl.BlockSpec(memory_space=pltpu.VMEM)
    column = lambda value: pl.BlockSpec((value.shape[0], wide), lambda n: (0, n))
    return pl.pallas_call(
        functools.partial(down_kernel, len(own)),
        grid=(width // wide,),
        in_specs=[whole] * (1 + len(own)) + [column(down), column(low), column(high)],
        out_specs=pl.BlockSpec((slots, wide), lambda n: (0, n)),
        out_shape=jax.ShapeDtypeStruct((slots, width), jnp.bfloat16),
        compiler_params=pltpu.CompilerParams(vmem_limit_bytes=VMEM),
        cost_estimate=pl.CostEstimate(
            flops=2 * slots * hidden * width, bytes_accessed=2 * width * (2 * hidden + slots), transcendentals=0
        ),
    )(*own, hot, down, low, high)


def combine_kernel(is_late, starts, scales, given, hot, low, high, theirs, mine, late, pair):
    block_rows = mine.shape[0] // SIDE
    half = low.shape[0]
    total = given.shape[0] + late.shape[0]
    value = jnp.dot(hot[:, :half], low[...], preferred_element_type=jnp.float32)
    value += jnp.dot(hot[:, half:], high[...], preferred_element_type=jnp.float32)
    late[...] = value.astype(jnp.bfloat16)
    for out, first in ((theirs, 0), (mine, SIDE)):
        for b in range(SIDE):
            block = first + b
            own_start = pl.multiple_of(starts[2 * block], ALIGN)
            pair[block, :WINDOW, :] = given[pl.ds(own_start, WINDOW), :]
            if is_late[block]:
                pair[block, WINDOW:, :] = late[...]
            else:
                hot_start = pl.multiple_of(starts[2 * block + 1], ALIGN)
                pair[block, WINDOW:, :] = given[pl.ds(total // 2 + hot_start, WINDOW), :]
            scale = scales[block * block_rows : (block + 1) * block_rows, :]
            value = jnp.dot(scale, pair[block], preferred_element_type=jnp.float32)
            out[b * block_rows : (b + 1) * block_rows, :] = value.astype(jnp.bfloat16)


def combine_call(part, parts, is_late, starts, scales, given, hot, low, high):
    width = given.shape[1] // parts
    steps = 2
    wide = width // steps
    rows = scales.shape[0]
    whole = pl.BlockSpec(memory_space=pltpu.VMEM)
    column = lambda value: pl.BlockSpec((value.shape[0], wide), lambda n: (0, part * steps + n))
    result = pl.BlockSpec((rows // 2, wide), lambda n: (0, n))
    return pl.pallas_call(
        functools.partial(combine_kernel, is_late),
        grid=(steps,),
        in_specs=[pl.BlockSpec(memory_space=pltpu.SMEM), whole, column(given), whole, column(low), column(high)],
        out_specs=[result, result],
        out_shape=[jax.ShapeDtypeStruct((rows // 2, width), jnp.bfloat16)] * 2,
        scratch_shapes=[
            pltpu.VMEM((hot.shape[0], wide), jnp.bfloat16),
            pltpu.VMEM((2 * SIDE, 2 * WINDOW, wide), jnp.bfloat16),
        ],
        compiler_params=pltpu.CompilerParams(vmem_limit_bytes=VMEM),
        cost_estimate=pl.CostEstimate(
            flops=2 * hot.size * width + 4 * rows * WINDOW * width,
            bytes_accessed=2 * width * (given.shape[0] + hot.shape[1] + rows),
            transcendentals=0,
        ),
    )(starts, scales, given, hot, low, high)


def add(*values):
    return sum(v.astype(jnp.float32) for v in values).astype(jnp.bfloat16)


def sent_back(hot):
    cut = hot.shape[1] // 2
    ahead, behind = shift_z(hot[2, :cut], 1), shift_z(hot[2, cut:], -1)
    forward = jnp.concatenate([hot[1, :cut] + ahead, hot[1, cut:]], axis=0)
    backward = jnp.concatenate([hot[3, :cut], hot[3, cut:] + behind], axis=0)
    return hot[0] + shift_z(forward, 1) + shift_z(backward, -1)


def sum_to_owners(theirs, mine, rows):
    width = mine.shape[1]
    total = add(mine, swap_cores(theirs)).reshape(SIDE, SIDE, rows, width)
    cut = SIDE // 2
    ahead = shift_ring(total[2, :cut], 1, 1)
    behind = shift_ring(total[2, cut:], 1, -1)
    forward = jnp.concatenate([add(total[1, :cut], ahead), total[1, cut:]], axis=0)
    backward = jnp.concatenate([total[3, :cut], add(total[3, cut:], behind)], axis=0)
    total = add(total[0], shift_ring(forward, 1, 1), shift_ring(backward, 1, -1))
    return add(total[0], shift_ring(total[1], 0, 1), shift_ring(total[3], 0, -1), shift_ring(total[2], 0, 2))


def local(tokens, route_ids, route_gates, w_gate, w_up, w_down, hot_source):
    n_ep = lax.axis_size("ep")
    grp, ep = lax.axis_index("grp"), lax.axis_index("ep")
    core, x, y = lax.rem(ep, 2), ep // (2 * SIDE), lax.rem(ep // 2, SIDE)
    rows = tokens[0]
    row_count, width = rows.shape
    picks = route_ids.shape[2]
    cap = row_count * picks // n_ep
    donor = hot_source[0]
    own_gate, own_up, own_down = w_gate[0, 0], w_up[0, 0], w_down[0, 0]


    info = jnp.concatenate([route_ids[0].astype(jnp.bfloat16), route_gates[0]], axis=1).T
    below, above = shift_z(rows, 1), shift_z(rows, -1)
    info = from_all(shift_z, info.reshape(-1, 128))
    cut = row_count // 2
    far = (shift_z(below[:cut], 1), shift_z(above[cut:], -1))
    unit_low = jnp.stack([rows, above])
    below_low, above_low = shift_ring(unit_low, 0, 1), shift_ring(unit_low, 0, -1)
    info = from_all(lambda value, step: shift_ring(value, 0, step), tie(info, unit_low))
    unit_high = tie(jnp.stack([jnp.concatenate(far, axis=0), below]), info)
    below_high, above_high = shift_ring(unit_high, 0, 1), shift_ring(unit_high, 0, -1)
    info = from_all(lambda value, step: shift_ring(value, 1, step), tie(info, below_low, above_low))
    far_low, far_high = shift_ring(below_low, 0, 1), shift_ring(above_high, 0, -1)
    info = jnp.stack([info, swap_cores(info)])
    info = info.reshape(2 * SIDE, SIDE, SIDE, 2 * picks, row_count)
    join = lambda first, second: jnp.concatenate([jnp.concatenate(first), jnp.concatenate(second)]).reshape(
        2, SIDE, row_count, width
    )
    low = tie(join((unit_low, unit_high), (above_low, above_high)), info)
    high = join((far_low, far_high), (below_low, below_high))

    away = lax.rem(jnp.where(core == 0, grp - donor, donor - grp) + SIDE, SIDE)
    half = own_down.shape[0] // 2
    own_halves = own_down[:half], own_down[half:]

    low_below, high_above = shift_ring(low, 1, 1), shift_ring(high, 1, -1)
    passed = [pass_on(tie(own_halves[0], low))]
    near = [low, high] + [swap_cores(low), swap_cores(high)]
    high_on, low_on = (tie(value, low_below, high_above, passed[0]) for value in (high, low))
    high_below, low_above = shift_ring(high_on, 1, 1), shift_ring(low_on, 1, -1)
    passed.append(pass_on(jnp.where(away == 0, own_halves[1], passed[0])))
    low_on, high_on = (tie(value, high_below, low_above, passed[1]) for value in (low_below, high_above))
    low_far, high_far = shift_ring(low_on, 1, 1), shift_ring(high_on, 1, -1)
    high_below, low_above = tie(high_below, passed[1]), tie(low_above, passed[1])
    passed.append(pass_on(passed[1]))
    beside = [low_above, high_above, low_below, high_below]
    beside = beside + [swap_cores(piece) for piece in beside]

    order = [(other, second) for seconds in STAGES for other in (0, 1) for second in seconds]
    info = jnp.stack([info[other * SIDE + second] for other, second in order])
    ids = info[:, :, :, :picks].astype(jnp.int32)
    gates = info[:, :, :, picks:].astype(jnp.float32)
    is_own, is_hot = ids[:, :, 0] == ep, ids == ep + n_ep
    block_rows = BLOCK * row_count
    member = jnp.concatenate([jnp.any(is_own, axis=2)[:, :, None], jnp.any(is_hot, axis=3)], axis=2)
    member = member.transpose(2, 0, 1, 3).reshape(SEGMENTS, len(order), block_rows).astype(jnp.int32)
    own_scale = jnp.sum(jnp.where(is_own, gates[:, :, 0], 0.0), axis=2).reshape(len(order), block_rows)
    hot_scale = jnp.sum(jnp.where(is_hot[:, :, 0], gates[:, :, 0], 0.0), axis=2).reshape(len(order), block_rows)
    donates = (donor == grp).astype(jnp.int32)

    own_hidden, hot_hidden, afters, befores = [], [], [], []
    begin, begin_slot = 0, 0
    for stage, seconds in enumerate(STAGES):
        if stage == 2:
            far = [tie(piece, own_hidden[-1], passed[2]) for piece in (low_far, high_far)]
            pieces = far + [swap_cores(piece) for piece in far]
        else:
            pieces = (near, beside)[stage]
        blocks = 2 * len(seconds)
        slots = blocks * BLOCK * cap
        meta, places, after, before = tables(member[:, begin : begin + blocks], donates)
        sources = [
            [(2 * block + first // 2, first % 2) for first in range(SIDE)] for block in range(blocks)
        ]
        own, hot = hidden_call(
            slots, 256 if blocks > 2 else 128, sources, meta, places, own_gate, own_up, pieces, after=own_hidden[-1:]
        )
        own_hidden.append(own)
        hot_hidden.append(hot)
        afters.append(after[:2] + begin_slot)
        befores.append(before[:2] + begin_slot)
        begin, begin_slot = begin + blocks, begin_slot + slots

    early = sent_back(jnp.concatenate(hot_hidden[:-1], axis=1))
    late = sent_back(hot_hidden[-1])
    passed.append(pass_on(passed[2]))
    copied_low, copied_high = own_halves
    for distance in range(1, SIDE):
        copied_low = jnp.where(away == distance, passed[distance - 1], copied_low)
        copied_high = jnp.where(away == distance, passed[distance], copied_high)
    given = down_call(own_hidden, early, own_down, copied_low, copied_high)

    after, before = jnp.concatenate(afters, axis=1), jnp.concatenate(befores, axis=1)
    wanted = [order.index((other, second)) for other in (1, 0) for second in range(SIDE)]
    take = lambda value: jnp.stack([value[:, index] for index in wanted], axis=1)
    is_late = [order[index][1] in STAGES[-1] for index in wanted]
    most = [begin_slot - WINDOW if late_block else begin_slot - slots - WINDOW for late_block in is_late]
    starts = jnp.minimum(take(before) // ALIGN * ALIGN, jnp.array(most, jnp.int32))
    slots = jnp.arange(WINDOW, dtype=jnp.int32)
    chosen = (take(after) - 1 - starts[:, :, None])[..., None] == slots
    scale = take(jnp.stack([own_scale, hot_scale]))[..., None]
    scales = jnp.where(chosen, scale, 0.0).astype(jnp.bfloat16)
    scales = jnp.concatenate([scales[0], scales[1]], axis=-1).reshape(len(order) * block_rows, 2 * WINDOW)
    starts = starts.T.reshape(-1)

    parts = 2
    results = []
    for part in range(parts):
        theirs, mine = combine_call(part, parts, is_late, starts, scales, given, late, copied_low, copied_high)
        results.append(sum_to_owners(theirs, mine, row_count))
    return jnp.concatenate(results, axis=1)[None]


def solution(mesh):
    placed = (
        P("grp", "ep", None),
        P("grp", "ep", None),
        P("grp", "ep", None),
        P("grp", "ep", None, None),
        P("grp", "ep", None, None),
        P("grp", "ep", None, None),
        P("ep"),
    )
    return jax.shard_map(
        local, mesh=mesh, in_specs=placed, out_specs=P("grp", "ep", None), check_vma=False
    )
```

```python
import functools

import jax
import jax.numpy as jnp
from jax import lax
from jax.experimental import pallas as pl
from jax.experimental.pallas import tpu as pltpu
from jax.sharding import PartitionSpec as P

SIDE = 4
SEGMENTS = 1 + SIDE
BLOCK = 4
WINDOW = 128
ALIGN = 16
PIECES = 2
STAGES = ((0, 1, 3), (2,))
VMEM = 60 * 1024 * 1024


def ep_of(x, y, core):
    return (x * SIDE + y) * 2 + core


def moved(index, ring, step):
    x, y, core = index // (2 * SIDE), index // 2 % SIDE, index % 2
    if (ring == 0) == (core == 0):
        return ep_of(x, (y + step) % SIDE, core)
    return ep_of((x + step) % SIDE, y, core)


def shift_z(value, step):
    return lax.ppermute(value, "grp", [(i, (i + step) % SIDE) for i in range(SIDE)])


def shift_ring(value, ring, step):
    count = 2 * SIDE * SIDE
    return lax.ppermute(value, "ep", [(i, moved(i, ring, step)) for i in range(count)])


def swap_cores(value):
    count = 2 * SIDE * SIDE
    return lax.ppermute(value, "ep", [(i, i ^ 1) for i in range(count)])


def pass_on(value):
    count = 2 * SIDE * SIDE
    pairs = [(g * count + i, (g + 1 - 2 * (i % 2)) % SIDE * count + i) for g in range(SIDE) for i in range(count)]
    return lax.ppermute(value, ("grp", "ep"), pairs)


def from_all(shift, value):
    return jnp.stack([value, shift(value, -1), shift(value, 2), shift(value, 1)])


def tie(value, *others):
    anywhere = pl.BlockSpec(memory_space=pl.ANY)
    return pl.pallas_call(
        lambda *refs: None,
        in_specs=[anywhere] * (1 + len(others)),
        out_specs=anywhere,
        out_shape=jax.ShapeDtypeStruct(value.shape, value.dtype),
        input_output_aliases={0: 0},
    )(value, *others)


def choose_kernel(steps, which, *refs):
    own, passed, out, sems = refs[0], refs[1 : 1 + steps], refs[1 + steps], refs[2 + steps]
    pieces = sems.shape[0]
    size = out.shape[0] // pieces
    for away in range(SIDE):

        @pl.when(which[0] == away)
        def _(away=away):
            copies = []
            for piece in range(pieces):
                span = pl.ds(piece * size, size)
                source = passed[piece + away - 1] if away else own.at[span]
                copies.append(pltpu.make_async_copy(source, out.at[span], sems.at[piece]))
            for copy in copies:
                copy.start()
            for copy in copies:
                copy.wait()


def choose_call(away, own, passed):
    anywhere = pl.BlockSpec(memory_space=pl.ANY)
    return pl.pallas_call(
        functools.partial(choose_kernel, len(passed)),
        in_specs=[pl.BlockSpec(memory_space=pltpu.SMEM)] + [anywhere] * (1 + len(passed)),
        out_specs=anywhere,
        out_shape=jax.ShapeDtypeStruct(own.shape, own.dtype),
        scratch_shapes=[pltpu.SemaphoreType.DMA((PIECES,))],
    )(away.reshape(1), own, *passed)


def hidden_kernel(capacity, tile, sources, meta, places, gate_hbm, up_hbm, *rest):
    blocks = len(sources)
    count = max(piece for block in sources for piece, _ in block) + 1
    pieces = rest[:count]
    own_out, hot_out, gate, up, gathered, compact, packed, weight_sems, row_sems = rest[-9:]
    rows = pieces[0].shape[2]
    width, hidden = gate.shape
    block_rows = BLOCK * rows
    donates, total = meta[0] == 1, meta[1]
    offsets, counts, begins = 2, 2 + SEGMENTS, 2 + 2 * SEGMENTS

    def load(block, distance):
        for unit, (piece, place) in enumerate(sources[block]):
            pltpu.make_async_copy(
                pieces[piece].at[place, distance],
                gathered.at[block, pl.ds(unit * rows, rows)],
                row_sems.at[block],
            ).start()

    def arrive(block):
        pltpu.make_async_copy(gathered.at[block], gathered.at[block], row_sems.at[block]).wait()

    def pick(segment, block):
        start = pl.multiple_of(meta[begins + segment * blocks + block], ALIGN)
        place = places[pl.ds(segment * blocks + block, 1), :] - start
        slots = lax.broadcasted_iota(jnp.int32, (WINDOW, block_rows), 0)
        choose = jnp.where(slots == place, 1.0, 0.0).astype(jnp.bfloat16)

        found = jnp.dot(choose, gathered[block], preferred_element_type=jnp.float32).astype(jnp.bfloat16)
        compact[pl.ds(start, ALIGN), :] = compact[pl.ds(start, ALIGN), :] + found[:ALIGN]
        compact[pl.ds(start + ALIGN, WINDOW - ALIGN), :] = found[ALIGN:]

    weights = (
        pltpu.make_async_copy(gate_hbm, gate, weight_sems.at[0]),
        pltpu.make_async_copy(up_hbm, up, weight_sems.at[1]),
    )
    for block in range(blocks):
        load(block, 0)
    for copy in weights:
        copy.start()
    compact[:ALIGN, :] = jnp.zeros((ALIGN, width), jnp.bfloat16)
    for block in range(blocks):
        arrive(block)
        pick(0, block)

    @pl.when(donates)
    def _():
        def group(distance, carry):
            for block in range(blocks):
                pl.when(distance > 0)(functools.partial(arrive, block))
                pick(1 + distance, block)
                pl.when(distance < SIDE - 1)(functools.partial(load, block, distance + 1))
            return carry
        lax.fori_loop(0, SIDE, group, 0)

    for copy in weights:
        copy.wait()

    def serve(t, carry):
        span = pl.ds(pl.multiple_of(t * tile, tile), tile)
        gate_part = jnp.dot(compact[span, :], gate[...], preferred_element_type=jnp.float32)
        up_part = jnp.dot(compact[span, :], up[...], preferred_element_type=jnp.float32)
        packed[span, :] = (jax.nn.silu(gate_part) * up_part).astype(jnp.bfloat16)
        return carry

    lax.fori_loop(0, lax.div(total + tile - 1, tile), serve, 0)

    def unpack(segment, store):
        for t in range(0, capacity, WINDOW):
            begin = pl.multiple_of(meta[offsets + segment] + t, ALIGN)
            live = lax.broadcasted_iota(jnp.int32, (WINDOW, hidden), 0) < meta[counts + segment] - t
            value = packed[pl.ds(begin, WINDOW), :]
            store(pl.ds(t, WINDOW), jnp.where(live, value, jnp.zeros_like(value)))

    def own_store(span, value):
        own_out[span, :] = value

    unpack(0, own_store)
    for distance in range(SIDE):

        def hot_store(span, value, distance=distance):
            hot_out[distance, span, :] = value

        unpack(1 + distance, hot_store)


def hidden_call(capacity, tile, sources, meta, places, gate, up, pieces, after=()):
    rows = pieces[0].shape[2]
    width, hidden = gate.shape
    blocks = len(sources)
    block_rows = BLOCK * rows
    most = SEGMENTS * capacity + tile
    anywhere = pl.BlockSpec(memory_space=pl.ANY)
    return pl.pallas_call(
        functools.partial(hidden_kernel, capacity, tile, sources),
        in_specs=[pl.BlockSpec(memory_space=pltpu.SMEM), pl.BlockSpec(memory_space=pltpu.VMEM)]
        + [anywhere] * (2 + len(pieces) + len(after)),
        out_specs=[pl.BlockSpec(memory_space=pltpu.VMEM)] * 2,
        out_shape=[
            jax.ShapeDtypeStruct((capacity, hidden), jnp.bfloat16),
            jax.ShapeDtypeStruct((SIDE, capacity, hidden), jnp.bfloat16),
        ],
        scratch_shapes=[
            pltpu.VMEM((width, hidden), jnp.bfloat16),
            pltpu.VMEM((width, hidden), jnp.bfloat16),
            pltpu.VMEM((blocks, block_rows, width), jnp.bfloat16),
            pltpu.VMEM((most, width), jnp.bfloat16),
            pltpu.VMEM((most, hidden), jnp.bfloat16),
            pltpu.SemaphoreType.DMA((2,)),
            pltpu.SemaphoreType.DMA((blocks,)),
        ],
        compiler_params=pltpu.CompilerParams(vmem_limit_bytes=VMEM),
        cost_estimate=pl.CostEstimate(
            flops=SEGMENTS * capacity * width * hidden * 2,
            bytes_accessed=2 * width * hidden * 2 + 4 * blocks * block_rows * width * 2,
            transcendentals=SEGMENTS * capacity * hidden,
        ),
    )(meta, places, gate, up, *pieces, *after)

def tables(member, donates):
    blocks, block_rows = member.shape[1:]
    after = jnp.cumsum(member.reshape(SEGMENTS, -1), axis=1).reshape(member.shape)
    counts = after[:, -1, -1]
    before = jnp.concatenate([jnp.zeros((SEGMENTS, 1), jnp.int32), after[:, :-1, -1]], axis=1)
    serves = jnp.where(jnp.arange(SEGMENTS) == 0, 1, donates)
    room = (counts + ALIGN - 1) // ALIGN * ALIGN * serves
    offsets = jnp.cumsum(room) - room
    begins = offsets[:, None] + before // ALIGN * ALIGN
    places = jnp.where(member == 1, offsets[:, None, None] + after - 1, -1).reshape(SEGMENTS * blocks, block_rows)
    meta = jnp.concatenate([jnp.stack([donates, jnp.sum(room)]), offsets, counts * serves, begins.reshape(-1)])
    return meta.astype(jnp.int32), places, after, before


def down_kernel(stages, *rest):
    hot, down, copied, out = rest[stages:]
    begin = 0
    for ref, weight in [(ref, down) for ref in rest[:stages]] + [(hot, copied)]:
        value = jnp.dot(ref[...], weight[...], preferred_element_type=jnp.float32)
        out[begin : begin + ref.shape[0], :] = value.astype(jnp.bfloat16)
        begin += ref.shape[0]


def down_call(own, hot, down, copied):
    hidden, width = down.shape
    wide = 512
    slots = sum(value.shape[0] for value in own) + hot.shape[0]
    whole = pl.BlockSpec(memory_space=pltpu.VMEM)
    column = lambda value: pl.BlockSpec((value.shape[0], wide), lambda n: (0, n))
    return pl.pallas_call(
        functools.partial(down_kernel, len(own)),
        grid=(width // wide,),
        in_specs=[whole] * (1 + len(own)) + [column(down), column(copied)],
        out_specs=pl.BlockSpec((slots, wide), lambda n: (0, n)),
        out_shape=jax.ShapeDtypeStruct((slots, width), jnp.bfloat16),
        compiler_params=pltpu.CompilerParams(vmem_limit_bytes=VMEM),
        cost_estimate=pl.CostEstimate(
            flops=2 * slots * hidden * width, bytes_accessed=2 * width * (2 * hidden + slots), transcendentals=0
        ),
    )(*own, hot, down, copied)


def combine_kernel(is_late, starts, scales, given, hot, copied, theirs, mine, late, pair):
    block_rows = mine.shape[0] // SIDE
    total = given.shape[0] + late.shape[0]
    late[...] = jnp.dot(hot[...], copied[...], preferred_element_type=jnp.float32).astype(jnp.bfloat16)
    for out, first in ((theirs, 0), (mine, SIDE)):
        for b in range(SIDE):
            block = first + b
            own_start = pl.multiple_of(starts[2 * block], ALIGN)
            pair[block, :WINDOW, :] = given[pl.ds(own_start, WINDOW), :]
            if is_late[block]:
                pair[block, WINDOW:, :] = late[...]
            else:
                hot_start = pl.multiple_of(starts[2 * block + 1], ALIGN)
                pair[block, WINDOW:, :] = given[pl.ds(total // 2 + hot_start, WINDOW), :]
            scale = scales[block * block_rows : (block + 1) * block_rows, :]
            value = jnp.dot(scale, pair[block], preferred_element_type=jnp.float32)
            out[b * block_rows : (b + 1) * block_rows, :] = value.astype(jnp.bfloat16)


def combine_call(part, parts, is_late, starts, scales, given, hot, copied):
    width = given.shape[1] // parts
    steps = 2
    wide = width // steps
    rows = scales.shape[0]
    whole = pl.BlockSpec(memory_space=pltpu.VMEM)
    column = lambda value: pl.BlockSpec((value.shape[0], wide), lambda n: (0, part * steps + n))
    result = pl.BlockSpec((rows // 2, wide), lambda n: (0, n))
    return pl.pallas_call(
        functools.partial(combine_kernel, is_late),
        grid=(steps,),
        in_specs=[pl.BlockSpec(memory_space=pltpu.SMEM), whole, column(given), whole, column(copied)],
        out_specs=[result, result],
        out_shape=[jax.ShapeDtypeStruct((rows // 2, width), jnp.bfloat16)] * 2,
        scratch_shapes=[
            pltpu.VMEM((hot.shape[0], wide), jnp.bfloat16),
            pltpu.VMEM((2 * SIDE, 2 * WINDOW, wide), jnp.bfloat16),
        ],
        compiler_params=pltpu.CompilerParams(vmem_limit_bytes=VMEM),
        cost_estimate=pl.CostEstimate(
            flops=2 * hot.size * width + 4 * rows * WINDOW * width,
            bytes_accessed=2 * width * (given.shape[0] + hot.shape[1] + rows),
            transcendentals=0,
        ),
    )(starts, scales, given, hot, copied)


def add(*values):
    return sum(v.astype(jnp.float32) for v in values).astype(jnp.bfloat16)


def sent_back(hot):
    cut = hot.shape[1] // 2
    ahead, behind = shift_z(hot[2, :cut], 1), shift_z(hot[2, cut:], -1)
    forward = jnp.concatenate([hot[1, :cut] + ahead, hot[1, cut:]], axis=0)
    backward = jnp.concatenate([hot[3, :cut], hot[3, cut:] + behind], axis=0)
    return hot[0] + shift_z(forward, 1) + shift_z(backward, -1)


def sum_to_owners(theirs, mine, rows):
    width = mine.shape[1]
    total = add(mine, swap_cores(theirs)).reshape(SIDE, SIDE, rows, width)
    cut = SIDE // 2
    ahead = shift_ring(total[2, :cut], 1, 1)
    behind = shift_ring(total[2, cut:], 1, -1)
    forward = jnp.concatenate([add(total[1, :cut], ahead), total[1, cut:]], axis=0)
    backward = jnp.concatenate([total[3, :cut], add(total[3, cut:], behind)], axis=0)
    total = add(total[0], shift_ring(forward, 1, 1), shift_ring(backward, 1, -1))
    return add(total[0], shift_ring(total[1], 0, 1), shift_ring(total[3], 0, -1), shift_ring(total[2], 0, 2))


def local(tokens, route_ids, route_gates, w_gate, w_up, w_down, hot_source):
    n_ep = lax.axis_size("ep")
    grp, ep = lax.axis_index("grp"), lax.axis_index("ep")
    core, x, y = lax.rem(ep, 2), ep // (2 * SIDE), lax.rem(ep // 2, SIDE)
    rows = tokens[0]
    row_count, width = rows.shape
    picks = route_ids.shape[2]
    cap = row_count * picks // n_ep
    donor = hot_source[0]
    own_gate, own_up, own_down = w_gate[0, 0], w_up[0, 0], w_down[0, 0]


    passed = []
    away = lax.rem(jnp.where(core == 0, grp - donor, donor - grp) + SIDE, SIDE)
    size = own_down.shape[0] // PIECES

    def passing(step, *after):
        if step < PIECES:
            piece = own_down[step * size : (step + 1) * size]
            piece = tie(piece, *after) if after else piece
            piece = jnp.where(away == 0, piece, passed[-1]) if step else piece
        else:
            piece = passed[-1]
        passed.append(pass_on(piece))

    info = jnp.concatenate([route_ids[0].astype(jnp.bfloat16), route_gates[0]], axis=1).T
    below, above = shift_z(rows, 1), shift_z(rows, -1)
    info = from_all(shift_z, info.reshape(-1, 128))
    cut = row_count // 2
    far = (shift_z(below[:cut], 1), shift_z(above[cut:], -1))
    unit_low = jnp.stack([rows, above])
    below_low, above_low = shift_ring(unit_low, 0, 1), shift_ring(unit_low, 0, -1)
    info = from_all(lambda value, step: shift_ring(value, 0, step), info)
    info = from_all(lambda value, step: shift_ring(value, 1, step), info)
    info = jnp.stack([info, swap_cores(info)])
    unit_high = tie(jnp.stack([jnp.concatenate(far, axis=0), below]), info)
    passing(0, unit_high)
    below_high, above_high = shift_ring(unit_high, 0, 1), shift_ring(unit_high, 0, -1)
    far_low, far_high = shift_ring(below_low, 0, 1), shift_ring(above_high, 0, -1)
    info = info.reshape(2 * SIDE, SIDE, SIDE, 2 * picks, row_count)
    join = lambda first, second: jnp.concatenate([jnp.concatenate(first), jnp.concatenate(second)]).reshape(
        2, SIDE, row_count, width
    )
    low = tie(join((unit_low, unit_high), (above_low, above_high)), passed[0])
    high = join((far_low, far_high), (below_low, below_high))

    low_below, high_above = shift_ring(low, 1, 1), shift_ring(high, 1, -1)
    near = [low, high]
    near_other = [swap_cores(piece) for piece in near]
    passing(1)
    high_on, low_on = (tie(value, low_below, high_above, passed[1], *near_other) for value in (high, low))
    high_below, low_above = shift_ring(high_on, 1, 1), shift_ring(low_on, 1, -1)
    first = [low_below, high_above]
    first_other = [swap_cores(piece) for piece in first]
    passing(2)
    last_low, last_high = (tie(value, high_below, low_above, passed[2], *first_other) for value in first)
    low_far, high_far = shift_ring(last_low, 1, 1), shift_ring(last_high, 1, -1)
    second = [tie(high_below, passed[2]), tie(low_above, passed[2])]
    second_other = [swap_cores(piece) for piece in second]
    passing(3)
    early = near + [second[1], first[1], first[0], second[0]]
    early = early + near_other + [second_other[1], first_other[1], first_other[0], second_other[0]]

    order = [(other, second) for seconds in STAGES for other in (0, 1) for second in seconds]
    info = jnp.stack([info[other * SIDE + second] for other, second in order])
    ids = info[:, :, :, :picks].astype(jnp.int32)
    gates = info[:, :, :, picks:].astype(jnp.float32)
    is_own, is_hot = ids[:, :, 0] == ep, ids == ep + n_ep
    block_rows = BLOCK * row_count
    member = jnp.concatenate([jnp.any(is_own, axis=2)[:, :, None], jnp.any(is_hot, axis=3)], axis=2)
    member = member.transpose(2, 0, 1, 3).reshape(SEGMENTS, len(order), block_rows).astype(jnp.int32)
    own_scale = jnp.sum(jnp.where(is_own, gates[:, :, 0], 0.0), axis=2).reshape(len(order), block_rows)
    hot_scale = jnp.sum(jnp.where(is_hot[:, :, 0], gates[:, :, 0], 0.0), axis=2).reshape(len(order), block_rows)
    donates = (donor == grp).astype(jnp.int32)

    own_hidden, hot_hidden, afters, befores = [], [], [], []
    begin, begin_slot = 0, 0
    copied = choose_call(away, own_down, passed)
    for stage, seconds in enumerate(STAGES):
        if stage:
            far = [tie(piece, own_hidden[-1], passed[3]) for piece in (low_far, high_far)]
            pieces = far + [swap_cores(piece) for piece in far]
        else:
            pieces = early
        blocks = 2 * len(seconds)
        slots = blocks * BLOCK * cap
        meta, places, after, before = tables(member[:, begin : begin + blocks], donates)
        sources = [
            [(2 * block + first // 2, first % 2) for first in range(SIDE)] for block in range(blocks)
        ]
        own, hot = hidden_call(
            slots, 256 if blocks > 2 else 128, sources, meta, places, own_gate, own_up, pieces, after=own_hidden[-1:] + [copied] * stage
        )
        own_hidden.append(own)
        hot_hidden.append(hot)
        afters.append(after[:2] + begin_slot)
        befores.append(before[:2] + begin_slot)
        begin, begin_slot = begin + blocks, begin_slot + slots

    early, late = (sent_back(hot) for hot in hot_hidden)
    given = down_call(own_hidden, early, own_down, copied)

    after, before = jnp.concatenate(afters, axis=1), jnp.concatenate(befores, axis=1)
    wanted = [order.index((other, second)) for other in (1, 0) for second in range(SIDE)]
    take = lambda value: jnp.stack([value[:, index] for index in wanted], axis=1)
    is_late = [order[index][1] in STAGES[-1] for index in wanted]
    most = [begin_slot - WINDOW if late_block else begin_slot - slots - WINDOW for late_block in is_late]
    starts = jnp.minimum(take(before) // ALIGN * ALIGN, jnp.array(most, jnp.int32))
    slots = jnp.arange(WINDOW, dtype=jnp.int32)
    chosen = (take(after) - 1 - starts[:, :, None])[..., None] == slots
    scale = take(jnp.stack([own_scale, hot_scale]))[..., None]
    scales = jnp.where(chosen, scale, 0.0).astype(jnp.bfloat16)
    scales = jnp.concatenate([scales[0], scales[1]], axis=-1).reshape(len(order) * block_rows, 2 * WINDOW)
    starts = starts.T.reshape(-1)

    parts = 2
    results = []
    for part in range(parts):
        theirs, mine = combine_call(part, parts, is_late, starts, scales, given, late, copied)
        results.append(sum_to_owners(theirs, mine, row_count))
    return jnp.concatenate(results, axis=1)[None]


def solution(mesh):
    placed = (
        P("grp", "ep", None),
        P("grp", "ep", None),
        P("grp", "ep", None),
        P("grp", "ep", None, None),
        P("grp", "ep", None, None),
        P("grp", "ep", None, None),
        P("ep"),
    )
    return jax.shard_map(
        local, mesh=mesh, in_specs=placed, out_specs=P("grp", "ep", None), check_vma=False
    )
```

```python
import functools

import jax
import jax.numpy as jnp
from jax import lax
from jax.experimental import pallas as pl
from jax.experimental.pallas import tpu as pltpu
from jax.sharding import PartitionSpec as P

SIDE = 4
SEGMENTS = 1 + SIDE
BLOCK = 4
WINDOW = 128
ALIGN = 16
PIECES = 2
STAGES = ((0, 1, 3), (2,))
VMEM = 60 * 1024 * 1024


def ep_of(x, y, core):
    return (x * SIDE + y) * 2 + core


def moved(index, ring, step):
    x, y, core = index // (2 * SIDE), index // 2 % SIDE, index % 2
    if (ring == 0) == (core == 0):
        return ep_of(x, (y + step) % SIDE, core)
    return ep_of((x + step) % SIDE, y, core)


def shift_z(value, step):
    return lax.ppermute(value, "grp", [(i, (i + step) % SIDE) for i in range(SIDE)])


def shift_ring(value, ring, step):
    count = 2 * SIDE * SIDE
    return lax.ppermute(value, "ep", [(i, moved(i, ring, step)) for i in range(count)])


def swap_cores(value):
    count = 2 * SIDE * SIDE
    return lax.ppermute(value, "ep", [(i, i ^ 1) for i in range(count)])


def pass_on(value):
    count = 2 * SIDE * SIDE
    pairs = [(g * count + i, (g + 1 - 2 * (i % 2)) % SIDE * count + i) for g in range(SIDE) for i in range(count)]
    return lax.ppermute(value, ("grp", "ep"), pairs)


def from_all(shift, value):
    return jnp.stack([value, shift(value, -1), shift(value, 2), shift(value, 1)])


def tie(value, *others):
    anywhere = pl.BlockSpec(memory_space=pl.ANY)
    return pl.pallas_call(
        lambda *refs: None,
        in_specs=[anywhere] * (1 + len(others)),
        out_specs=anywhere,
        out_shape=jax.ShapeDtypeStruct(value.shape, value.dtype),
        input_output_aliases={0: 0},
    )(value, *others)


def choose_kernel(steps, which, *refs):
    own, passed, out, sems = refs[0], refs[1 : 1 + steps], refs[1 + steps], refs[2 + steps]
    size = out.shape[0] // PIECES
    for away in range(SIDE):

        @pl.when(which[0] == away)
        def _(away=away):
            copies = []
            for piece in range(PIECES):
                span = pl.ds(piece * size, size)
                source = passed[piece + away - 1] if away else own.at[span]
                copies.append(pltpu.make_async_copy(source, out.at[span], sems.at[piece]))
            for copy in copies:
                copy.start()
            for copy in copies:
                copy.wait()


def choose_call(away, own, passed):
    anywhere = pl.BlockSpec(memory_space=pl.ANY)
    return pl.pallas_call(
        functools.partial(choose_kernel, len(passed)),
        in_specs=[pl.BlockSpec(memory_space=pltpu.SMEM)] + [anywhere] * (1 + len(passed)),
        out_specs=pl.BlockSpec(memory_space=pltpu.VMEM),
        out_shape=jax.ShapeDtypeStruct(own.shape, own.dtype),
        scratch_shapes=[pltpu.SemaphoreType.DMA((PIECES,))],
        compiler_params=pltpu.CompilerParams(vmem_limit_bytes=VMEM),
    )(away.reshape(1), own, *passed)


def hidden_kernel(capacity, tile, sources, meta, places, gate_hbm, up_hbm, *rest):
    blocks = len(sources)
    count = max(piece for block in sources for piece, _ in block) + 1
    pieces = rest[:count]
    own_out, hot_out, gate, up, gathered, compact, packed, weight_sems, row_sems = rest[-9:]
    rows = pieces[0].shape[2]
    width, hidden = gate.shape
    block_rows = BLOCK * rows
    donates, total = meta[0] == 1, meta[1]
    offsets, counts, begins = 2, 2 + SEGMENTS, 2 + 2 * SEGMENTS

    def load(block, distance):
        for unit, (piece, place) in enumerate(sources[block]):
            pltpu.make_async_copy(
                pieces[piece].at[place, distance],
                gathered.at[block, pl.ds(unit * rows, rows)],
                row_sems.at[block],
            ).start()

    def arrive(block):
        pltpu.make_async_copy(gathered.at[block], gathered.at[block], row_sems.at[block]).wait()

    def pick(segment, block):
        start = pl.multiple_of(meta[begins + segment * blocks + block], ALIGN)
        place = places[pl.ds(segment * blocks + block, 1), :] - start
        slots = lax.broadcasted_iota(jnp.int32, (WINDOW, block_rows), 0)
        choose = jnp.where(slots == place, 1.0, 0.0).astype(jnp.bfloat16)

        found = jnp.dot(choose, gathered[block], preferred_element_type=jnp.float32).astype(jnp.bfloat16)
        compact[pl.ds(start, ALIGN), :] = compact[pl.ds(start, ALIGN), :] + found[:ALIGN]
        compact[pl.ds(start + ALIGN, WINDOW - ALIGN), :] = found[ALIGN:]

    weights = (
        pltpu.make_async_copy(gate_hbm, gate, weight_sems.at[0]),
        pltpu.make_async_copy(up_hbm, up, weight_sems.at[1]),
    )
    for block in range(blocks):
        load(block, 0)
    for copy in weights:
        copy.start()
    compact[:ALIGN, :] = jnp.zeros((ALIGN, width), jnp.bfloat16)
    for block in range(blocks):
        arrive(block)
        pick(0, block)

    @pl.when(donates)
    def _():
        def group(distance, carry):
            for block in range(blocks):
                pl.when(distance > 0)(functools.partial(arrive, block))
                pick(1 + distance, block)
                pl.when(distance < SIDE - 1)(functools.partial(load, block, distance + 1))
            return carry
        lax.fori_loop(0, SIDE, group, 0)

    for copy in weights:
        copy.wait()

    def serve(t, carry):
        span = pl.ds(pl.multiple_of(t * tile, tile), tile)
        gate_part = jnp.dot(compact[span, :], gate[...], preferred_element_type=jnp.float32)
        up_part = jnp.dot(compact[span, :], up[...], preferred_element_type=jnp.float32)
        packed[span, :] = (jax.nn.silu(gate_part) * up_part).astype(jnp.bfloat16)
        return carry

    lax.fori_loop(0, lax.div(total + tile - 1, tile), serve, 0)

    def unpack(segment, store):
        for t in range(0, capacity, WINDOW):
            begin = pl.multiple_of(meta[offsets + segment] + t, ALIGN)
            live = lax.broadcasted_iota(jnp.int32, (WINDOW, hidden), 0) < meta[counts + segment] - t
            value = packed[pl.ds(begin, WINDOW), :]
            store(pl.ds(t, WINDOW), jnp.where(live, value, jnp.zeros_like(value)))

    def own_store(span, value):
        own_out[span, :] = value

    unpack(0, own_store)
    for distance in range(SIDE):

        def hot_store(span, value, distance=distance):
            hot_out[distance, span, :] = value

        unpack(1 + distance, hot_store)


def hidden_call(capacity, tile, sources, meta, places, gate, up, pieces, after=()):
    rows = pieces[0].shape[2]
    width, hidden = gate.shape
    blocks = len(sources)
    block_rows = BLOCK * rows
    most = SEGMENTS * capacity + tile
    anywhere = pl.BlockSpec(memory_space=pl.ANY)
    return pl.pallas_call(
        functools.partial(hidden_kernel, capacity, tile, sources),
        in_specs=[pl.BlockSpec(memory_space=pltpu.SMEM), pl.BlockSpec(memory_space=pltpu.VMEM)]
        + [anywhere] * (2 + len(pieces) + len(after)),
        out_specs=[pl.BlockSpec(memory_space=pltpu.VMEM)] * 2,
        out_shape=[
            jax.ShapeDtypeStruct((capacity, hidden), jnp.bfloat16),
            jax.ShapeDtypeStruct((SIDE, capacity, hidden), jnp.bfloat16),
        ],
        scratch_shapes=[
            pltpu.VMEM((width, hidden), jnp.bfloat16),
            pltpu.VMEM((width, hidden), jnp.bfloat16),
            pltpu.VMEM((blocks, block_rows, width), jnp.bfloat16),
            pltpu.VMEM((most, width), jnp.bfloat16),
            pltpu.VMEM((most, hidden), jnp.bfloat16),
            pltpu.SemaphoreType.DMA((2,)),
            pltpu.SemaphoreType.DMA((blocks,)),
        ],
        compiler_params=pltpu.CompilerParams(vmem_limit_bytes=VMEM),
        cost_estimate=pl.CostEstimate(
            flops=SEGMENTS * capacity * width * hidden * 2,
            bytes_accessed=2 * width * hidden * 2 + 4 * blocks * block_rows * width * 2,
            transcendentals=SEGMENTS * capacity * hidden,
        ),
    )(meta, places, gate, up, *pieces, *after)

def tables(member, donates):
    blocks, block_rows = member.shape[1:]
    after = jnp.cumsum(member.reshape(SEGMENTS, -1), axis=1).reshape(member.shape)
    counts = after[:, -1, -1]
    before = jnp.concatenate([jnp.zeros((SEGMENTS, 1), jnp.int32), after[:, :-1, -1]], axis=1)
    serves = jnp.where(jnp.arange(SEGMENTS) == 0, 1, donates)
    room = (counts + ALIGN - 1) // ALIGN * ALIGN * serves
    offsets = jnp.cumsum(room) - room
    begins = offsets[:, None] + before // ALIGN * ALIGN
    places = jnp.where(member == 1, offsets[:, None, None] + after - 1, -1).reshape(SEGMENTS * blocks, block_rows)
    meta = jnp.concatenate([jnp.stack([donates, jnp.sum(room)]), offsets, counts * serves, begins.reshape(-1)])
    return meta.astype(jnp.int32), places, after, before


def down_kernel(hidden, down, out):
    out[...] = jnp.dot(hidden[...], down[...], preferred_element_type=jnp.float32).astype(jnp.bfloat16)


def down_call(hidden, down):
    slots, width = hidden.shape[0], down.shape[1]
    wide = 512
    column = lambda rows: pl.BlockSpec((rows, wide), lambda n: (0, n))
    return pl.pallas_call(
        down_kernel,
        grid=(width // wide,),
        in_specs=[pl.BlockSpec(memory_space=pltpu.VMEM), column(down.shape[0])],
        out_specs=column(slots),
        out_shape=jax.ShapeDtypeStruct((slots, width), jnp.bfloat16),
        compiler_params=pltpu.CompilerParams(vmem_limit_bytes=VMEM),
        cost_estimate=pl.CostEstimate(
            flops=2 * hidden.size * width, bytes_accessed=2 * (down.size + slots * width), transcendentals=0
        ),
    )(hidden, down)


def combine_kernel(is_late, starts, scales, own_early, hot_early, own_late, hot_late, down, copied,
                   theirs, mine, late, pair):
    block_rows = mine.shape[0] // SIDE
    late[:WINDOW, :] = jnp.dot(own_late[...], down[...], preferred_element_type=jnp.float32).astype(jnp.bfloat16)
    late[WINDOW:, :] = jnp.dot(hot_late[...], copied[...], preferred_element_type=jnp.float32).astype(jnp.bfloat16)
    for out, first in ((theirs, 0), (mine, SIDE)):
        for b in range(SIDE):
            block = first + b
            scale = scales[block * block_rows : (block + 1) * block_rows, :]
            if is_late[block]:
                value = jnp.dot(scale, late[...], preferred_element_type=jnp.float32)
            else:
                for part, ref in enumerate((own_early, hot_early)):
                    start = pl.multiple_of(starts[2 * block + part], ALIGN)
                    pair[block, part * WINDOW : (part + 1) * WINDOW, :] = ref[pl.ds(start, WINDOW), :]
                value = jnp.dot(scale, pair[block], preferred_element_type=jnp.float32)
            out[b * block_rows : (b + 1) * block_rows, :] = value.astype(jnp.bfloat16)


def combine_call(part, parts, is_late, starts, scales, own_early, hot_early, own_late, hot_late, down, copied):
    width = down.shape[1] // parts
    steps = 2
    wide = width // steps
    rows = scales.shape[0]
    whole = pl.BlockSpec(memory_space=pltpu.VMEM)
    column = lambda value: pl.BlockSpec((value.shape[0], wide), lambda n: (0, part * steps + n))
    result = pl.BlockSpec((rows // 2, wide), lambda n: (0, n))
    return pl.pallas_call(
        functools.partial(combine_kernel, is_late),
        grid=(steps,),
        in_specs=[pl.BlockSpec(memory_space=pltpu.SMEM), whole, column(own_early), column(hot_early), whole, whole]
        + [column(down), column(copied)],
        out_specs=[result, result],
        out_shape=[jax.ShapeDtypeStruct((rows // 2, width), jnp.bfloat16)] * 2,
        scratch_shapes=[
            pltpu.VMEM((2 * WINDOW, wide), jnp.bfloat16),
            pltpu.VMEM((2 * SIDE, 2 * WINDOW, wide), jnp.bfloat16),
        ],
        compiler_params=pltpu.CompilerParams(vmem_limit_bytes=VMEM),
        cost_estimate=pl.CostEstimate(
            flops=4 * hot_late.size * width + 4 * rows * WINDOW * width,
            bytes_accessed=2 * width * (2 * own_early.shape[0] + 2 * hot_late.shape[1] + rows),
            transcendentals=0,
        ),
    )(starts, scales, own_early, hot_early, own_late, hot_late, down, copied)


def add(*values):
    return sum(v.astype(jnp.float32) for v in values).astype(jnp.bfloat16)


def sent_back(hot, *others):
    cut = hot.shape[1] // 2
    ahead, behind = shift_z(hot[2, :cut], 1), shift_z(hot[2, cut:], -1)
    forward = jnp.concatenate([hot[1, :cut] + ahead, hot[1, cut:]], axis=0)
    backward = jnp.concatenate([hot[3, :cut], hot[3, cut:] + behind], axis=0)
    return tie(hot[0], *others) + shift_z(forward, 1) + shift_z(backward, -1)


def sent_back_at_once(hot):
    return hot[0] + shift_z(hot[1], 1) + shift_z(hot[3], -1) + shift_z(hot[2], 2)


def sum_to_owners(theirs, mine, rows):
    width = mine.shape[1]
    total = add(mine, swap_cores(theirs)).reshape(SIDE, SIDE, rows, width)
    cut = SIDE // 2
    ahead = shift_ring(total[2, :cut], 1, 1)
    behind = shift_ring(total[2, cut:], 1, -1)
    forward = jnp.concatenate([add(total[1, :cut], ahead), total[1, cut:]], axis=0)
    backward = jnp.concatenate([total[3, :cut], add(total[3, cut:], behind)], axis=0)
    total = add(total[0], shift_ring(forward, 1, 1), shift_ring(backward, 1, -1))
    return add(total[0], shift_ring(total[1], 0, 1), shift_ring(total[3], 0, -1), shift_ring(total[2], 0, 2))


def local(tokens, route_ids, route_gates, w_gate, w_up, w_down, hot_source):
    n_ep = lax.axis_size("ep")
    grp, ep = lax.axis_index("grp"), lax.axis_index("ep")
    core, x, y = lax.rem(ep, 2), ep // (2 * SIDE), lax.rem(ep // 2, SIDE)
    rows = tokens[0]
    row_count, width = rows.shape
    picks = route_ids.shape[2]
    cap = row_count * picks // n_ep
    donor = hot_source[0]
    own_gate, own_up, own_down = w_gate[0, 0], w_up[0, 0], w_down[0, 0]


    passed = []
    away = lax.rem(jnp.where(core == 0, grp - donor, donor - grp) + SIDE, SIDE)
    size = own_down.shape[0] // PIECES

    def passing(step, *after):
        if step < PIECES:
            piece = own_down[step * size : (step + 1) * size]
            piece = tie(piece, *after) if after else piece
            piece = jnp.where(away == 0, piece, passed[-1]) if step else piece
        else:
            piece = passed[-1]
        passed.append(pass_on(piece))

    routes = jnp.concatenate([route_ids[0].astype(jnp.bfloat16), route_gates[0]], axis=1)
    rows = jnp.concatenate([rows, jnp.pad(routes, ((0, 0), (0, 128 - 2 * picks)))], axis=1)
    below, above = shift_z(rows, 1), shift_z(rows, -1)
    cut = row_count // 2
    far = (shift_z(below[:cut], 1), shift_z(above[cut:], -1))
    unit_low = jnp.stack([rows, above])
    passing(0, unit_low)
    below_low, above_low = shift_ring(unit_low, 0, 1), shift_ring(unit_low, 0, -1)
    unit_high = jnp.stack([jnp.concatenate(far, axis=0), below])
    below_high, above_high = shift_ring(unit_high, 0, 1), shift_ring(unit_high, 0, -1)
    far_low, far_high = shift_ring(below_low, 0, 1), shift_ring(above_high, 0, -1)

    def join(*parts):
        parts = [part[:, :, :width] for part in parts]
        return jnp.concatenate(parts).reshape(2, SIDE, row_count, width)

    near_parts = (unit_low, unit_high, above_low, above_high, far_low, far_high, below_low, below_high)
    low = tie(join(*near_parts[:4]), passed[0])
    high = join(*near_parts[4:])
    info = jnp.concatenate([part[:, :, width : width + 2 * picks] for part in near_parts])
    info = info.transpose(0, 2, 1).reshape(SIDE, SIDE, -1, 128)
    info = from_all(lambda value, step: shift_ring(value, 1, step), tie(info, low))

    low_below, high_above = shift_ring(low, 1, 1), shift_ring(high, 1, -1)
    near = [low, high]
    near_other = [swap_cores(piece) for piece in near]
    passing(1)
    high_on, low_on = (tie(value, low_below, high_above, passed[1], info, *near_other) for value in (high, low))
    high_below, low_above = shift_ring(high_on, 1, 1), shift_ring(low_on, 1, -1)
    info = jnp.stack([info, swap_cores(info)])
    info = info.reshape(2 * SIDE, SIDE, SIDE, 2 * picks, row_count)
    first = [low_below, high_above]
    first_other = [swap_cores(piece) for piece in first]
    passing(2)
    last_low, last_high = (tie(value, high_below, low_above, passed[2], info, *first_other) for value in first)
    low_far, high_far = shift_ring(last_low, 1, 1), shift_ring(last_high, 1, -1)
    second = [tie(high_below, passed[2]), tie(low_above, passed[2])]
    second_other = [swap_cores(piece) for piece in second]
    passing(3)
    early = near + [second[1], first[1], first[0], second[0]]
    early = early + near_other + [second_other[1], first_other[1], first_other[0], second_other[0]]

    order = [(other, second) for seconds in STAGES for other in (0, 1) for second in seconds]
    info = jnp.stack([info[other * SIDE + second] for other, second in order])
    ids = info[:, :, :, :picks].astype(jnp.int32)
    gates = info[:, :, :, picks:].astype(jnp.float32)
    is_own, is_hot = ids[:, :, 0] == ep, ids == ep + n_ep
    block_rows = BLOCK * row_count
    member = jnp.concatenate([jnp.any(is_own, axis=2)[:, :, None], jnp.any(is_hot, axis=3)], axis=2)
    member = member.transpose(2, 0, 1, 3).reshape(SEGMENTS, len(order), block_rows).astype(jnp.int32)
    own_scale = jnp.sum(jnp.where(is_own, gates[:, :, 0], 0.0), axis=2).reshape(len(order), block_rows)
    hot_scale = jnp.sum(jnp.where(is_hot[:, :, 0], gates[:, :, 0], 0.0), axis=2).reshape(len(order), block_rows)
    donates = (donor == grp).astype(jnp.int32)

    own_hidden, hot_hidden, afters, befores = [], [], [], []
    begin, begin_slot = 0, 0
    copied = choose_call(away, own_down, passed)
    for stage, seconds in enumerate(STAGES):
        if stage:
            far = [tie(piece, own_hidden[-1], passed[3]) for piece in (low_far, high_far)]
            pieces = far + [swap_cores(piece) for piece in far]
            own_early = down_call(tie(own_hidden[0], *far), own_down)
        else:
            pieces = early
        blocks = 2 * len(seconds)
        slots = blocks * BLOCK * cap
        meta, places, after, before = tables(member[:, begin : begin + blocks], donates)
        sources = [
            [(2 * block + first // 2, first % 2) for first in range(SIDE)] for block in range(blocks)
        ]
        own, hot = hidden_call(
            slots, 256 if blocks > 2 else 128, sources, meta, places, own_gate, own_up, pieces, after=[copied, own_early] if stage else ()
        )
        own_hidden.append(own)
        hot_hidden.append(hot)
        afters.append(after[:2] + begin_slot)
        befores.append(before[:2] + begin_slot)
        begin, begin_slot = begin + blocks, begin_slot + slots

    hot_early = down_call(sent_back(hot_hidden[0], own_hidden[1]), copied)
    hot_late = sent_back_at_once(hot_hidden[1])

    after, before = jnp.concatenate(afters, axis=1), jnp.concatenate(befores, axis=1)
    wanted = [order.index((other, second)) for other in (1, 0) for second in range(SIDE)]
    take = lambda value: jnp.stack([value[:, index] for index in wanted], axis=1)
    is_late = [order[index][1] in STAGES[-1] for index in wanted]
    most = [begin_slot - WINDOW if late_block else begin_slot - slots - WINDOW for late_block in is_late]
    starts = jnp.minimum(take(before) // ALIGN * ALIGN, jnp.array(most, jnp.int32))
    slots = jnp.arange(WINDOW, dtype=jnp.int32)
    chosen = (take(after) - 1 - starts[:, :, None])[..., None] == slots
    scale = take(jnp.stack([own_scale, hot_scale]))[..., None]
    scales = jnp.where(chosen, scale, 0.0).astype(jnp.bfloat16)
    scales = jnp.concatenate([scales[0], scales[1]], axis=-1).reshape(len(order) * block_rows, 2 * WINDOW)
    starts = starts.T.reshape(-1)

    parts = 2
    results = []
    for part in range(parts):
        theirs, mine = combine_call(
            part, parts, is_late, starts, scales, own_early, hot_early, own_hidden[1], hot_late, own_down, copied
        )
        results.append(sum_to_owners(theirs, mine, row_count))
    return jnp.concatenate(results, axis=1)[None]


def solution(mesh):
    placed = (
        P("grp", "ep", None),
        P("grp", "ep", None),
        P("grp", "ep", None),
        P("grp", "ep", None, None),
        P("grp", "ep", None, None),
        P("grp", "ep", None, None),
        P("ep"),
    )
    return jax.shard_map(
        local, mesh=mesh, in_specs=placed, out_specs=P("grp", "ep", None), check_vma=False
    )
```

```python
import functools

import jax
import jax.numpy as jnp
from jax import lax
from jax.experimental import pallas as pl
from jax.experimental.pallas import tpu as pltpu
from jax.sharding import PartitionSpec as P

SIDE = 4
SEGMENTS = 1 + SIDE
BLOCK = 4
WINDOW = 128
ALIGN = 16
PIECES = 2
STAGES = ((0, 1, 3), (2,))
VMEM = 60 * 1024 * 1024


def ep_of(x, y, core):
    return (x * SIDE + y) * 2 + core


def moved(index, ring, step):
    x, y, core = index // (2 * SIDE), index // 2 % SIDE, index % 2
    if (ring == 0) == (core == 0):
        return ep_of(x, (y + step) % SIDE, core)
    return ep_of((x + step) % SIDE, y, core)


def shift_z(value, step):
    return lax.ppermute(value, "grp", [(i, (i + step) % SIDE) for i in range(SIDE)])


def shift_ring(value, ring, step):
    count = 2 * SIDE * SIDE
    return lax.ppermute(value, "ep", [(i, moved(i, ring, step)) for i in range(count)])


def swap_cores(value):
    count = 2 * SIDE * SIDE
    return lax.ppermute(value, "ep", [(i, i ^ 1) for i in range(count)])


def pass_on(value):
    count = 2 * SIDE * SIDE
    pairs = [(g * count + i, (g + 1 - 2 * (i % 2)) % SIDE * count + i) for g in range(SIDE) for i in range(count)]
    return lax.ppermute(value, ("grp", "ep"), pairs)


def from_all(shift, value):
    return jnp.stack([value, shift(value, -1), shift(value, 2), shift(value, 1)])


def tie(value, *others):
    anywhere = pl.BlockSpec(memory_space=pl.ANY)
    return pl.pallas_call(
        lambda *refs: None,
        in_specs=[anywhere] * (1 + len(others)),
        out_specs=anywhere,
        out_shape=jax.ShapeDtypeStruct(value.shape, value.dtype),
        input_output_aliases={0: 0},
    )(value, *others)


def choose_kernel(steps, which, *refs):
    own, passed, out, sems = refs[0], refs[1 : 1 + steps], refs[1 + steps], refs[2 + steps]
    size = out.shape[0] // PIECES
    for away in range(SIDE):

        @pl.when(which[0] == away)
        def _(away=away):
            copies = []
            for piece in range(PIECES):
                span = pl.ds(piece * size, size)
                source = passed[piece + away - 1] if away else own.at[span]
                copies.append(pltpu.make_async_copy(source, out.at[span], sems.at[piece]))
            for copy in copies:
                copy.start()
            for copy in copies:
                copy.wait()


def choose_call(away, own, passed):
    anywhere = pl.BlockSpec(memory_space=pl.ANY)
    return pl.pallas_call(
        functools.partial(choose_kernel, len(passed)),
        in_specs=[pl.BlockSpec(memory_space=pltpu.SMEM)] + [anywhere] * (1 + len(passed)),
        out_specs=pl.BlockSpec(memory_space=pltpu.VMEM),
        out_shape=jax.ShapeDtypeStruct(own.shape, own.dtype),
        scratch_shapes=[pltpu.SemaphoreType.DMA((PIECES,))],
        compiler_params=pltpu.CompilerParams(vmem_limit_bytes=VMEM),
    )(away, own, *passed)


def hidden_kernel(capacity, tile, sources, meta, places, gate_hbm, up_hbm, *rest):
    blocks = len(sources)
    count = max(piece for block in sources for piece, _ in block) + 1
    pieces = rest[:count]
    own_out, hot_out, gate, up, gathered, compact, packed, weight_sems, row_sems = rest[-9:]
    rows = pieces[0].shape[2]
    width, hidden = gate.shape
    block_rows = BLOCK * rows
    donates, total = meta[0] == 1, meta[1]
    offsets, counts, begins = 2, 2 + SEGMENTS, 2 + 2 * SEGMENTS

    def load(block, distance):
        for unit, (piece, place) in enumerate(sources[block]):
            pltpu.make_async_copy(
                pieces[piece].at[place, distance, :, pl.ds(0, width)],
                gathered.at[block, pl.ds(unit * rows, rows)],
                row_sems.at[block],
            ).start()

    def arrive(block):
        pltpu.make_async_copy(gathered.at[block], gathered.at[block], row_sems.at[block]).wait()

    def pick(segment, block):
        start = pl.multiple_of(meta[begins + segment * blocks + block], ALIGN)
        place = places[pl.ds(segment * blocks + block, 1), :] - start
        slots = lax.broadcasted_iota(jnp.int32, (WINDOW, block_rows), 0)
        choose = jnp.where(slots == place, 1.0, 0.0).astype(jnp.bfloat16)

        found = jnp.dot(choose, gathered[block], preferred_element_type=jnp.float32).astype(jnp.bfloat16)
        compact[pl.ds(start, ALIGN), :] = compact[pl.ds(start, ALIGN), :] + found[:ALIGN]
        compact[pl.ds(start + ALIGN, WINDOW - ALIGN), :] = found[ALIGN:]

    weights = (
        pltpu.make_async_copy(gate_hbm, gate, weight_sems.at[0]),
        pltpu.make_async_copy(up_hbm, up, weight_sems.at[1]),
    )
    for block in range(blocks):
        load(block, 0)
    for copy in weights:
        copy.start()
    compact[:ALIGN, :] = jnp.zeros((ALIGN, width), jnp.bfloat16)
    for block in range(blocks):
        arrive(block)
        pick(0, block)

    @pl.when(donates)
    def _():
        def group(distance, carry):
            for block in range(blocks):
                pl.when(distance > 0)(functools.partial(arrive, block))
                pick(1 + distance, block)
                pl.when(distance < SIDE - 1)(functools.partial(load, block, distance + 1))
            return carry
        lax.fori_loop(0, SIDE, group, 0)

    for copy in weights:
        copy.wait()

    def serve(t, carry):
        span = pl.ds(pl.multiple_of(t * tile, tile), tile)
        gate_part = jnp.dot(compact[span, :], gate[...], preferred_element_type=jnp.float32)
        up_part = jnp.dot(compact[span, :], up[...], preferred_element_type=jnp.float32)
        packed[span, :] = (jax.nn.silu(gate_part) * up_part).astype(jnp.bfloat16)
        return carry

    lax.fori_loop(0, lax.div(total + tile - 1, tile), serve, 0)

    def unpack(segment, store):
        for t in range(0, capacity, WINDOW):
            begin = pl.multiple_of(meta[offsets + segment] + t, ALIGN)
            live = lax.broadcasted_iota(jnp.int32, (WINDOW, hidden), 0) < meta[counts + segment] - t
            value = packed[pl.ds(begin, WINDOW), :]
            store(pl.ds(t, WINDOW), jnp.where(live, value, jnp.zeros_like(value)))

    def own_store(span, value):
        own_out[span, :] = value

    unpack(0, own_store)
    for distance in range(SIDE):

        def hot_store(span, value, distance=distance):
            hot_out[distance, span, :] = value

        unpack(1 + distance, hot_store)


def hidden_call(capacity, tile, sources, meta, places, gate, up, pieces, after=()):
    rows = pieces[0].shape[2]
    width, hidden = gate.shape
    blocks = len(sources)
    block_rows = BLOCK * rows
    most = SEGMENTS * capacity + tile
    anywhere = pl.BlockSpec(memory_space=pl.ANY)
    return pl.pallas_call(
        functools.partial(hidden_kernel, capacity, tile, sources),
        in_specs=[pl.BlockSpec(memory_space=pltpu.SMEM), pl.BlockSpec(memory_space=pltpu.VMEM)]
        + [anywhere] * (2 + len(pieces) + len(after)),
        out_specs=[pl.BlockSpec(memory_space=pltpu.VMEM)] * 2,
        out_shape=[
            jax.ShapeDtypeStruct((capacity, hidden), jnp.bfloat16),
            jax.ShapeDtypeStruct((SIDE, capacity, hidden), jnp.bfloat16),
        ],
        scratch_shapes=[
            pltpu.VMEM((width, hidden), jnp.bfloat16),
            pltpu.VMEM((width, hidden), jnp.bfloat16),
            pltpu.VMEM((blocks, block_rows, width), jnp.bfloat16),
            pltpu.VMEM((most, width), jnp.bfloat16),
            pltpu.VMEM((most, hidden), jnp.bfloat16),
            pltpu.SemaphoreType.DMA((2,)),
            pltpu.SemaphoreType.DMA((blocks,)),
        ],
        compiler_params=pltpu.CompilerParams(vmem_limit_bytes=VMEM),
        cost_estimate=pl.CostEstimate(
            flops=SEGMENTS * capacity * width * hidden * 2,
            bytes_accessed=2 * width * hidden * 2 + 4 * blocks * block_rows * width * 2,
            transcendentals=SEGMENTS * capacity * hidden,
        ),
    )(meta, places, gate, up, *pieces, *after)

def tables(member, donates):
    blocks, block_rows = member.shape[1:]
    after = jnp.cumsum(member.reshape(SEGMENTS, -1), axis=1).reshape(member.shape)
    counts = after[:, -1, -1]
    before = jnp.concatenate([jnp.zeros((SEGMENTS, 1), jnp.int32), after[:, :-1, -1]], axis=1)
    serves = jnp.where(jnp.arange(SEGMENTS) == 0, 1, donates)
    room = (counts + ALIGN - 1) // ALIGN * ALIGN * serves
    offsets = jnp.cumsum(room) - room
    begins = offsets[:, None] + before // ALIGN * ALIGN
    places = jnp.where(member == 1, offsets[:, None, None] + after - 1, -1).reshape(SEGMENTS * blocks, block_rows)
    meta = jnp.concatenate([jnp.stack([donates, jnp.sum(room)]), offsets, counts * serves, begins.reshape(-1)])
    return meta.astype(jnp.int32), places, after, before


def down_kernel(hidden, down, out):
    out[...] = jnp.dot(hidden[...], down[...], preferred_element_type=jnp.float32).astype(jnp.bfloat16)


def down_call(hidden, down):
    slots, width = hidden.shape[0], down.shape[1]
    wide = 512
    column = lambda rows: pl.BlockSpec((rows, wide), lambda n: (0, n))
    return pl.pallas_call(
        down_kernel,
        grid=(width // wide,),
        in_specs=[pl.BlockSpec(memory_space=pltpu.VMEM), column(down.shape[0])],
        out_specs=column(slots),
        out_shape=jax.ShapeDtypeStruct((slots, width), jnp.bfloat16),
        compiler_params=pltpu.CompilerParams(vmem_limit_bytes=VMEM),
        cost_estimate=pl.CostEstimate(
            flops=2 * hidden.size * width, bytes_accessed=2 * (down.size + slots * width), transcendentals=0
        ),
    )(hidden, down)


def combine_kernel(is_late, starts, scales, own_early, hot_early, own_late, hot_late, down, copied,
                   theirs, mine, late, pair):
    block_rows = mine.shape[0] // SIDE
    late[:WINDOW, :] = jnp.dot(own_late[...], down[...], preferred_element_type=jnp.float32).astype(jnp.bfloat16)
    late[WINDOW:, :] = jnp.dot(hot_late[...], copied[...], preferred_element_type=jnp.float32).astype(jnp.bfloat16)
    for out, first in ((theirs, 0), (mine, SIDE)):
        for b in range(SIDE):
            block = first + b
            scale = scales[block * block_rows : (block + 1) * block_rows, :]
            if is_late[block]:
                value = jnp.dot(scale, late[...], preferred_element_type=jnp.float32)
            else:
                for part, ref in enumerate((own_early, hot_early)):
                    start = pl.multiple_of(starts[2 * block + part], ALIGN)
                    pair[block, part * WINDOW : (part + 1) * WINDOW, :] = ref[pl.ds(start, WINDOW), :]
                value = jnp.dot(scale, pair[block], preferred_element_type=jnp.float32)
            out[b * block_rows : (b + 1) * block_rows, :] = value.astype(jnp.bfloat16)


def combine_call(part, parts, is_late, starts, scales, own_early, hot_early, own_late, hot_late, down, copied):
    width = down.shape[1] // parts
    steps = 2
    wide = width // steps
    rows = scales.shape[0]
    whole = pl.BlockSpec(memory_space=pltpu.VMEM)
    column = lambda value: pl.BlockSpec((value.shape[0], wide), lambda n: (0, part * steps + n))
    result = pl.BlockSpec((rows // 2, wide), lambda n: (0, n))
    return pl.pallas_call(
        functools.partial(combine_kernel, is_late),
        grid=(steps,),
        in_specs=[pl.BlockSpec(memory_space=pltpu.SMEM), whole, column(own_early), column(hot_early), whole, whole]
        + [column(down), column(copied)],
        out_specs=[result, result],
        out_shape=[jax.ShapeDtypeStruct((rows // 2, width), jnp.bfloat16)] * 2,
        scratch_shapes=[
            pltpu.VMEM((2 * WINDOW, wide), jnp.bfloat16),
            pltpu.VMEM((2 * SIDE, 2 * WINDOW, wide), jnp.bfloat16),
        ],
        compiler_params=pltpu.CompilerParams(vmem_limit_bytes=VMEM),
        cost_estimate=pl.CostEstimate(
            flops=4 * hot_late.size * width + 4 * rows * WINDOW * width,
            bytes_accessed=2 * width * (2 * own_early.shape[0] + 2 * hot_late.shape[1] + rows),
            transcendentals=0,
        ),
    )(starts, scales, own_early, hot_early, own_late, hot_late, down, copied)


def add(*values):
    return sum(v.astype(jnp.float32) for v in values).astype(jnp.bfloat16)


def sent_back(hot, *others):
    cut = hot.shape[1] // 2
    ahead, behind = shift_z(hot[2, :cut], 1), shift_z(hot[2, cut:], -1)
    forward = jnp.concatenate([hot[1, :cut] + ahead, hot[1, cut:]], axis=0)
    backward = jnp.concatenate([hot[3, :cut], hot[3, cut:] + behind], axis=0)
    return tie(hot[0], *others) + shift_z(forward, 1) + shift_z(backward, -1)


def sent_back_at_once(hot):
    return hot[0] + shift_z(hot[1], 1) + shift_z(hot[3], -1) + shift_z(hot[2], 2)


def sum_to_owners(theirs, mine, rows):
    width = mine.shape[1]
    total = add(mine, swap_cores(theirs)).reshape(SIDE, SIDE, rows, width)
    cut = SIDE // 2
    ahead = shift_ring(total[2, :cut], 1, 1)
    behind = shift_ring(total[2, cut:], 1, -1)
    forward = jnp.concatenate([add(total[1, :cut], ahead), total[1, cut:]], axis=0)
    backward = jnp.concatenate([total[3, :cut], add(total[3, cut:], behind)], axis=0)
    total = add(total[0], shift_ring(forward, 1, 1), shift_ring(backward, 1, -1))
    return add(total[0], shift_ring(total[1], 0, 1), shift_ring(total[3], 0, -1), shift_ring(total[2], 0, 2))


def local(tokens, route_ids, route_gates, w_gate, w_up, w_down, hot_source):
    n_ep = lax.axis_size("ep")
    grp, ep = lax.axis_index("grp"), lax.axis_index("ep")
    core, x, y = lax.rem(ep, 2), ep // (2 * SIDE), lax.rem(ep // 2, SIDE)
    rows = tokens[0]
    row_count, width = rows.shape
    picks = route_ids.shape[2]
    cap = row_count * picks // n_ep
    donor = hot_source[0]
    own_gate, own_up, own_down = w_gate[0, 0], w_up[0, 0], w_down[0, 0]


    passed = []
    away = lax.rem(jnp.where(core == 0, grp - donor, donor - grp) + SIDE, SIDE).reshape(1)
    size = own_down.shape[0] // PIECES

    def passing(step, *after):
        if step < PIECES:
            piece = own_down[step * size : (step + 1) * size]
            piece = tie(piece, *after) if after else piece
            piece = jnp.where(away[0] == 0, piece, passed[-1]) if step else piece
        else:
            piece = passed[-1]
        passed.append(pass_on(piece))

    routes = jnp.concatenate([route_ids[0].astype(jnp.bfloat16), route_gates[0]], axis=1)
    rows = jnp.concatenate([rows, jnp.pad(routes, ((0, 0), (0, 128 - 2 * picks)))], axis=1)
    below, above = shift_z(rows, 1), shift_z(rows, -1)
    cut = row_count // 2
    far = (shift_z(below[:cut], 1), shift_z(above[cut:], -1))
    unit_low = jnp.stack([rows, above])
    passing(0, unit_low)
    below_low, above_low = shift_ring(unit_low, 0, 1), shift_ring(unit_low, 0, -1)
    unit_high = jnp.stack([jnp.concatenate(far, axis=0), below])
    below_high, above_high = shift_ring(unit_high, 0, 1), shift_ring(unit_high, 0, -1)
    far_low, far_high = shift_ring(below_low, 0, 1), shift_ring(above_high, 0, -1)

    def join(*parts):
        return jnp.concatenate(parts).reshape(2, SIDE, row_count, rows.shape[1])

    near_parts = (unit_low, unit_high, above_low, above_high, far_low, far_high, below_low, below_high)
    info = jnp.concatenate([part[:, :, width : width + 2 * picks] for part in near_parts])
    info = info.transpose(0, 2, 1).reshape(SIDE, SIDE, -1, 128)
    info = from_all(lambda value, step: shift_ring(value, 1, step), info)
    low = tie(join(*near_parts[:4]), passed[0], info)
    high = tie(join(*near_parts[4:]), info)

    low_below, high_above = shift_ring(low, 1, 1), shift_ring(high, 1, -1)
    near = [low, high]
    near_other = [swap_cores(piece) for piece in near]
    passing(1)
    high_on, low_on = (tie(value, low_below, high_above, passed[1], *near_other) for value in (high, low))
    high_below, low_above = shift_ring(high_on, 1, 1), shift_ring(low_on, 1, -1)
    info = jnp.stack([info, swap_cores(info)])
    info = info.reshape(2 * SIDE, SIDE, SIDE, 2 * picks, row_count)
    first = [low_below, high_above]
    first_other = [swap_cores(piece) for piece in first]
    passing(2)
    last_low, last_high = (tie(value, high_below, low_above, passed[2], info, *first_other) for value in first)
    low_far, high_far = shift_ring(last_low, 1, 1), shift_ring(last_high, 1, -1)
    second = [tie(high_below, passed[2]), tie(low_above, passed[2])]
    second_other = [swap_cores(piece) for piece in second]
    passing(3)
    early = near + [second[1], first[1], first[0], second[0]]
    early = early + near_other + [second_other[1], first_other[1], first_other[0], second_other[0]]

    order = [(other, second) for seconds in STAGES for other in (0, 1) for second in seconds]
    info = jnp.stack([info[other * SIDE + second] for other, second in order])
    ids = info[:, :, :, :picks].astype(jnp.int32)
    gates = info[:, :, :, picks:].astype(jnp.float32)
    is_own, is_hot = ids[:, :, 0] == ep, ids == ep + n_ep
    block_rows = BLOCK * row_count
    member = jnp.concatenate([jnp.any(is_own, axis=2)[:, :, None], jnp.any(is_hot, axis=3)], axis=2)
    member = member.transpose(2, 0, 1, 3).reshape(SEGMENTS, len(order), block_rows).astype(jnp.int32)
    own_scale = jnp.sum(jnp.where(is_own, gates[:, :, 0], 0.0), axis=2).reshape(len(order), block_rows)
    hot_scale = jnp.sum(jnp.where(is_hot[:, :, 0], gates[:, :, 0], 0.0), axis=2).reshape(len(order), block_rows)
    donates = (donor == grp).astype(jnp.int32)

    own_hidden, hot_hidden, afters, befores = [], [], [], []
    begin, begin_slot = 0, 0
    for stage, seconds in enumerate(STAGES):
        if stage:
            far = [tie(piece, own_hidden[-1], passed[3]) for piece in (low_far, high_far)]
            pieces = far + [swap_cores(piece) for piece in far]
            own_early = down_call(tie(own_hidden[0], *far), own_down)
        else:
            pieces = early
        blocks = 2 * len(seconds)
        slots = blocks * BLOCK * cap
        meta, places, after, before = tables(member[:, begin : begin + blocks], donates)
        sources = [
            [(2 * block + first // 2, first % 2) for first in range(SIDE)] for block in range(blocks)
        ]
        own, hot = hidden_call(
            slots, 256 if blocks > 2 else 128, sources, meta, places, own_gate, own_up, pieces, after=[own_early] if stage else ()
        )
        own_hidden.append(own)
        hot_hidden.append(hot)
        afters.append(after[:2] + begin_slot)
        befores.append(before[:2] + begin_slot)
        begin, begin_slot = begin + blocks, begin_slot + slots

    copied = choose_call(tie(away, own_hidden[1]), own_down, passed)
    hot_early = down_call(sent_back(hot_hidden[0], own_hidden[1]), copied)
    hot_late = sent_back_at_once(hot_hidden[1])

    after, before = jnp.concatenate(afters, axis=1), jnp.concatenate(befores, axis=1)
    wanted = [order.index((other, second)) for other in (1, 0) for second in range(SIDE)]
    take = lambda value: jnp.stack([value[:, index] for index in wanted], axis=1)
    is_late = [order[index][1] in STAGES[-1] for index in wanted]
    most = [begin_slot - WINDOW if late_block else begin_slot - slots - WINDOW for late_block in is_late]
    starts = jnp.minimum(take(before) // ALIGN * ALIGN, jnp.array(most, jnp.int32))
    slots = jnp.arange(WINDOW, dtype=jnp.int32)
    chosen = (take(after) - 1 - starts[:, :, None])[..., None] == slots
    scale = take(jnp.stack([own_scale, hot_scale]))[..., None]
    scales = jnp.where(chosen, scale, 0.0).astype(jnp.bfloat16)
    scales = jnp.concatenate([scales[0], scales[1]], axis=-1).reshape(len(order) * block_rows, 2 * WINDOW)
    starts = starts.T.reshape(-1)

    parts = 2
    results = []
    for part in range(parts):
        theirs, mine = combine_call(
            part, parts, is_late, starts, scales, own_early, hot_early, own_hidden[1], hot_late, own_down, copied
        )
        results.append(sum_to_owners(theirs, mine, row_count))
    return jnp.concatenate(results, axis=1)[None]


def solution(mesh):
    placed = (
        P("grp", "ep", None),
        P("grp", "ep", None),
        P("grp", "ep", None),
        P("grp", "ep", None, None),
        P("grp", "ep", None, None),
        P("grp", "ep", None, None),
        P("ep"),
    )
    return jax.shard_map(
        local, mesh=mesh, in_specs=placed, out_specs=P("grp", "ep", None), check_vma=False
    )
```

```python
import functools

import jax
import jax.numpy as jnp
from jax import lax
from jax.experimental import pallas as pl
from jax.experimental.pallas import tpu as pltpu
from jax.sharding import PartitionSpec as P

SIDE = 4
SEGMENTS = 1 + SIDE
BLOCK = 4
WINDOW = 128
ALIGN = 16
PIECES = 2
STAGES = ((0, 1, 3), (2,))
VMEM = 60 * 1024 * 1024


def ep_of(x, y, core):
    return (x * SIDE + y) * 2 + core


def moved(index, ring, step):
    x, y, core = index // (2 * SIDE), index // 2 % SIDE, index % 2
    if (ring == 0) == (core == 0):
        return ep_of(x, (y + step) % SIDE, core)
    return ep_of((x + step) % SIDE, y, core)


def shift_z(value, step):
    return lax.ppermute(value, "grp", [(i, (i + step) % SIDE) for i in range(SIDE)])


def shift_ring(value, ring, step):
    count = 2 * SIDE * SIDE
    return lax.ppermute(value, "ep", [(i, moved(i, ring, step)) for i in range(count)])


def swap_cores(value):
    count = 2 * SIDE * SIDE
    return lax.ppermute(value, "ep", [(i, i ^ 1) for i in range(count)])


def pass_on(value):
    count = 2 * SIDE * SIDE
    pairs = [(g * count + i, (g + 1 - 2 * (i % 2)) % SIDE * count + i) for g in range(SIDE) for i in range(count)]
    return lax.ppermute(value, ("grp", "ep"), pairs)


def from_all(shift, value):
    return jnp.stack([value, shift(value, -1), shift(value, 2), shift(value, 1)])


def tie(value, *others):
    anywhere = pl.BlockSpec(memory_space=pl.ANY)
    return pl.pallas_call(
        lambda *refs: None,
        in_specs=[anywhere] * (1 + len(others)),
        out_specs=anywhere,
        out_shape=jax.ShapeDtypeStruct(value.shape, value.dtype),
        input_output_aliases={0: 0},
    )(value, *others)


def choose_kernel(steps, which, hot, own, *refs):
    passed, (copied, out, held, in_sems, out_sems) = refs[:steps], refs[steps:]
    chunks = in_sems.shape[0]
    size = held.shape[0] // chunks
    each = chunks // PIECES
    wide = 512 if held.shape[1] % 512 == 0 else 256
    spans = [pl.ds(chunk * size, size) for chunk in range(chunks)]
    for away in range(SIDE):

        @pl.when(which[0] == away)
        def _(away=away):
            for chunk, span in enumerate(spans):
                source = passed[chunk // each + away - 1].at[spans[chunk % each]] if away else own.at[span]
                pltpu.make_async_copy(source, held.at[span], in_sems.at[chunk]).start()

    copies = []
    for chunk, span in enumerate(spans):
        pltpu.make_async_copy(held.at[span], held.at[span], in_sems.at[chunk]).wait()
        copies.append(pltpu.make_async_copy(held.at[span], copied.at[span], out_sems.at[chunk]))
        copies[-1].start()

    def part(n, carry):
        columns = pl.ds(pl.multiple_of(n * wide, wide), wide)
        out[:, columns] = jnp.dot(hot[...], held[:, columns], preferred_element_type=jnp.float32).astype(jnp.bfloat16)
        return carry

    lax.fori_loop(0, held.shape[1] // wide, part, 0)
    for copy in copies:
        copy.wait()


def choose_call(away, hot, own, passed):
    anywhere, whole = pl.BlockSpec(memory_space=pl.ANY), pl.BlockSpec(memory_space=pltpu.VMEM)
    chunks = 4 * PIECES
    return pl.pallas_call(
        functools.partial(choose_kernel, len(passed)),
        in_specs=[pl.BlockSpec(memory_space=pltpu.SMEM), whole] + [anywhere] * (1 + len(passed)),
        out_specs=[anywhere, whole],
        out_shape=[
            jax.ShapeDtypeStruct(own.shape, own.dtype),
            jax.ShapeDtypeStruct((hot.shape[0], own.shape[1]), own.dtype),
        ],
        scratch_shapes=[
            pltpu.VMEM(own.shape, own.dtype),
            pltpu.SemaphoreType.DMA((chunks,)),
            pltpu.SemaphoreType.DMA((chunks,)),
        ],
        compiler_params=pltpu.CompilerParams(vmem_limit_bytes=VMEM),
        cost_estimate=pl.CostEstimate(
            flops=2 * hot.size * own.shape[1], bytes_accessed=6 * own.size, transcendentals=0
        ),
    )(away, hot, own, *passed)


def hidden_kernel(capacity, tile, sources, meta, places, gate_hbm, up_hbm, *rest):
    blocks = len(sources)
    count = max(piece for block in sources for piece, _ in block) + 1
    pieces = rest[:count]
    own_out, hot_out, gate, up, gathered, compact, packed, weight_sems, row_sems = rest[-9:]
    rows = pieces[0].shape[2]
    width, hidden = gate.shape
    block_rows = BLOCK * rows
    donates, total = meta[0] == 1, meta[1]
    offsets, counts, begins = 2, 2 + SEGMENTS, 2 + 2 * SEGMENTS

    at_once = gathered.shape[0] == SIDE * blocks

    def slot_of(block, distance):
        return distance * blocks + block if at_once else block

    def load(block, distance):
        slot = slot_of(block, distance)
        for unit, (piece, place) in enumerate(sources[block]):
            pltpu.make_async_copy(
                pieces[piece].at[place, distance, :, pl.ds(0, width)],
                gathered.at[slot, pl.ds(unit * rows, rows)],
                row_sems.at[slot],
            ).start()

    def arrive(block, distance):
        slot = slot_of(block, distance)
        pltpu.make_async_copy(gathered.at[slot], gathered.at[slot], row_sems.at[slot]).wait()

    def pick(segment, block, distance):
        start = pl.multiple_of(meta[begins + segment * blocks + block], ALIGN)
        place = places[pl.ds(segment * blocks + block, 1), :] - start
        slots = lax.broadcasted_iota(jnp.int32, (WINDOW, block_rows), 0)
        choose = jnp.where(slots == place, 1.0, 0.0).astype(jnp.bfloat16)

        found = jnp.dot(choose, gathered[slot_of(block, distance)], preferred_element_type=jnp.float32).astype(jnp.bfloat16)
        compact[pl.ds(start, ALIGN), :] = compact[pl.ds(start, ALIGN), :] + found[:ALIGN]
        compact[pl.ds(start + ALIGN, WINDOW - ALIGN), :] = found[ALIGN:]

    weights = (
        pltpu.make_async_copy(gate_hbm, gate, weight_sems.at[0]),
        pltpu.make_async_copy(up_hbm, up, weight_sems.at[1]),
    )
    for block in range(blocks):
        load(block, 0)
    for copy in weights:
        copy.start()
    if at_once:

        @pl.when(donates)
        def _():
            for distance in range(1, SIDE):
                for block in range(blocks):
                    load(block, distance)

    compact[:ALIGN, :] = jnp.zeros((ALIGN, width), jnp.bfloat16)
    for block in range(blocks):
        arrive(block, 0)
        pick(0, block, 0)

    @pl.when(donates)
    def _():
        def group(distance, carry):
            for block in range(blocks):
                pl.when(distance > 0)(functools.partial(arrive, block, distance))
                pick(1 + distance, block, distance)
                if not at_once:
                    pl.when(distance < SIDE - 1)(functools.partial(load, block, distance + 1))
            return carry
        lax.fori_loop(0, SIDE, group, 0)

    for copy in weights:
        copy.wait()

    def serve(t, carry):
        span = pl.ds(pl.multiple_of(t * tile, tile), tile)
        gate_part = jnp.dot(compact[span, :], gate[...], preferred_element_type=jnp.float32)
        up_part = jnp.dot(compact[span, :], up[...], preferred_element_type=jnp.float32)
        packed[span, :] = (jax.nn.silu(gate_part) * up_part).astype(jnp.bfloat16)
        return carry

    lax.fori_loop(0, lax.div(total + tile - 1, tile), serve, 0)

    def unpack(segment, store):
        for t in range(0, capacity, WINDOW):
            begin = pl.multiple_of(meta[offsets + segment] + t, ALIGN)
            live = lax.broadcasted_iota(jnp.int32, (WINDOW, hidden), 0) < meta[counts + segment] - t
            value = packed[pl.ds(begin, WINDOW), :]
            store(pl.ds(t, WINDOW), jnp.where(live, value, jnp.zeros_like(value)))

    def own_store(span, value):
        own_out[span, :] = value

    unpack(0, own_store)
    for distance in range(SIDE):

        def hot_store(span, value, distance=distance):
            hot_out[distance, span, :] = value

        unpack(1 + distance, hot_store)


def hidden_call(capacity, tile, sources, meta, places, gate, up, pieces, after=()):
    rows = pieces[0].shape[2]
    width, hidden = gate.shape
    blocks = len(sources)
    block_rows = BLOCK * rows
    most = SEGMENTS * capacity + tile
    slots = blocks if blocks > 2 else SIDE * blocks
    anywhere = pl.BlockSpec(memory_space=pl.ANY)
    return pl.pallas_call(
        functools.partial(hidden_kernel, capacity, tile, sources),
        in_specs=[pl.BlockSpec(memory_space=pltpu.SMEM), pl.BlockSpec(memory_space=pltpu.VMEM)]
        + [anywhere] * (2 + len(pieces) + len(after)),
        out_specs=[pl.BlockSpec(memory_space=pltpu.VMEM)] * 2,
        out_shape=[
            jax.ShapeDtypeStruct((capacity, hidden), jnp.bfloat16),
            jax.ShapeDtypeStruct((SIDE, capacity, hidden), jnp.bfloat16),
        ],
        scratch_shapes=[
            pltpu.VMEM((width, hidden), jnp.bfloat16),
            pltpu.VMEM((width, hidden), jnp.bfloat16),
            pltpu.VMEM((slots, block_rows, width), jnp.bfloat16),
            pltpu.VMEM((most, width), jnp.bfloat16),
            pltpu.VMEM((most, hidden), jnp.bfloat16),
            pltpu.SemaphoreType.DMA((2,)),
            pltpu.SemaphoreType.DMA((slots,)),
        ],
        compiler_params=pltpu.CompilerParams(vmem_limit_bytes=VMEM),
        cost_estimate=pl.CostEstimate(
            flops=SEGMENTS * capacity * width * hidden * 2,
            bytes_accessed=2 * width * hidden * 2 + 4 * blocks * block_rows * width * 2,
            transcendentals=SEGMENTS * capacity * hidden,
        ),
    )(meta, places, gate, up, *pieces, *after)

def tables(member, donates):
    blocks, block_rows = member.shape[1:]
    after = jnp.cumsum(member.reshape(SEGMENTS, -1), axis=1).reshape(member.shape)
    counts = after[:, -1, -1]
    before = jnp.concatenate([jnp.zeros((SEGMENTS, 1), jnp.int32), after[:, :-1, -1]], axis=1)
    serves = jnp.where(jnp.arange(SEGMENTS) == 0, 1, donates)
    room = (counts + ALIGN - 1) // ALIGN * ALIGN * serves
    offsets = jnp.cumsum(room) - room
    begins = offsets[:, None] + before // ALIGN * ALIGN
    places = jnp.where(member == 1, offsets[:, None, None] + after - 1, -1).reshape(SEGMENTS * blocks, block_rows)
    meta = jnp.concatenate([jnp.stack([donates, jnp.sum(room)]), offsets, counts * serves, begins.reshape(-1)])
    return meta.astype(jnp.int32), places, after, before


def down_kernel(hidden, down, out):
    out[...] = jnp.dot(hidden[...], down[...], preferred_element_type=jnp.float32).astype(jnp.bfloat16)


def down_call(hidden, down):
    slots, width = hidden.shape[0], down.shape[1]
    wide = width // 2
    column = lambda rows: pl.BlockSpec((rows, wide), lambda n: (0, n))
    return pl.pallas_call(
        down_kernel,
        grid=(width // wide,),
        in_specs=[pl.BlockSpec(memory_space=pltpu.VMEM), column(down.shape[0])],
        out_specs=column(slots),
        out_shape=jax.ShapeDtypeStruct((slots, width), jnp.bfloat16),
        compiler_params=pltpu.CompilerParams(vmem_limit_bytes=VMEM),
        cost_estimate=pl.CostEstimate(
            flops=2 * hidden.size * width, bytes_accessed=2 * (down.size + slots * width), transcendentals=0
        ),
    )(hidden, down)


def combine_kernel(is_late, starts, scales, own_early, hot_early, own_late, hot_late, down, copied,
                   theirs, mine, late, pair):
    block_rows = mine.shape[0] // SIDE
    late[:WINDOW, :] = jnp.dot(own_late[...], down[...], preferred_element_type=jnp.float32).astype(jnp.bfloat16)
    late[WINDOW:, :] = jnp.dot(hot_late[...], copied[...], preferred_element_type=jnp.float32).astype(jnp.bfloat16)
    for out, first in ((theirs, 0), (mine, SIDE)):
        for b in range(SIDE):
            block = first + b
            scale = scales[block * block_rows : (block + 1) * block_rows, :]
            if is_late[block]:
                value = jnp.dot(scale, late[...], preferred_element_type=jnp.float32)
            else:
                for part, ref in enumerate((own_early, hot_early)):
                    start = pl.multiple_of(starts[2 * block + part], ALIGN)
                    pair[block, part * WINDOW : (part + 1) * WINDOW, :] = ref[pl.ds(start, WINDOW), :]
                value = jnp.dot(scale, pair[block], preferred_element_type=jnp.float32)
            out[b * block_rows : (b + 1) * block_rows, :] = value.astype(jnp.bfloat16)


def combine_call(part, parts, is_late, starts, scales, own_early, hot_early, own_late, hot_late, down, copied):
    width = down.shape[1] // parts
    steps = 2
    wide = width // steps
    rows = scales.shape[0]
    whole = pl.BlockSpec(memory_space=pltpu.VMEM)
    column = lambda value: pl.BlockSpec((value.shape[0], wide), lambda n: (0, part * steps + n))
    result = pl.BlockSpec((rows // 2, wide), lambda n: (0, n))
    return pl.pallas_call(
        functools.partial(combine_kernel, is_late),
        grid=(steps,),
        in_specs=[pl.BlockSpec(memory_space=pltpu.SMEM), whole, column(own_early), column(hot_early), whole, whole]
        + [column(down), column(copied)],
        out_specs=[result, result],
        out_shape=[jax.ShapeDtypeStruct((rows // 2, width), jnp.bfloat16)] * 2,
        scratch_shapes=[
            pltpu.VMEM((2 * WINDOW, wide), jnp.bfloat16),
            pltpu.VMEM((2 * SIDE, 2 * WINDOW, wide), jnp.bfloat16),
        ],
        compiler_params=pltpu.CompilerParams(vmem_limit_bytes=VMEM),
        cost_estimate=pl.CostEstimate(
            flops=4 * hot_late.size * width + 4 * rows * WINDOW * width,
            bytes_accessed=2 * width * (2 * own_early.shape[0] + 2 * hot_late.shape[1] + rows),
            transcendentals=0,
        ),
    )(starts, scales, own_early, hot_early, own_late, hot_late, down, copied)


def add(*values):
    return sum(v.astype(jnp.float32) for v in values).astype(jnp.bfloat16)


def sent_back(hot, *others):
    cut = hot.shape[1] // 2
    ahead, behind = shift_z(hot[2, :cut], 1), shift_z(hot[2, cut:], -1)
    forward = jnp.concatenate([hot[1, :cut] + ahead, hot[1, cut:]], axis=0)
    backward = jnp.concatenate([hot[3, :cut], hot[3, cut:] + behind], axis=0)
    return tie(hot[0], *others) + shift_z(forward, 1) + shift_z(backward, -1)


def sent_back_at_once(hot):
    return hot[0] + shift_z(hot[1], 1) + shift_z(hot[3], -1) + shift_z(hot[2], 2)


def sum_to_owners(theirs, mine, rows):
    width = mine.shape[1]
    total = add(mine, swap_cores(theirs)).reshape(SIDE, SIDE, rows, width)
    cut = SIDE // 2
    ahead = shift_ring(total[2, :cut], 1, 1)
    behind = shift_ring(total[2, cut:], 1, -1)
    forward = jnp.concatenate([add(total[1, :cut], ahead), total[1, cut:]], axis=0)
    backward = jnp.concatenate([total[3, :cut], add(total[3, cut:], behind)], axis=0)
    total = add(total[0], shift_ring(forward, 1, 1), shift_ring(backward, 1, -1))
    return add(total[0], shift_ring(total[1], 0, 1), shift_ring(total[3], 0, -1), shift_ring(total[2], 0, 2))


def local(tokens, route_ids, route_gates, w_gate, w_up, w_down, hot_source):
    n_ep = lax.axis_size("ep")
    grp, ep = lax.axis_index("grp"), lax.axis_index("ep")
    core, x, y = lax.rem(ep, 2), ep // (2 * SIDE), lax.rem(ep // 2, SIDE)
    rows = tokens[0]
    row_count, width = rows.shape
    picks = route_ids.shape[2]
    cap = row_count * picks // n_ep
    donor = hot_source[0]
    own_gate, own_up, own_down = w_gate[0, 0], w_up[0, 0], w_down[0, 0]


    passed = []
    away = lax.rem(jnp.where(core == 0, grp - donor, donor - grp) + SIDE, SIDE).reshape(1)
    size = own_down.shape[0] // PIECES

    def passing(step, *after):
        if step < PIECES:
            piece = own_down[step * size : (step + 1) * size]
            piece = tie(piece, *after) if after else piece
            piece = jnp.where(away[0] == 0, piece, passed[-1]) if step else piece
        else:
            piece = passed[-1]
        passed.append(pass_on(piece))

    routes = jnp.concatenate([route_ids[0].astype(jnp.bfloat16), route_gates[0]], axis=1)
    rows = jnp.concatenate([rows, jnp.pad(routes, ((0, 0), (0, 128 - 2 * picks)))], axis=1)
    below, above = shift_z(rows, 1), shift_z(rows, -1)
    cut = row_count // 2
    far = (shift_z(below[:cut], 1), shift_z(above[cut:], -1))
    unit_low = jnp.stack([rows, above])
    passing(0, unit_low)
    below_low, above_low = shift_ring(unit_low, 0, 1), shift_ring(unit_low, 0, -1)
    unit_high = jnp.stack([jnp.concatenate(far, axis=0), below])
    below_high, above_high = shift_ring(unit_high, 0, 1), shift_ring(unit_high, 0, -1)
    far_low, far_high = shift_ring(below_low, 0, 1), shift_ring(above_high, 0, -1)

    def join(*parts):
        return jnp.concatenate(parts).reshape(2, SIDE, row_count, rows.shape[1])

    near_parts = (unit_low, unit_high, above_low, above_high, far_low, far_high, below_low, below_high)
    info = jnp.concatenate([part[:, :, width : width + 2 * picks] for part in near_parts])
    info = info.transpose(0, 2, 1).reshape(SIDE, SIDE, -1, 128)
    info = from_all(lambda value, step: shift_ring(value, 1, step), info)
    low = tie(join(*near_parts[:4]), passed[0], info)
    high = tie(join(*near_parts[4:]), info)

    low_below, high_above = shift_ring(low, 1, 1), shift_ring(high, 1, -1)
    near = [low, high]
    near_other = [swap_cores(piece) for piece in near]
    passing(1)
    high_on, low_on = (tie(value, low_below, high_above, passed[1], *near_other) for value in (high, low))
    high_below, low_above = shift_ring(high_on, 1, 1), shift_ring(low_on, 1, -1)
    info = jnp.stack([info, swap_cores(info)])
    info = info.reshape(2 * SIDE, SIDE, SIDE, 2 * picks, row_count)
    first = [low_below, high_above]
    first_other = [swap_cores(piece) for piece in first]
    passing(2)
    last_low, last_high = (tie(value, high_below, low_above, passed[2], info, *first_other) for value in first)
    low_far, high_far = shift_ring(last_low, 1, 1), shift_ring(last_high, 1, -1)
    second = [tie(high_below, passed[2]), tie(low_above, passed[2])]
    second_other = [swap_cores(piece) for piece in second]
    passing(3)
    early = near + [second[1], first[1], first[0], second[0]]
    early = early + near_other + [second_other[1], first_other[1], first_other[0], second_other[0]]

    order = [(other, second) for seconds in STAGES for other in (0, 1) for second in seconds]
    info = jnp.stack([info[other * SIDE + second] for other, second in order])
    ids = info[:, :, :, :picks].astype(jnp.int32)
    gates = info[:, :, :, picks:].astype(jnp.float32)
    is_own, is_hot = ids[:, :, 0] == ep, ids == ep + n_ep
    block_rows = BLOCK * row_count
    member = jnp.concatenate([jnp.any(is_own, axis=2)[:, :, None], jnp.any(is_hot, axis=3)], axis=2)
    member = member.transpose(2, 0, 1, 3).reshape(SEGMENTS, len(order), block_rows).astype(jnp.int32)
    own_scale = jnp.sum(jnp.where(is_own, gates[:, :, 0], 0.0), axis=2).reshape(len(order), block_rows)
    hot_scale = jnp.sum(jnp.where(is_hot[:, :, 0], gates[:, :, 0], 0.0), axis=2).reshape(len(order), block_rows)
    donates = (donor == grp).astype(jnp.int32)

    own_hidden, hot_hidden, afters, befores = [], [], [], []
    begin, begin_slot = 0, 0
    for stage, seconds in enumerate(STAGES):
        if stage:
            far = [tie(piece, own_hidden[-1], passed[3]) for piece in (low_far, high_far)]
            pieces = far + [swap_cores(piece) for piece in far]
            own_early = down_call(tie(own_hidden[0], *far), own_down)
        else:
            pieces = early
        blocks = 2 * len(seconds)
        slots = blocks * BLOCK * cap
        meta, places, after, before = tables(member[:, begin : begin + blocks], donates)
        sources = [
            [(2 * block + first // 2, first % 2) for first in range(SIDE)] for block in range(blocks)
        ]
        own, hot = hidden_call(
            slots, 256 if blocks > 2 else 128, sources, meta, places, own_gate, own_up, pieces, after=[own_early] if stage else ()
        )
        own_hidden.append(own)
        hot_hidden.append(hot)
        afters.append(after[:2] + begin_slot)
        befores.append(before[:2] + begin_slot)
        begin, begin_slot = begin + blocks, begin_slot + slots

    copied, hot_early = choose_call(away, sent_back(hot_hidden[0], own_hidden[1]), own_down, passed)
    hot_late = sent_back_at_once(hot_hidden[1])

    after, before = jnp.concatenate(afters, axis=1), jnp.concatenate(befores, axis=1)
    wanted = [order.index((other, second)) for other in (1, 0) for second in range(SIDE)]
    take = lambda value: jnp.stack([value[:, index] for index in wanted], axis=1)
    is_late = [order[index][1] in STAGES[-1] for index in wanted]
    most = [begin_slot - WINDOW if late_block else begin_slot - slots - WINDOW for late_block in is_late]
    starts = jnp.minimum(take(before) // ALIGN * ALIGN, jnp.array(most, jnp.int32))
    slots = jnp.arange(WINDOW, dtype=jnp.int32)
    chosen = (take(after) - 1 - starts[:, :, None])[..., None] == slots
    scale = take(jnp.stack([own_scale, hot_scale]))[..., None]
    scales = jnp.where(chosen, scale, 0.0).astype(jnp.bfloat16)
    scales = jnp.concatenate([scales[0], scales[1]], axis=-1).reshape(len(order) * block_rows, 2 * WINDOW)
    starts = starts.T.reshape(-1)

    parts = 2
    results = []
    for part in range(parts):
        theirs, mine = combine_call(
            part, parts, is_late, starts, scales, own_early, hot_early, own_hidden[1], hot_late, own_down, copied
        )
        results.append(sum_to_owners(theirs, mine, row_count))
    return jnp.concatenate(results, axis=1)[None]


def solution(mesh):
    placed = (
        P("grp", "ep", None),
        P("grp", "ep", None),
        P("grp", "ep", None),
        P("grp", "ep", None, None),
        P("grp", "ep", None, None),
        P("grp", "ep", None, None),
        P("ep"),
    )
    return jax.shard_map(
        local, mesh=mesh, in_specs=placed, out_specs=P("grp", "ep", None), check_vma=False
    )
```

```python
import functools

import jax
import jax.numpy as jnp
from jax import lax
from jax.experimental import pallas as pl
from jax.experimental.pallas import tpu as pltpu
from jax.sharding import PartitionSpec as P

SIDE = 4
SEGMENTS = 1 + SIDE
BLOCK = 4
WINDOW = 128
ALIGN = 16
PIECES = 2
STAGES = ((0, 1, 3), (2,))
VMEM = 60 * 1024 * 1024


def ep_of(x, y, core):
    return (x * SIDE + y) * 2 + core


def moved(index, ring, step):
    x, y, core = index // (2 * SIDE), index // 2 % SIDE, index % 2
    if (ring == 0) == (core == 0):
        return ep_of(x, (y + step) % SIDE, core)
    return ep_of((x + step) % SIDE, y, core)


def shift_z(value, step):
    return lax.ppermute(value, "grp", [(i, (i + step) % SIDE) for i in range(SIDE)])


def shift_ring(value, ring, step):
    count = 2 * SIDE * SIDE
    return lax.ppermute(value, "ep", [(i, moved(i, ring, step)) for i in range(count)])


def swap_cores(value):
    count = 2 * SIDE * SIDE
    return lax.ppermute(value, "ep", [(i, i ^ 1) for i in range(count)])


def pass_on(value):
    count = 2 * SIDE * SIDE
    pairs = [(g * count + i, (g + 1 - 2 * (i % 2)) % SIDE * count + i) for g in range(SIDE) for i in range(count)]
    return lax.ppermute(value, ("grp", "ep"), pairs)


def from_all(shift, value):
    return jnp.stack([value, shift(value, -1), shift(value, 2), shift(value, 1)])


def tie(value, *others):
    anywhere = pl.BlockSpec(memory_space=pl.ANY)
    return pl.pallas_call(
        lambda *refs: None,
        in_specs=[anywhere] * (1 + len(others)),
        out_specs=anywhere,
        out_shape=jax.ShapeDtypeStruct(value.shape, value.dtype),
        input_output_aliases={0: 0},
    )(value, *others)


def choose_kernel(steps, which, hot, own, *refs):
    passed, (copied, out, held, in_sems, out_sems) = refs[:steps], refs[steps:]
    chunks = in_sems.shape[0]
    size = held.shape[0] // chunks
    each = chunks // PIECES
    wide = 512 if held.shape[1] % 512 == 0 else 256
    spans = [pl.ds(chunk * size, size) for chunk in range(chunks)]
    for away in range(SIDE):

        @pl.when(which[0] == away)
        def _(away=away):
            for chunk, span in enumerate(spans):
                source = passed[chunk // each + away - 1].at[spans[chunk % each]] if away else own.at[span]
                pltpu.make_async_copy(source, held.at[span], in_sems.at[chunk]).start()

    copies = []
    for chunk, span in enumerate(spans):
        pltpu.make_async_copy(held.at[span], held.at[span], in_sems.at[chunk]).wait()
        copies.append(pltpu.make_async_copy(held.at[span], copied.at[span], out_sems.at[chunk]))
        copies[-1].start()

    def part(n, carry):
        columns = pl.ds(pl.multiple_of(n * wide, wide), wide)
        out[:, columns] = jnp.dot(hot[...], held[:, columns], preferred_element_type=jnp.float32).astype(jnp.bfloat16)
        return carry

    lax.fori_loop(0, held.shape[1] // wide, part, 0)
    for copy in copies:
        copy.wait()


def choose_call(away, hot, own, passed):
    anywhere, whole = pl.BlockSpec(memory_space=pl.ANY), pl.BlockSpec(memory_space=pltpu.VMEM)
    chunks = 4 * PIECES
    return pl.pallas_call(
        functools.partial(choose_kernel, len(passed)),
        in_specs=[pl.BlockSpec(memory_space=pltpu.SMEM), whole] + [anywhere] * (1 + len(passed)),
        out_specs=[anywhere, whole],
        out_shape=[
            jax.ShapeDtypeStruct(own.shape, own.dtype),
            jax.ShapeDtypeStruct((hot.shape[0], own.shape[1]), own.dtype),
        ],
        scratch_shapes=[
            pltpu.VMEM(own.shape, own.dtype),
            pltpu.SemaphoreType.DMA((chunks,)),
            pltpu.SemaphoreType.DMA((chunks,)),
        ],
        compiler_params=pltpu.CompilerParams(vmem_limit_bytes=VMEM),
        cost_estimate=pl.CostEstimate(
            flops=2 * hot.size * own.shape[1], bytes_accessed=6 * own.size, transcendentals=0
        ),
    )(away, hot, own, *passed)


def hidden_kernel(capacity, tile, sources, meta, places, gate_hbm, up_hbm, *rest):
    blocks = len(sources)
    count = max(piece for block in sources for piece, _ in block) + 1
    pieces = rest[:count]
    own_out, hot_out, gate, up, gathered, compact, packed, weight_sems, row_sems = rest[-9:]
    rows = pieces[0].shape[2]
    width, hidden = gate.shape
    block_rows = BLOCK * rows
    donates, total = meta[0] == 1, meta[1]
    offsets, counts, begins = 3, 3 + SEGMENTS, 3 + 2 * SEGMENTS

    at_once = gathered.shape[0] == SIDE * blocks

    def slot_of(block, distance):
        return distance * blocks + block if at_once else block

    def load(block, distance):
        slot = slot_of(block, distance)
        for unit, (piece, place) in enumerate(sources[block]):
            pltpu.make_async_copy(
                pieces[piece].at[place, distance, :, pl.ds(0, width)],
                gathered.at[slot, pl.ds(unit * rows, rows)],
                row_sems.at[slot],
            ).start()

    def arrive(block, distance):
        slot = slot_of(block, distance)
        pltpu.make_async_copy(gathered.at[slot], gathered.at[slot], row_sems.at[slot]).wait()

    def pick(segment, block, distance):
        start = pl.multiple_of(meta[begins + segment * blocks + block], ALIGN)
        place = places[pl.ds(segment * blocks + block, 1), :] - start
        slots = lax.broadcasted_iota(jnp.int32, (WINDOW, block_rows), 0)
        choose = jnp.where(slots == place, 1.0, 0.0).astype(jnp.bfloat16)

        found = jnp.dot(choose, gathered[slot_of(block, distance)], preferred_element_type=jnp.float32).astype(jnp.bfloat16)
        compact[pl.ds(start, ALIGN), :] = compact[pl.ds(start, ALIGN), :] + found[:ALIGN]
        compact[pl.ds(start + ALIGN, WINDOW - ALIGN), :] = found[ALIGN:]

    weights = (
        pltpu.make_async_copy(gate_hbm, gate, weight_sems.at[0]),
        pltpu.make_async_copy(up_hbm, up, weight_sems.at[1]),
    )
    for block in range(blocks):
        load(block, 0)
    for copy in weights:
        copy.start()
    if at_once:

        @pl.when(donates)
        def _():
            for distance in range(1, SIDE):
                for block in range(blocks):
                    load(block, distance)

    compact[:ALIGN, :] = jnp.zeros((ALIGN, width), jnp.bfloat16)
    for block in range(blocks):
        arrive(block, 0)
        pick(0, block, 0)

    @pl.when(donates)
    def _():
        def group(distance, carry):
            for block in range(blocks):
                pl.when(distance > 0)(functools.partial(arrive, block, distance))
                pick(1 + distance, block, distance)
                if not at_once:
                    pl.when(distance < SIDE - 1)(functools.partial(load, block, distance + 1))
            return carry
        lax.fori_loop(0, SIDE, group, 0)

    for copy in weights:
        copy.wait()

    def serve(t, carry):
        span = pl.ds(pl.multiple_of(t * tile, tile), tile)
        gate_part = jnp.dot(compact[span, :], gate[...], preferred_element_type=jnp.float32)
        up_part = jnp.dot(compact[span, :], up[...], preferred_element_type=jnp.float32)
        packed[span, :] = (jax.nn.silu(gate_part) * up_part).astype(jnp.bfloat16)
        return carry

    lax.fori_loop(0, lax.div(total + tile - 1, tile), serve, 0)

    def unpack(segment, store):
        for t in range(0, capacity, WINDOW):
            begin = pl.multiple_of(meta[offsets + segment] + t, ALIGN)
            live = lax.broadcasted_iota(jnp.int32, (WINDOW, hidden), 0) < meta[counts + segment] - t
            value = packed[pl.ds(begin, WINDOW), :]
            store(pl.ds(t, WINDOW), jnp.where(live, value, jnp.zeros_like(value)))

    def own_store(span, value):
        own_out[span, :] = value

    unpack(0, own_store)
    for distance in range(SIDE):

        group = lax.rem(meta[2] + distance, SIDE)

        def hot_store(span, value, group=group):
            hot_out[group, span, :] = value

        unpack(1 + distance, hot_store)


def hidden_call(capacity, tile, sources, meta, places, gate, up, pieces, after=()):
    rows = pieces[0].shape[2]
    width, hidden = gate.shape
    blocks = len(sources)
    block_rows = BLOCK * rows
    most = SEGMENTS * capacity + tile
    slots = blocks if blocks > 2 else SIDE * blocks
    anywhere = pl.BlockSpec(memory_space=pl.ANY)
    return pl.pallas_call(
        functools.partial(hidden_kernel, capacity, tile, sources),
        in_specs=[pl.BlockSpec(memory_space=pltpu.SMEM), pl.BlockSpec(memory_space=pltpu.VMEM)]
        + [anywhere] * (2 + len(pieces) + len(after)),
        out_specs=[pl.BlockSpec(memory_space=pltpu.VMEM)] * 2,
        out_shape=[
            jax.ShapeDtypeStruct((capacity, hidden), jnp.bfloat16),
            jax.ShapeDtypeStruct((SIDE, capacity, hidden), jnp.bfloat16),
        ],
        scratch_shapes=[
            pltpu.VMEM((width, hidden), jnp.bfloat16),
            pltpu.VMEM((width, hidden), jnp.bfloat16),
            pltpu.VMEM((slots, block_rows, width), jnp.bfloat16),
            pltpu.VMEM((most, width), jnp.bfloat16),
            pltpu.VMEM((most, hidden), jnp.bfloat16),
            pltpu.SemaphoreType.DMA((2,)),
            pltpu.SemaphoreType.DMA((slots,)),
        ],
        compiler_params=pltpu.CompilerParams(vmem_limit_bytes=VMEM),
        cost_estimate=pl.CostEstimate(
            flops=SEGMENTS * capacity * width * hidden * 2,
            bytes_accessed=2 * width * hidden * 2 + 4 * blocks * block_rows * width * 2,
            transcendentals=SEGMENTS * capacity * hidden,
        ),
    )(meta, places, gate, up, *pieces, *after)

def tables(member, donates, first_group):
    blocks, block_rows = member.shape[1:]
    after = jnp.cumsum(member.reshape(SEGMENTS, -1), axis=1).reshape(member.shape)
    counts = after[:, -1, -1]
    before = jnp.concatenate([jnp.zeros((SEGMENTS, 1), jnp.int32), after[:, :-1, -1]], axis=1)
    serves = jnp.where(jnp.arange(SEGMENTS) == 0, 1, donates)
    room = (counts + ALIGN - 1) // ALIGN * ALIGN * serves
    offsets = jnp.cumsum(room) - room
    begins = offsets[:, None] + before // ALIGN * ALIGN
    places = jnp.where(member == 1, offsets[:, None, None] + after - 1, -1).reshape(SEGMENTS * blocks, block_rows)
    meta = jnp.concatenate([jnp.stack([donates, jnp.sum(room), first_group]), offsets, counts * serves, begins.reshape(-1)])
    return meta.astype(jnp.int32), places, after, before


def down_kernel(hidden, down, out):
    out[...] = jnp.dot(hidden[...], down[...], preferred_element_type=jnp.float32).astype(jnp.bfloat16)


def down_call(hidden, down):
    slots, width = hidden.shape[0], down.shape[1]
    wide = width // 2
    column = lambda rows: pl.BlockSpec((rows, wide), lambda n: (0, n))
    return pl.pallas_call(
        down_kernel,
        grid=(width // wide,),
        in_specs=[pl.BlockSpec(memory_space=pltpu.VMEM), column(down.shape[0])],
        out_specs=column(slots),
        out_shape=jax.ShapeDtypeStruct((slots, width), jnp.bfloat16),
        compiler_params=pltpu.CompilerParams(vmem_limit_bytes=VMEM),
        cost_estimate=pl.CostEstimate(
            flops=2 * hidden.size * width, bytes_accessed=2 * (down.size + slots * width), transcendentals=0
        ),
    )(hidden, down)


def combine_kernel(is_late, starts, scales, own_early, hot_early, own_late, hot_late, down, copied,
                   theirs, mine, late, pair):
    block_rows = mine.shape[0] // SIDE
    late[:WINDOW, :] = jnp.dot(own_late[...], down[...], preferred_element_type=jnp.float32).astype(jnp.bfloat16)
    late[WINDOW:, :] = jnp.dot(hot_late[...], copied[...], preferred_element_type=jnp.float32).astype(jnp.bfloat16)
    for out, first in ((theirs, 0), (mine, SIDE)):
        for b in range(SIDE):
            block = first + b
            scale = scales[block * block_rows : (block + 1) * block_rows, :]
            if is_late[block]:
                value = jnp.dot(scale, late[...], preferred_element_type=jnp.float32)
            else:
                for part, ref in enumerate((own_early, hot_early)):
                    start = pl.multiple_of(starts[2 * block + part], ALIGN)
                    pair[block, part * WINDOW : (part + 1) * WINDOW, :] = ref[pl.ds(start, WINDOW), :]
                value = jnp.dot(scale, pair[block], preferred_element_type=jnp.float32)
            out[b * block_rows : (b + 1) * block_rows, :] = value.astype(jnp.bfloat16)


def combine_call(part, parts, is_late, starts, scales, own_early, hot_early, own_late, hot_late, down, copied):
    width = down.shape[1] // parts
    steps = 2
    wide = width // steps
    rows = scales.shape[0]
    whole = pl.BlockSpec(memory_space=pltpu.VMEM)
    column = lambda value: pl.BlockSpec((value.shape[0], wide), lambda n: (0, part * steps + n))
    result = pl.BlockSpec((rows // 2, wide), lambda n: (0, n))
    return pl.pallas_call(
        functools.partial(combine_kernel, is_late),
        grid=(steps,),
        in_specs=[pl.BlockSpec(memory_space=pltpu.SMEM), whole, column(own_early), column(hot_early), whole, whole]
        + [column(down), column(copied)],
        out_specs=[result, result],
        out_shape=[jax.ShapeDtypeStruct((rows // 2, width), jnp.bfloat16)] * 2,
        scratch_shapes=[
            pltpu.VMEM((2 * WINDOW, wide), jnp.bfloat16),
            pltpu.VMEM((2 * SIDE, 2 * WINDOW, wide), jnp.bfloat16),
        ],
        compiler_params=pltpu.CompilerParams(vmem_limit_bytes=VMEM),
        cost_estimate=pl.CostEstimate(
            flops=4 * hot_late.size * width + 4 * rows * WINDOW * width,
            bytes_accessed=2 * width * (2 * own_early.shape[0] + 2 * hot_late.shape[1] + rows),
            transcendentals=0,
        ),
    )(starts, scales, own_early, hot_early, own_late, hot_late, down, copied)


def add(*values):
    return sum(v.astype(jnp.float32) for v in values).astype(jnp.bfloat16)


def sent_back(hot, *others):
    return tie(hot[0], *others) + shift_z(hot[1], 1) + shift_z(hot[3], -1) + shift_z(hot[2], 2)


def sum_to_owners(theirs, mine, rows):
    width = mine.shape[1]
    total = add(mine, swap_cores(theirs)).reshape(SIDE, SIDE, rows, width)
    cut = SIDE // 2
    ahead = shift_ring(total[2, :cut], 1, 1)
    behind = shift_ring(total[2, cut:], 1, -1)
    forward = jnp.concatenate([add(total[1, :cut], ahead), total[1, cut:]], axis=0)
    backward = jnp.concatenate([total[3, :cut], add(total[3, cut:], behind)], axis=0)
    total = add(total[0], shift_ring(forward, 1, 1), shift_ring(backward, 1, -1))
    return add(total[0], shift_ring(total[1], 0, 1), shift_ring(total[3], 0, -1), shift_ring(total[2], 0, 2))


def local(tokens, route_ids, route_gates, w_gate, w_up, w_down, hot_source):
    n_ep = lax.axis_size("ep")
    grp, ep = lax.axis_index("grp"), lax.axis_index("ep")
    core, x, y = lax.rem(ep, 2), ep // (2 * SIDE), lax.rem(ep // 2, SIDE)
    rows = tokens[0]
    row_count, width = rows.shape
    picks = route_ids.shape[2]
    cap = row_count * picks // n_ep
    donor = hot_source[0]
    own_gate, own_up, own_down = w_gate[0, 0], w_up[0, 0], w_down[0, 0]


    passed = []
    away = lax.rem(jnp.where(core == 0, grp - donor, donor - grp) + SIDE, SIDE).reshape(1)
    size = own_down.shape[0] // PIECES

    def passing(step, *after):
        if step < PIECES:
            piece = own_down[step * size : (step + 1) * size]
            piece = tie(piece, *after) if after else piece
            piece = jnp.where(away[0] == 0, piece, passed[-1]) if step else piece
        else:
            piece = passed[-1]
        passed.append(pass_on(piece))

    routes = jnp.concatenate([route_ids[0].astype(jnp.bfloat16), route_gates[0]], axis=1)
    rows = jnp.concatenate([rows, jnp.pad(routes, ((0, 0), (0, 128 - 2 * picks)))], axis=1)
    below, above = shift_z(rows, 1), shift_z(rows, -1)
    cut = row_count // 2
    far = (shift_z(below[:cut], 1), shift_z(above[cut:], -1))
    unit_low = jnp.stack([rows, above])
    passing(0, unit_low)
    below_low, above_low = shift_ring(unit_low, 0, 1), shift_ring(unit_low, 0, -1)
    unit_high = jnp.stack([jnp.concatenate(far, axis=0), below])
    below_high, above_high = shift_ring(unit_high, 0, 1), shift_ring(unit_high, 0, -1)
    far_low, far_high = shift_ring(below_low, 0, 1), shift_ring(above_high, 0, -1)

    def join(*parts):
        return jnp.concatenate(parts).reshape(2, SIDE, row_count, rows.shape[1])

    near_parts = (unit_low, unit_high, above_low, above_high, far_low, far_high, below_low, below_high)
    info = jnp.concatenate([part[:, :, width : width + 2 * picks] for part in near_parts])
    info = info.transpose(0, 2, 1).reshape(SIDE, SIDE, -1, 128)
    info = from_all(lambda value, step: shift_ring(value, 1, step), info)
    low = tie(join(*near_parts[:4]), passed[0], info)
    high = tie(join(*near_parts[4:]), info)

    low_below, high_above = shift_ring(low, 1, 1), shift_ring(high, 1, -1)
    near = [low, high]
    near_other = [swap_cores(piece) for piece in near]
    passing(1)
    high_on, low_on = (tie(value, low_below, high_above, passed[1], *near_other) for value in (high, low))
    high_below, low_above = shift_ring(high_on, 1, 1), shift_ring(low_on, 1, -1)
    info = jnp.stack([info, swap_cores(info)])
    info = info.reshape(2 * SIDE, SIDE, SIDE, 2 * picks, row_count)
    first = [low_below, high_above]
    first_other = [swap_cores(piece) for piece in first]
    passing(2)
    last_low, last_high = (tie(value, high_below, low_above, passed[2], info, *first_other) for value in first)
    low_far, high_far = shift_ring(last_low, 1, 1), shift_ring(last_high, 1, -1)
    second = [tie(high_below, passed[2]), tie(low_above, passed[2])]
    second_other = [swap_cores(piece) for piece in second]
    passing(3)
    early = near + [second[1], first[1], first[0], second[0]]
    early = early + near_other + [second_other[1], first_other[1], first_other[0], second_other[0]]

    order = [(other, second) for seconds in STAGES for other in (0, 1) for second in seconds]
    info = jnp.stack([info[other * SIDE + second] for other, second in order])
    ids = info[:, :, :, :picks].astype(jnp.int32)
    gates = info[:, :, :, picks:].astype(jnp.float32)
    is_own, is_hot = ids[:, :, 0] == ep, ids == ep + n_ep
    block_rows = BLOCK * row_count
    member = jnp.concatenate([jnp.any(is_own, axis=2)[:, :, None], jnp.any(is_hot, axis=3)], axis=2)
    member = member.transpose(2, 0, 1, 3).reshape(SEGMENTS, len(order), block_rows).astype(jnp.int32)
    own_scale = jnp.sum(jnp.where(is_own, gates[:, :, 0], 0.0), axis=2).reshape(len(order), block_rows)
    hot_scale = jnp.sum(jnp.where(is_hot[:, :, 0], gates[:, :, 0], 0.0), axis=2).reshape(len(order), block_rows)
    donates = (donor == grp).astype(jnp.int32)

    own_hidden, hot_hidden, afters, befores = [], [], [], []
    begin, begin_slot = 0, 0
    for stage, seconds in enumerate(STAGES):
        if stage:
            far = [tie(piece, own_hidden[-1], passed[3]) for piece in (low_far, high_far)]
            pieces = far + [swap_cores(piece) for piece in far]
            own_early = down_call(tie(own_hidden[0], *far), own_down)
        else:
            pieces = early
        blocks = 2 * len(seconds)
        slots = blocks * BLOCK * cap
        meta, places, after, before = tables(member[:, begin : begin + blocks], donates, jnp.int32(0) if stage else grp)
        sources = [
            [(2 * block + first // 2, first % 2) for first in range(SIDE)] for block in range(blocks)
        ]
        own, hot = hidden_call(
            slots, 256 if blocks > 2 else 128, sources, meta, places, own_gate, own_up, pieces, after=[own_early] if stage else ()
        )
        own_hidden.append(own)
        hot_hidden.append(hot)
        afters.append(after[:2] + begin_slot)
        befores.append(before[:2] + begin_slot)
        begin, begin_slot = begin + blocks, begin_slot + slots

    hot_early = lax.psum_scatter(hot_hidden[0].reshape(-1, hot_hidden[0].shape[2]), "grp", tiled=True)
    copied, hot_early = choose_call(away, tie(hot_early, own_hidden[1]), own_down, passed)
    hot_late = sent_back(hot_hidden[1], hot_early)

    after, before = jnp.concatenate(afters, axis=1), jnp.concatenate(befores, axis=1)
    wanted = [order.index((other, second)) for other in (1, 0) for second in range(SIDE)]
    take = lambda value: jnp.stack([value[:, index] for index in wanted], axis=1)
    is_late = [order[index][1] in STAGES[-1] for index in wanted]
    most = [begin_slot - WINDOW if late_block else begin_slot - slots - WINDOW for late_block in is_late]
    starts = jnp.minimum(take(before) // ALIGN * ALIGN, jnp.array(most, jnp.int32))
    slots = jnp.arange(WINDOW, dtype=jnp.int32)
    chosen = (take(after) - 1 - starts[:, :, None])[..., None] == slots
    scale = take(jnp.stack([own_scale, hot_scale]))[..., None]
    scales = jnp.where(chosen, scale, 0.0).astype(jnp.bfloat16)
    scales = jnp.concatenate([scales[0], scales[1]], axis=-1).reshape(len(order) * block_rows, 2 * WINDOW)
    starts = starts.T.reshape(-1)

    parts = 2
    results = []
    for part in range(parts):
        theirs, mine = combine_call(
            part, parts, is_late, starts, scales, own_early, hot_early, own_hidden[1], hot_late, own_down, copied
        )
        results.append(sum_to_owners(theirs, mine, row_count))
    return jnp.concatenate(results, axis=1)[None]


def solution(mesh):
    placed = (
        P("grp", "ep", None),
        P("grp", "ep", None),
        P("grp", "ep", None),
        P("grp", "ep", None, None),
        P("grp", "ep", None, None),
        P("grp", "ep", None, None),
        P("ep"),
    )
    return jax.shard_map(
        local, mesh=mesh, in_specs=placed, out_specs=P("grp", "ep", None), check_vma=False
    )
```

```python
import functools

import jax
import jax.numpy as jnp
from jax import lax
from jax.experimental import pallas as pl
from jax.experimental.pallas import tpu as pltpu
from jax.sharding import PartitionSpec as P

SIDE = 4
SEGMENTS = 1 + SIDE
BLOCK = 4
WINDOW = 128
ALIGN = 16
PIECES = 2
STAGES = ((0, 1, 3), (2,))
VMEM = 60 * 1024 * 1024


def ep_of(x, y, core):
    return (x * SIDE + y) * 2 + core


def moved(index, ring, step):
    x, y, core = index // (2 * SIDE), index // 2 % SIDE, index % 2
    if (ring == 0) == (core == 0):
        return ep_of(x, (y + step) % SIDE, core)
    return ep_of((x + step) % SIDE, y, core)


def shift_z(value, step):
    return lax.ppermute(value, "grp", [(i, (i + step) % SIDE) for i in range(SIDE)])


def shift_ring(value, ring, step):
    count = 2 * SIDE * SIDE
    return lax.ppermute(value, "ep", [(i, moved(i, ring, step)) for i in range(count)])


def swap_cores(value):
    count = 2 * SIDE * SIDE
    return lax.ppermute(value, "ep", [(i, i ^ 1) for i in range(count)])


def pass_on(value):
    count = 2 * SIDE * SIDE
    pairs = [(g * count + i, (g + 1 - 2 * (i % 2)) % SIDE * count + i) for g in range(SIDE) for i in range(count)]
    return lax.ppermute(value, ("grp", "ep"), pairs)


def from_all(shift, value):
    return jnp.stack([value, shift(value, -1), shift(value, 2), shift(value, 1)])


def tie(value, *others):
    anywhere = pl.BlockSpec(memory_space=pl.ANY)
    return pl.pallas_call(
        lambda *refs: None,
        in_specs=[anywhere] * (1 + len(others)),
        out_specs=anywhere,
        out_shape=jax.ShapeDtypeStruct(value.shape, value.dtype),
        input_output_aliases={0: 0},
    )(value, *others)


def choose_kernel(steps, which, hot, own, *refs):
    passed, (copied, out, held, in_sems, out_sems) = refs[:steps], refs[steps:]
    chunks = in_sems.shape[0]
    size = held.shape[0] // chunks
    each = chunks // PIECES
    wide = 512 if held.shape[1] % 512 == 0 else 256
    spans = [pl.ds(chunk * size, size) for chunk in range(chunks)]
    for away in range(SIDE):

        @pl.when(which[0] == away)
        def _(away=away):
            for chunk, span in enumerate(spans):
                source = passed[chunk // each + away - 1].at[spans[chunk % each]] if away else own.at[span]
                pltpu.make_async_copy(source, held.at[span], in_sems.at[chunk]).start()

    copies = []
    for chunk, span in enumerate(spans):
        pltpu.make_async_copy(held.at[span], held.at[span], in_sems.at[chunk]).wait()
        copies.append(pltpu.make_async_copy(held.at[span], copied.at[span], out_sems.at[chunk]))
        copies[-1].start()

    def part(n, carry):
        columns = pl.ds(pl.multiple_of(n * wide, wide), wide)
        out[:, columns] = jnp.dot(hot[...], held[:, columns], preferred_element_type=jnp.float32).astype(jnp.bfloat16)
        return carry

    lax.fori_loop(0, held.shape[1] // wide, part, 0)
    for copy in copies:
        copy.wait()


def choose_call(away, hot, own, passed):
    anywhere, whole = pl.BlockSpec(memory_space=pl.ANY), pl.BlockSpec(memory_space=pltpu.VMEM)
    chunks = 4 * PIECES
    return pl.pallas_call(
        functools.partial(choose_kernel, len(passed)),
        in_specs=[pl.BlockSpec(memory_space=pltpu.SMEM), whole] + [anywhere] * (1 + len(passed)),
        out_specs=[anywhere, whole],
        out_shape=[
            jax.ShapeDtypeStruct(own.shape, own.dtype),
            jax.ShapeDtypeStruct((hot.shape[0], own.shape[1]), own.dtype),
        ],
        scratch_shapes=[
            pltpu.VMEM(own.shape, own.dtype),
            pltpu.SemaphoreType.DMA((chunks,)),
            pltpu.SemaphoreType.DMA((chunks,)),
        ],
        compiler_params=pltpu.CompilerParams(vmem_limit_bytes=VMEM),
        cost_estimate=pl.CostEstimate(
            flops=2 * hot.size * own.shape[1], bytes_accessed=6 * own.size, transcendentals=0
        ),
    )(away, hot, own, *passed)


def hidden_kernel(capacity, tile, sources, meta, places, gate_hbm, up_hbm, *rest):
    blocks = len(sources)
    count = max(piece for block in sources for piece, _ in block) + 1
    pieces = rest[:count]
    own_out, hot_out, gate, up, gathered, compact, packed, weight_sems, row_sems = rest[-9:]
    rows = pieces[0].shape[2]
    width, hidden = gate.shape
    block_rows = BLOCK * rows
    donates, total = meta[0] == 1, meta[1]
    offsets, counts, begins = 2, 2 + SEGMENTS, 2 + 2 * SEGMENTS

    at_once = gathered.shape[0] == SIDE * blocks

    def slot_of(block, distance):
        return distance * blocks + block if at_once else block

    def load(block, distance):
        slot = slot_of(block, distance)
        for unit, (piece, place) in enumerate(sources[block]):
            pltpu.make_async_copy(
                pieces[piece].at[place, distance, :, pl.ds(0, width)],
                gathered.at[slot, pl.ds(unit * rows, rows)],
                row_sems.at[slot],
            ).start()

    def arrive(block, distance):
        slot = slot_of(block, distance)
        pltpu.make_async_copy(gathered.at[slot], gathered.at[slot], row_sems.at[slot]).wait()

    def pick(segment, block, distance):
        start = pl.multiple_of(meta[begins + segment * blocks + block], ALIGN)
        place = places[pl.ds(segment * blocks + block, 1), :] - start
        slots = lax.broadcasted_iota(jnp.int32, (WINDOW, block_rows), 0)
        choose = jnp.where(slots == place, 1.0, 0.0).astype(jnp.bfloat16)

        found = jnp.dot(choose, gathered[slot_of(block, distance)], preferred_element_type=jnp.float32).astype(jnp.bfloat16)
        compact[pl.ds(start, ALIGN), :] = compact[pl.ds(start, ALIGN), :] + found[:ALIGN]
        compact[pl.ds(start + ALIGN, WINDOW - ALIGN), :] = found[ALIGN:]

    weights = (
        pltpu.make_async_copy(gate_hbm, gate, weight_sems.at[0]),
        pltpu.make_async_copy(up_hbm, up, weight_sems.at[1]),
    )
    for block in range(blocks):
        load(block, 0)
    for copy in weights:
        copy.start()
    if at_once:

        @pl.when(donates)
        def _():
            for distance in range(1, SIDE):
                for block in range(blocks):
                    load(block, distance)

    compact[:ALIGN, :] = jnp.zeros((ALIGN, width), jnp.bfloat16)
    for block in range(blocks):
        arrive(block, 0)
        pick(0, block, 0)

    @pl.when(donates)
    def _():
        def group(distance, carry):
            for block in range(blocks):
                pl.when(distance > 0)(functools.partial(arrive, block, distance))
                pick(1 + distance, block, distance)
                if not at_once:
                    pl.when(distance < SIDE - 1)(functools.partial(load, block, distance + 1))
            return carry
        lax.fori_loop(0, SIDE, group, 0)

    for copy in weights:
        copy.wait()

    def serve(t, carry):
        span = pl.ds(pl.multiple_of(t * tile, tile), tile)
        gate_part = jnp.dot(compact[span, :], gate[...], preferred_element_type=jnp.float32)
        up_part = jnp.dot(compact[span, :], up[...], preferred_element_type=jnp.float32)
        packed[span, :] = (jax.nn.silu(gate_part) * up_part).astype(jnp.bfloat16)
        return carry

    lax.fori_loop(0, lax.div(total + tile - 1, tile), serve, 0)

    def unpack(segment, store):
        for t in range(0, capacity, WINDOW):
            begin = pl.multiple_of(meta[offsets + segment] + t, ALIGN)
            live = lax.broadcasted_iota(jnp.int32, (WINDOW, hidden), 0) < meta[counts + segment] - t
            value = packed[pl.ds(begin, WINDOW), :]
            store(pl.ds(t, WINDOW), jnp.where(live, value, jnp.zeros_like(value)))

    def own_store(span, value):
        own_out[span, :] = value

    unpack(0, own_store)
    for distance in range(SIDE):

        def hot_store(span, value, distance=distance):
            hot_out[distance, span, :] = value

        unpack(1 + distance, hot_store)


def hidden_call(capacity, tile, sources, meta, places, gate, up, pieces, after=()):
    rows = pieces[0].shape[2]
    width, hidden = gate.shape
    blocks = len(sources)
    block_rows = BLOCK * rows
    most = SEGMENTS * capacity + tile
    slots = blocks if blocks > 2 else SIDE * blocks
    anywhere = pl.BlockSpec(memory_space=pl.ANY)
    return pl.pallas_call(
        functools.partial(hidden_kernel, capacity, tile, sources),
        in_specs=[pl.BlockSpec(memory_space=pltpu.SMEM), pl.BlockSpec(memory_space=pltpu.VMEM)]
        + [anywhere] * (2 + len(pieces) + len(after)),
        out_specs=[pl.BlockSpec(memory_space=pltpu.VMEM)] * 2,
        out_shape=[
            jax.ShapeDtypeStruct((capacity, hidden), jnp.bfloat16),
            jax.ShapeDtypeStruct((SIDE, capacity, hidden), jnp.bfloat16),
        ],
        scratch_shapes=[
            pltpu.VMEM((width, hidden), jnp.bfloat16),
            pltpu.VMEM((width, hidden), jnp.bfloat16),
            pltpu.VMEM((slots, block_rows, width), jnp.bfloat16),
            pltpu.VMEM((most, width), jnp.bfloat16),
            pltpu.VMEM((most, hidden), jnp.bfloat16),
            pltpu.SemaphoreType.DMA((2,)),
            pltpu.SemaphoreType.DMA((slots,)),
        ],
        compiler_params=pltpu.CompilerParams(vmem_limit_bytes=VMEM),
        cost_estimate=pl.CostEstimate(
            flops=SEGMENTS * capacity * width * hidden * 2,
            bytes_accessed=2 * width * hidden * 2 + 4 * blocks * block_rows * width * 2,
            transcendentals=SEGMENTS * capacity * hidden,
        ),
    )(meta, places, gate, up, *pieces, *after)

def tables(member, donates):
    blocks, block_rows = member.shape[1:]
    after = jnp.cumsum(member.reshape(SEGMENTS, -1), axis=1).reshape(member.shape)
    counts = after[:, -1, -1]
    before = jnp.concatenate([jnp.zeros((SEGMENTS, 1), jnp.int32), after[:, :-1, -1]], axis=1)
    serves = jnp.where(jnp.arange(SEGMENTS) == 0, 1, donates)
    room = (counts + ALIGN - 1) // ALIGN * ALIGN * serves
    offsets = jnp.cumsum(room) - room
    begins = offsets[:, None] + before // ALIGN * ALIGN
    places = jnp.where(member == 1, offsets[:, None, None] + after - 1, -1).reshape(SEGMENTS * blocks, block_rows)
    meta = jnp.concatenate([jnp.stack([donates, jnp.sum(room)]), offsets, counts * serves, begins.reshape(-1)])
    return meta.astype(jnp.int32), places, after, before


def down_kernel(hidden, down, out):
    out[...] = jnp.dot(hidden[...], down[...], preferred_element_type=jnp.float32).astype(jnp.bfloat16)


def down_call(hidden, down):
    slots, width = hidden.shape[0], down.shape[1]
    wide = width // 2
    column = lambda rows: pl.BlockSpec((rows, wide), lambda n: (0, n))
    return pl.pallas_call(
        down_kernel,
        grid=(width // wide,),
        in_specs=[pl.BlockSpec(memory_space=pltpu.VMEM), column(down.shape[0])],
        out_specs=column(slots),
        out_shape=jax.ShapeDtypeStruct((slots, width), jnp.bfloat16),
        compiler_params=pltpu.CompilerParams(vmem_limit_bytes=VMEM),
        cost_estimate=pl.CostEstimate(
            flops=2 * hidden.size * width, bytes_accessed=2 * (down.size + slots * width), transcendentals=0
        ),
    )(hidden, down)


def combine_kernel(is_late, starts, scales, own_early, hot_early, own_late, hot_late, down, copied,
                   theirs, mine, late, pair):
    block_rows = mine.shape[0] // SIDE
    late[:WINDOW, :] = jnp.dot(own_late[...], down[...], preferred_element_type=jnp.float32).astype(jnp.bfloat16)
    late[WINDOW:, :] = jnp.dot(hot_late[...], copied[...], preferred_element_type=jnp.float32).astype(jnp.bfloat16)
    for out, first in ((theirs, 0), (mine, SIDE)):
        for b in range(SIDE):
            block = first + b
            scale = scales[block * block_rows : (block + 1) * block_rows, :]
            if is_late[block]:
                value = jnp.dot(scale, late[...], preferred_element_type=jnp.float32)
            else:
                for part, ref in enumerate((own_early, hot_early)):
                    start = pl.multiple_of(starts[2 * block + part], ALIGN)
                    pair[block, part * WINDOW : (part + 1) * WINDOW, :] = ref[pl.ds(start, WINDOW), :]
                value = jnp.dot(scale, pair[block], preferred_element_type=jnp.float32)
            out[b * block_rows : (b + 1) * block_rows, :] = value.astype(jnp.bfloat16)


def combine_call(part, parts, is_late, starts, scales, own_early, hot_early, own_late, hot_late, down, copied):
    width = down.shape[1] // parts
    steps = 2
    wide = width // steps
    rows = scales.shape[0]
    whole = pl.BlockSpec(memory_space=pltpu.VMEM)
    column = lambda value: pl.BlockSpec((value.shape[0], wide), lambda n: (0, part * steps + n))
    result = pl.BlockSpec((rows // 2, wide), lambda n: (0, n))
    return pl.pallas_call(
        functools.partial(combine_kernel, is_late),
        grid=(steps,),
        in_specs=[pl.BlockSpec(memory_space=pltpu.SMEM), whole, column(own_early), column(hot_early), whole, whole]
        + [column(down), column(copied)],
        out_specs=[result, result],
        out_shape=[jax.ShapeDtypeStruct((rows // 2, width), jnp.bfloat16)] * 2,
        scratch_shapes=[
            pltpu.VMEM((2 * WINDOW, wide), jnp.bfloat16),
            pltpu.VMEM((2 * SIDE, 2 * WINDOW, wide), jnp.bfloat16),
        ],
        compiler_params=pltpu.CompilerParams(vmem_limit_bytes=VMEM),
        cost_estimate=pl.CostEstimate(
            flops=4 * hot_late.size * width + 4 * rows * WINDOW * width,
            bytes_accessed=2 * width * (2 * own_early.shape[0] + 2 * hot_late.shape[1] + rows),
            transcendentals=0,
        ),
    )(starts, scales, own_early, hot_early, own_late, hot_late, down, copied)


def add(*values):
    return sum(v.astype(jnp.float32) for v in values).astype(jnp.bfloat16)


def sent_back(hot, *others):
    return tie(hot[0], *others) + shift_z(hot[1], 1) + shift_z(hot[3], -1) + shift_z(hot[2], 2)


def sum_to_owners(theirs, mine, rows):
    width = mine.shape[1]
    total = add(mine, swap_cores(theirs)).reshape(SIDE, SIDE, rows, width)
    cut = SIDE // 2
    ahead = shift_ring(total[2, :cut], 1, 1)
    behind = shift_ring(total[2, cut:], 1, -1)
    forward = jnp.concatenate([add(total[1, :cut], ahead), total[1, cut:]], axis=0)
    backward = jnp.concatenate([total[3, :cut], add(total[3, cut:], behind)], axis=0)
    total = add(total[0], shift_ring(forward, 1, 1), shift_ring(backward, 1, -1))
    return add(total[0], shift_ring(total[1], 0, 1), shift_ring(total[3], 0, -1), shift_ring(total[2], 0, 2))


def local(tokens, route_ids, route_gates, w_gate, w_up, w_down, hot_source):
    n_ep = lax.axis_size("ep")
    grp, ep = lax.axis_index("grp"), lax.axis_index("ep")
    core, x, y = lax.rem(ep, 2), ep // (2 * SIDE), lax.rem(ep // 2, SIDE)
    rows = tokens[0]
    row_count, width = rows.shape
    picks = route_ids.shape[2]
    cap = row_count * picks // n_ep
    donor = hot_source[0]
    own_gate, own_up, own_down = w_gate[0, 0], w_up[0, 0], w_down[0, 0]


    passed = []
    away = lax.rem(jnp.where(core == 0, grp - donor, donor - grp) + SIDE, SIDE).reshape(1)
    size = own_down.shape[0] // PIECES

    def passing(step, *after):
        if step < PIECES:
            piece = own_down[step * size : (step + 1) * size]
            piece = tie(piece, *after) if after else piece
            piece = jnp.where(away[0] == 0, piece, passed[-1]) if step else piece
        else:
            piece = passed[-1]
        passed.append(pass_on(piece))

    routes = jnp.concatenate([route_ids[0].astype(jnp.bfloat16), route_gates[0]], axis=1)
    rows = jnp.concatenate([rows, jnp.pad(routes, ((0, 0), (0, 128 - 2 * picks)))], axis=1)
    below, above = shift_z(rows, 1), shift_z(rows, -1)
    cut = row_count // 2
    far = (shift_z(below[:cut], 1), shift_z(above[cut:], -1))
    unit_low = jnp.stack([rows, above])
    passing(0, unit_low)
    below_low, above_low = shift_ring(unit_low, 0, 1), shift_ring(unit_low, 0, -1)
    unit_high = jnp.stack([jnp.concatenate(far, axis=0), below])
    below_high, above_high = shift_ring(unit_high, 0, 1), shift_ring(unit_high, 0, -1)
    far_low, far_high = shift_ring(below_low, 0, 1), shift_ring(above_high, 0, -1)

    def join(*parts):
        return jnp.concatenate(parts).reshape(2, SIDE, row_count, rows.shape[1])

    near_parts = (unit_low, unit_high, above_low, above_high, far_low, far_high, below_low, below_high)
    info = jnp.concatenate([part[:, :, width : width + 2 * picks] for part in near_parts])
    info = info.transpose(0, 2, 1).reshape(SIDE, SIDE, -1, 128)
    info = from_all(lambda value, step: shift_ring(value, 1, step), info)
    low = tie(join(*near_parts[:4]), passed[0], info)
    high = tie(join(*near_parts[4:]), info)

    low_below, high_above = shift_ring(low, 1, 1), shift_ring(high, 1, -1)
    near = [low, high]
    near_other = [swap_cores(piece) for piece in near]
    passing(1)
    high_on, low_on = (tie(value, low_below, high_above, passed[1], *near_other) for value in (high, low))
    high_below, low_above = shift_ring(high_on, 1, 1), shift_ring(low_on, 1, -1)
    info = jnp.stack([info, swap_cores(info)])
    info = info.reshape(2 * SIDE, SIDE, SIDE, 2 * picks, row_count)
    first = [low_below, high_above]
    first_other = [swap_cores(piece) for piece in first]
    passing(2)
    last_low, last_high = (tie(value, high_below, low_above, passed[2], info, *first_other) for value in first)
    low_far, high_far = shift_ring(last_low, 1, 1), shift_ring(last_high, 1, -1)
    second = [tie(high_below, passed[2]), tie(low_above, passed[2])]
    second_other = [swap_cores(piece) for piece in second]
    passing(3)
    early = near + [second[1], first[1], first[0], second[0]]
    early = early + near_other + [second_other[1], first_other[1], first_other[0], second_other[0]]

    order = [(other, second) for seconds in STAGES for other in (0, 1) for second in seconds]
    info = jnp.stack([info[other * SIDE + second] for other, second in order])
    ids = info[:, :, :, :picks].astype(jnp.int32)
    gates = info[:, :, :, picks:].astype(jnp.float32)
    is_own, is_hot = ids[:, :, 0] == ep, ids == ep + n_ep
    block_rows = BLOCK * row_count
    member = jnp.concatenate([jnp.any(is_own, axis=2)[:, :, None], jnp.any(is_hot, axis=3)], axis=2)
    member = member.transpose(2, 0, 1, 3).reshape(SEGMENTS, len(order), block_rows).astype(jnp.int32)
    own_scale = jnp.sum(jnp.where(is_own, gates[:, :, 0], 0.0), axis=2).reshape(len(order), block_rows)
    hot_scale = jnp.sum(jnp.where(is_hot[:, :, 0], gates[:, :, 0], 0.0), axis=2).reshape(len(order), block_rows)
    donates = (donor == grp).astype(jnp.int32)

    own_hidden, hot_hidden, afters, befores = [], [], [], []
    begin, begin_slot = 0, 0
    for stage, seconds in enumerate(STAGES):
        if stage:
            far = [tie(piece, own_hidden[-1], passed[3]) for piece in (low_far, high_far)]
            pieces = far + [swap_cores(piece) for piece in far]
            own_early = down_call(tie(own_hidden[0], *far), own_down)
        else:
            pieces = early
        blocks = 2 * len(seconds)
        slots = blocks * BLOCK * cap
        meta, places, after, before = tables(member[:, begin : begin + blocks], donates)
        sources = [
            [(2 * block + first // 2, first % 2) for first in range(SIDE)] for block in range(blocks)
        ]
        own, hot = hidden_call(
            slots, 256 if blocks > 2 else 128, sources, meta, places, own_gate, own_up, pieces, after=[own_early] if stage else ()
        )
        own_hidden.append(own)
        hot_hidden.append(hot)
        afters.append(after[:2] + begin_slot)
        befores.append(before[:2] + begin_slot)
        begin, begin_slot = begin + blocks, begin_slot + slots

    copied, hot_early = choose_call(away, sent_back(hot_hidden[0], own_hidden[1]), own_down, passed)
    hot_late = sent_back(hot_hidden[1], hot_early)

    after, before = jnp.concatenate(afters, axis=1), jnp.concatenate(befores, axis=1)
    wanted = [order.index((other, second)) for other in (1, 0) for second in range(SIDE)]
    take = lambda value: jnp.stack([value[:, index] for index in wanted], axis=1)
    is_late = [order[index][1] in STAGES[-1] for index in wanted]
    most = [begin_slot - WINDOW if late_block else begin_slot - slots - WINDOW for late_block in is_late]
    starts = jnp.minimum(take(before) // ALIGN * ALIGN, jnp.array(most, jnp.int32))
    slots = jnp.arange(WINDOW, dtype=jnp.int32)
    chosen = (take(after) - 1 - starts[:, :, None])[..., None] == slots
    scale = take(jnp.stack([own_scale, hot_scale]))[..., None]
    scales = jnp.where(chosen, scale, 0.0).astype(jnp.bfloat16)
    scales = jnp.concatenate([scales[0], scales[1]], axis=-1).reshape(len(order) * block_rows, 2 * WINDOW)
    starts = starts.T.reshape(-1)

    parts = 2
    results = []
    for part in range(parts):
        theirs, mine = combine_call(
            part, parts, is_late, starts, scales, own_early, hot_early, own_hidden[1], hot_late, own_down, copied
        )
        results.append(sum_to_owners(theirs, mine, row_count))
    return jnp.concatenate(results, axis=1)[None]


def solution(mesh):
    placed = (
        P("grp", "ep", None),
        P("grp", "ep", None),
        P("grp", "ep", None),
        P("grp", "ep", None, None),
        P("grp", "ep", None, None),
        P("grp", "ep", None, None),
        P("ep"),
    )
    return jax.shard_map(
        local, mesh=mesh, in_specs=placed, out_specs=P("grp", "ep", None), check_vma=False
    )
```
